32 devices in a mesh: dp: 2 (over x), seq: 4 (over y, core), tensor: 4 (over z).
Axes of the slice: x: 2, y: 2, z: 4, core: 2. Of those that a mesh axis runs over, the one named last changes fastest.
Arguments:
- tokens: bfloat16 [2, 2, 3072, 2048], P(None, 'dp', 'seq'), may hold values from -6 to 6
- cotangent: bfloat16 [2, 2, 3072, 2048], P(None, 'dp', 'seq'), may hold values from -6 to 6
- w_query: bfloat16 [2048, 2048], P(('dp', 'seq'), 'tensor'), may hold values from -0.125 to 0.125
- w_key: bfloat16 [2048, 2048], P(('dp', 'seq'), 'tensor'), may hold values from -0.125 to 0.125
- w_value: bfloat16 [2048, 2048], P(('dp', 'seq'), 'tensor'), may hold values from -0.125 to 0.125
- w_out: bfloat16 [2048, 2048], P('tensor', ('dp', 'seq')), may hold values from -0.125 to 0.125
- w_gate: bfloat16 [2048, 8192], P(('dp', 'seq'), 'tensor'), may hold values from -0.125 to 0.125
- w_up: bfloat16 [2048, 8192], P(('dp', 'seq'), 'tensor'), may hold values from -0.125 to 0.125
- w_down: bfloat16 [8192, 2048], P('tensor', ('dp', 'seq')), may hold values from -0.0625 to 0.0625
- query_gain: bfloat16 [16, 128], P('tensor', ('dp', 'seq')), may hold values from 0.25 to 1.75
- key_gain: bfloat16 [16, 128], P('tensor', ('dp', 'seq')), may hold values from 0.25 to 1.75
- attn_gain: bfloat16 [2048], P(('dp', 'seq')), may hold values from 0.25 to 1.75
- mlp_gain: bfloat16 [2048], P(('dp', 'seq')), may hold values from 0.25 to 1.75
- parent_of: int32 [2, 2, 10], P(None, 'dp'), may hold values from 0 to 3, as said below
- seg_length: int32 [2, 2, 10], P(None, 'dp'), may hold values from 128 to 768, as said below
Outputs:
- layer_out: bfloat16 [2, 2, 3072, 2048], P(None, 'dp', 'seq')
- input_grad: float32 [2, 2, 3072, 2048], P(None, 'dp', 'seq')
- g_query: float32 [2048, 2048], P(('dp', 'seq'), 'tensor')
- g_key: float32 [2048, 2048], P(('dp', 'seq'), 'tensor')
- g_value: float32 [2048, 2048], P(('dp', 'seq'), 'tensor')
- g_out: float32 [2048, 2048], P('tensor', ('dp', 'seq'))
- g_gate: float32 [2048, 8192], P(('dp', 'seq'), 'tensor')
- g_up: float32 [2048, 8192], P(('dp', 'seq'), 'tensor')
- g_down: float32 [8192, 2048], P('tensor', ('dp', 'seq'))
- g_query_gain: float32 [16, 128], P('tensor', ('dp', 'seq'))
- g_key_gain: float32 [16, 128], P('tensor', ('dp', 'seq'))
- g_attn_gain: float32 [2048], P(('dp', 'seq'))
- g_mlp_gain: float32 [2048], P(('dp', 'seq'))
The draws below stay inside these ranges and needn't reach their ends.
Inputs may be any that keep to these rules, and one draw needn't show every extreme that they name: `parent_of`: segments 0 to 3 have parent 0; each of the segments 1 to 3 is the parent of exactly two of the segments 3 + 1 to 9. `seg_length`: the trunk (segment 0) has 384 valid positions or more, every other segment 256 / 2 or more and 256 at most.
All inputs are finite; a program needn't handle non-finite values.
Results may differ from the reference program's by a relative error of at most 0.02.
Values may be sent and summed in bfloat16 or wider, within the bound.
A program may use at most 384 MiB of HBM per device.

```python
import math
import jax
import jax.numpy as jnp
from jax import lax

D = 2048
NH = 16
HD = 128
FF = 8192
BLOCK = 256
MICRO = 2
NB = 12
SLOT = 3072
BR = 3
SEGS = 10
TB = 3
TREES = 2


def draw_parent_of(key, part):
    key = jax.random.fold_in(key, 11)
    tree_keys = jax.random.split(key, MICRO * TREES)

    def one_tree(tree_key):
        shuffled = jax.random.permutation(tree_key, 2 * BR)
        leaves = (1 + shuffled // 2).astype(jnp.int32)
        return jnp.concatenate([jnp.zeros((1 + BR,), jnp.int32), leaves])
    return jax.vmap(one_tree)(tree_keys).reshape(MICRO, TREES, SEGS).astype(jnp.int32)


def draw_seg_length(key, part):
    key = jax.random.fold_in(key, 23)
    trunk_key, other_key = jax.random.split(key)
    trunk_len = jax.random.randint(trunk_key, (MICRO, TREES, 1), TB * BLOCK // 2, TB * BLOCK + 1)
    other_len = jax.random.randint(other_key, (MICRO, TREES, SEGS - 1), BLOCK // 2, BLOCK + 1)
    lengths = jnp.concatenate([trunk_len, other_len], axis=2).astype(jnp.int32)
    lengths = lengths.at[0, 0, 0].set(TB * BLOCK).at[0, 0, 1].set(BLOCK // 2)
    return lengths


def steps_of(own_key, shape, pieces, low, high):
    factor_of = 1.0
    for dim, shards_of in pieces:
        steps = jax.random.uniform(jax.random.fold_in(jax.random.fold_in(own_key, 6), dim), (shards_of,), jnp.float32, low / len(pieces), high / len(pieces))
        factor_of = factor_of * jnp.repeat(jnp.exp(steps), shape[dim] // shards_of).reshape((-1,) + (1,) * (len(shape) - 1 - dim))
    return factor_of


def gaussian(stream_key, dims, deviation, bound, shards=(), kind=jnp.bfloat16):
    drawn = jax.random.normal(stream_key, dims, jnp.float32) * deviation
    if len(shards) > 0:
        drawn = steps_of(stream_key, dims, shards, -0.22, 0.18) * drawn
    return jnp.clip(drawn, min=-bound, max=bound).astype(kind)


def setup_inputs(seed: int = 0) -> dict:
    arg_keys = jax.random.split(jax.random.key(seed), 16)
    return {
        "tokens": gaussian(arg_keys[0], (MICRO, TREES, SLOT, D), 1.0, 6.0, ((1, 2), (2, 4))),
        "cotangent": gaussian(arg_keys[1], (MICRO, TREES, SLOT, D), 1.0, 6.0, ((1, 2), (2, 4))),
        "w_query": gaussian(arg_keys[2], (D, NH * HD), D ** -0.5, 0.125, ((0, 8), (1, 4))),
        "w_key": gaussian(arg_keys[3], (D, NH * HD), D ** -0.5, 0.125, ((0, 8), (1, 4))),
        "w_value": gaussian(arg_keys[4], (D, NH * HD), D ** -0.5, 0.125, ((0, 8), (1, 4))),
        "w_out": gaussian(arg_keys[5], (NH * HD, D), (NH * HD) ** -0.5, 0.125, ((0, 4), (1, 8))),
        "w_gate": gaussian(arg_keys[6], (D, FF), D ** -0.5, 0.125, ((0, 8), (1, 4))),
        "w_up": gaussian(arg_keys[7], (D, FF), D ** -0.5, 0.125, ((0, 8), (1, 4))),
        "w_down": gaussian(arg_keys[8], (FF, D), FF ** -0.5, 0.0625, ((0, 4), (1, 8))),
        "query_gain": jnp.clip(1.0 + 0.15 * jax.random.normal(arg_keys[9], (NH, HD), jnp.float32), 0.25, 1.75).astype(jnp.bfloat16),
        "key_gain": jnp.clip(1.0 + 0.15 * jax.random.normal(arg_keys[10], (NH, HD), jnp.float32), 0.25, 1.75).astype(jnp.bfloat16),
        "attn_gain": jnp.clip(1.0 + 0.15 * jax.random.normal(arg_keys[11], (D,), jnp.float32), 0.25, 1.75).astype(jnp.bfloat16),
        "mlp_gain": jnp.clip(1.0 + 0.15 * jax.random.normal(arg_keys[12], (D,), jnp.float32), 0.25, 1.75).astype(jnp.bfloat16),
        "parent_of": draw_parent_of(jax.random.fold_in(arg_keys[15], 71), 0),
        "seg_length": draw_seg_length(jax.random.fold_in(arg_keys[15], 71), 0),
    }


@jax.custom_vjp
def low(v):
    return lax.optimization_barrier(v.astype(jnp.bfloat16)).astype(jnp.float32)

@jax.custom_vjp
def low_back(v):
    return v

def low_keep(v):
    return (low(v), None)

def low_pass(kept, grad):
    return (grad,)

def back_keep(v):
    return (v, None)

def back_low(kept, grad):
    return (low(grad),)
low.defvjp(low_keep, low_pass)
low_back.defvjp(back_keep, back_low)
norm_eps = 1e-06
masked_score = -1e+30

def exact_dot(left, right):
    return jnp.dot(left, right, precision=lax.Precision.HIGHEST, preferred_element_type=jnp.float32)

def lookup_parent(segments, parents, seg_count):
    picked = segments[:, None] == jnp.arange(seg_count, dtype=jnp.int32)[None, :]
    return lax.optimization_barrier(jnp.sum(jnp.where(picked, parents[None, :], 0), axis=1)).astype(jnp.int32)

def tree_tables(parents, lengths, n_blocks, block_size):
    seg_count = parents.shape[0]
    branches = (seg_count - 1) // 3
    trunk_blocks = n_blocks - 3 * branches
    blocks = jnp.arange(n_blocks, dtype=jnp.int32)
    seg_of = jnp.maximum(blocks - trunk_blocks + 1, 0).astype(jnp.int32)
    seg_start = jnp.where(blocks < trunk_blocks, 0, blocks)
    seg_pick = seg_of[:, None] == jnp.arange(seg_count, dtype=jnp.int32)[None, :]
    seg_span = lax.optimization_barrier(jnp.sum(jnp.where(seg_pick, lengths[None, :], 0), axis=1))
    offset = (blocks - seg_start)[:, None] * block_size + jnp.arange(block_size, dtype=jnp.int32)[None, :]
    valid_keys = (offset < seg_span[:, None]).reshape(-1)
    parent_one = lookup_parent(seg_of, parents, seg_count)
    parent_two = lookup_parent(parent_one, parents, seg_count)
    key_seg = seg_of[None, :]
    vis_table = (key_seg == seg_of[:, None]) | (key_seg == parent_one[:, None]) | (key_seg == parent_two[:, None])
    return (vis_table, valid_keys)

def block_mask(vis_rows, valid_keys, first_row, block_size):
    row_blocks, n_blocks = vis_rows.shape
    row_count = row_blocks * block_size
    query_pos = first_row + jnp.arange(row_count, dtype=jnp.int32)
    key_pos = jnp.arange(n_blocks * block_size, dtype=jnp.int32)
    visible = jnp.broadcast_to(vis_rows[:, None, :, None], (row_blocks, block_size, n_blocks, block_size))
    visible = visible.reshape(row_count, n_blocks * block_size)
    return visible & valid_keys[None, :] & (key_pos[None, :] <= query_pos[:, None])

def rms_norm(values, gain):
    return values * lax.rsqrt(lax.optimization_barrier(jnp.mean(values * values, axis=-1, keepdims=True)) + norm_eps) * gain

def tree_forward(inputs, weights, vis_table, valid_keys):
    w_q, w_k, w_v, w_o, w_g, w_u, w_d, q_gain, k_gain, a_gain, m_gain = weights
    q_heads = low(rms_norm(low_back(exact_dot(inputs, w_q)), q_gain.reshape(-1))).reshape(SLOT, NH, HD)
    k_heads = low(rms_norm(low_back(exact_dot(inputs, w_k)), k_gain.reshape(-1))).reshape(SLOT, NH, HD)
    v_heads = low(low_back(exact_dot(inputs, w_v))).reshape(SLOT, NH, HD)
    row_block = math.gcd(512, SLOT)

    def attend(block_index):
        start_row = (block_index * row_block).astype(jnp.int32)
        query_rows = lax.dynamic_slice_in_dim(q_heads, start_row, row_block, 0)
        vis_rows = lax.dynamic_slice_in_dim(vis_table, (start_row // BLOCK).astype(jnp.int32), row_block // BLOCK, 0)
        visible = block_mask(vis_rows, valid_keys, start_row, BLOCK)
        raw_scores = jnp.einsum('qhd,khd->hqk', query_rows, k_heads, precision=lax.Precision.HIGHEST) * HD ** (-0.5)
        scores = jnp.where(visible[None], low_back(raw_scores), masked_score)
        top_score = lax.optimization_barrier(jnp.max(scores, axis=-1, keepdims=True))
        exp_scores = jnp.exp(scores - top_score)
        prob_rows = exp_scores / lax.optimization_barrier(jnp.sum(exp_scores, axis=-1, keepdims=True))
        return jnp.einsum('hqk,khd->qhd', low(prob_rows), v_heads, precision=lax.Precision.HIGHEST)
    attended = lax.map(jax.checkpoint(attend), jnp.arange(SLOT // row_block, dtype=jnp.int32))
    attn_low = low(low_back(attended.reshape(SLOT, NH * HD)))
    attn_proj = low_back(exact_dot(attn_low, w_o))
    hidden = inputs + rms_norm(attn_proj, a_gain)
    hidden_low = low(hidden)
    gate_pre = low_back(exact_dot(hidden_low, w_g))
    up_pre = low_back(exact_dot(hidden_low, w_u))
    inner_low = low(jax.nn.silu(gate_pre) * up_pre)
    mlp_proj = low_back(exact_dot(inner_low, w_d))
    return hidden + rms_norm(mlp_proj, m_gain)

def reference(tokens, cotangent, w_query, w_key, w_value, w_out, w_gate, w_up, w_down, query_gain, key_gain, attn_gain, mlp_gain, parent_of, seg_length):
    weights = tuple((item.astype(jnp.float32) for item in (w_query, w_key, w_value, w_out, w_gate, w_up, w_down, query_gain, key_gain, attn_gain, mlp_gain)))
    tree_count = MICRO * TREES
    inputs = tokens.astype(jnp.float32).reshape(tree_count, SLOT, D)
    cot_rows = cotangent.astype(jnp.float32).reshape(tree_count, SLOT, D)
    parents = parent_of.reshape(tree_count, SEGS)
    lengths = seg_length.reshape(tree_count, SEGS)

    def one_tree(totals, item):
        tree_in, tree_cot, tree_par, tree_len = item
        vis_table, valid_keys = tree_tables(tree_par, tree_len, NB, BLOCK)

        def forward(values, params):
            return tree_forward(values, params, vis_table, valid_keys)
        tree_out, pull = jax.vjp(forward, tree_in, weights)
        tree_grad, weight_grads = pull(tree_cot)
        return (jax.tree.map(jnp.add, totals, weight_grads), (tree_out.astype(jnp.bfloat16), tree_grad))
    zeros = jax.tree.map(jnp.zeros_like, weights)
    totals, (outs, grads) = lax.scan(one_tree, zeros, (inputs, cot_rows, parents, lengths))
    return (outs.reshape(MICRO, TREES, SLOT, D), grads.reshape(MICRO, TREES, SLOT, D), totals[0], totals[1], totals[2], totals[3], totals[4], totals[5], totals[6], totals[7], totals[8], totals[9], totals[10])
```

```python
import functools

import jax
import jax.numpy as jnp
from jax import lax
from jax.experimental import pallas as pl
from jax.experimental.pallas import tpu as pltpu
from jax.sharding import PartitionSpec as P

HD = 128
BLOCK = 256

norm_eps = 1e-06
masked_score = -1e30
f32 = jnp.float32
bf16 = jnp.bfloat16


def matmul(left, right):
    return jnp.dot(left, right, preferred_element_type=f32)


def left_t(left, right):
    return lax.dot_general(left, right, (((0,), (0,)), ((), ())), preferred_element_type=f32)


def right_t(left, right):
    return lax.dot_general(left, right, (((1,), (1,)), ((), ())), preferred_element_type=f32)


MESH = pl.DeviceIdType.MESH


class Line:
    def __init__(self, n, chunks, rows, part, out, s, land, res, sems):
        self.chunks, self.rows = chunks, rows
        self.part, self.out, self.s, self.land, self.res = part, out, s, land, res
        (
            self.load_sem,
            self.in_send,
            self.in_recv,
            self.out_send,
            self.out_recv,
            self.store_sem,
        ) = sems
        i = lax.axis_index("tensor")
        half = n // 2
        left = i < half
        self.inward = jnp.where(left, i + 1, i - 1)
        self.outward = jnp.where(left, i - 1, i + 1)
        self.relay = (i > 0) & (i < n - 1)
        self.mid = (i == half - 1) | (i == half)
        self.slot = jnp.where(self.mid, 1, 0)

    def at(self, c):
        return pl.ds(pl.multiple_of(c * self.rows, self.rows), self.rows)

    def load(self):
        return pltpu.make_async_copy(self.part, self.s, self.load_sem)

    def inward_copy(self, c, slot):
        return pltpu.make_async_remote_copy(
            src_ref=self.s.at[self.at(c)],
            dst_ref=self.land.at[slot, self.at(c)],
            send_sem=self.in_send.at[c],
            recv_sem=self.in_recv.at[slot, c],
            device_id={"tensor": self.inward},
            device_id_type=MESH,
        )

    def outward_copy(self, c):
        return pltpu.make_async_remote_copy(
            src_ref=self.res.at[self.at(c)],
            dst_ref=self.res.at[self.at(c)],
            send_sem=self.out_send.at[c],
            recv_sem=self.out_recv.at[c],
            device_id={"tensor": self.outward},
            device_id_type=MESH,
        )

    def store(self, c):
        return pltpu.make_async_copy(
            self.res.at[self.at(c)], self.out.at[self.at(c)], self.store_sem.at[c]
        )

    def begin(self):
        self.load().start()
        barrier = pltpu.get_barrier_semaphore()
        pl.semaphore_signal(
            barrier, inc=1, device_id={"tensor": self.inward}, device_id_type=MESH
        )

        @pl.when(self.relay)
        def _():
            pl.semaphore_signal(
                barrier, inc=1, device_id={"tensor": self.outward}, device_id_type=MESH
            )

        pl.semaphore_wait(barrier, jnp.where(self.relay, 2, 1))
        self.load().wait()

        @pl.when(~self.relay)
        def _():
            def one(c, carry):
                self.inward_copy(c, self.slot).start()
                return carry

            lax.fori_loop(0, self.chunks, one, 0)

    def reduce(self, c):
        @pl.when(self.relay)
        def _():
            self.inward_copy(c, 0).wait_recv()
            a = self.at(c)
            self.s[a, :] = (self.s[a, :].astype(f32) + self.land[0, a, :].astype(f32)).astype(bf16)
            self.inward_copy(c, self.slot).start()

    def spread(self, c):
        a = self.at(c)

        @pl.when(self.mid)
        def _():
            self.inward_copy(c, 1).wait_recv()
            self.res[a, :] = (
                self.s[a, :].astype(f32) + self.land[1, a, :].astype(f32)
            ).astype(bf16)

        @pl.when(~self.mid)
        def _():
            self.outward_copy(c).wait_recv()

        @pl.when(self.relay)
        def _():
            self.outward_copy(c).start()

        self.store(c).start()

    def end(self):
        def one(c, carry):
            self.inward_copy(c, self.slot).wait_send()

            @pl.when(self.relay)
            def _():
                self.outward_copy(c).wait_send()

            self.store(c).wait()
            return carry

        lax.fori_loop(0, self.chunks, one, 0)


def line_scratch(rows, width, chunks):
    dma = pltpu.SemaphoreType.DMA
    return [
        pltpu.VMEM((rows, width), bf16),
        pltpu.VMEM((2, rows, width), bf16),
        pltpu.VMEM((rows, width), bf16),
        dma(()),
        dma((chunks,)),
        dma((2, chunks)),
        dma((chunks,)),
        dma((chunks,)),
        dma((chunks,)),
    ]


def line_kernel(n, chunks, part, out, s, land, res, *sems):
    line = Line(n, chunks, part.shape[0] // chunks, part, out, s, land, res, sems)
    line.begin()

    def step(c, carry):
        line.reduce(c)

        @pl.when(c > 0)
        def _():
            line.spread(c - 1)

        return carry

    lax.fori_loop(0, chunks, step, 0)
    line.spread(chunks - 1)
    line.end()


def line_sum(part):
    rows, width = part.shape
    n = lax.axis_size("tensor")
    chunks = rows // 48
    return pl.pallas_call(
        functools.partial(line_kernel, n, chunks),
        in_specs=[pl.BlockSpec(memory_space=pl.ANY)],
        out_specs=pl.BlockSpec(memory_space=pl.ANY),
        out_shape=jax.ShapeDtypeStruct(part.shape, bf16),
        scratch_shapes=line_scratch(rows, width, chunks),
        compiler_params=pltpu.CompilerParams(
            collective_id=0, has_side_effects=True, vmem_limit_bytes=48 << 20
        ),
        name="line_sum",
    )(part)


def attn_scores(meta, i, trunk_rows, q, kt, kp, ko):
    scale = HD ** (-0.5)
    block = meta[i, 0]
    n_par = meta[i, 2]
    n_own = meta[i, 3]
    n_trunk = meta[i, 4]
    st = right_t(q, kt) * scale
    sp = right_t(q, kp) * scale
    so = right_t(q, ko) * scale
    row = lax.broadcasted_iota(jnp.int32, (BLOCK, trunk_rows), 0) + block * BLOCK
    col = lax.broadcasted_iota(jnp.int32, (BLOCK, trunk_rows), 1)
    st = jnp.where((col < n_trunk) & (col <= row), st, masked_score)
    row = lax.broadcasted_iota(jnp.int32, (BLOCK, BLOCK), 0)
    col = lax.broadcasted_iota(jnp.int32, (BLOCK, BLOCK), 1)
    sp = jnp.where(col < n_par, sp, masked_score)
    so = jnp.where((col < n_own) & (col <= row), so, masked_score)
    return st, sp, so


def attn_fwd_kernel(trunk_rows, meta, q, kt, vt, kp, vp, ko, vo, out, lse):
    i = pl.program_id(1)
    st, sp, so = attn_scores(meta, i, trunk_rows, q[...], kt[...], kp[...], ko[...])
    top = jnp.maximum(
        jnp.max(st, axis=1, keepdims=True),
        jnp.maximum(jnp.max(sp, axis=1, keepdims=True), jnp.max(so, axis=1, keepdims=True)),
    )
    et, ep, eo = jnp.exp(st - top), jnp.exp(sp - top), jnp.exp(so - top)
    total = (
        jnp.sum(et, axis=1, keepdims=True)
        + jnp.sum(ep, axis=1, keepdims=True)
        + jnp.sum(eo, axis=1, keepdims=True)
    )
    acc = matmul(et.astype(bf16), vt[...])
    acc += matmul(ep.astype(bf16), vp[...])
    acc += matmul(eo.astype(bf16), vo[...])
    out[...] = (acc / total).astype(bf16)
    lse[...] = jnp.broadcast_to(top + jnp.log(total), (BLOCK, HD))


def attn_bwd_kernel(
    trunk_rows, n_q, meta, q, do, lse, kt, vt, kp, vp, ko, vo,
    dq, dko, dvo, dkt, dvt, dkb, dvb, a_kt, a_vt, a_kb, a_vb,
):
    i = pl.program_id(1)

    @pl.when(i == 0)
    def _():
        for acc in (a_kt, a_vt, a_kb, a_vb):
            acc[...] = jnp.zeros_like(acc)

    scale = HD ** (-0.5)
    qv, dov = q[...], do[...]
    scores = attn_scores(meta, i, trunk_rows, qv, kt[...], kp[...], ko[...])
    top = lse[:, 0:1]
    probs = [jnp.exp(s - top) for s in scores]
    grads = [right_t(dov, v[...]) for v in (vt, vp, vo)]
    inner = sum(jnp.sum(p * g, axis=1, keepdims=True) for p, g in zip(probs, grads))
    low = [(p * (g - inner)).astype(bf16) for p, g in zip(probs, grads)]
    probs = [p.astype(bf16) for p in probs]
    dq[...] = scale * (
        matmul(low[0], kt[...]) + matmul(low[1], kp[...]) + matmul(low[2], ko[...])
    )
    a_kt[...] += left_t(low[0], qv)
    a_vt[...] += left_t(probs[0], dov)
    dko[...] = scale * left_t(low[2], qv)
    dvo[...] = left_t(probs[2], dov)
    at = pl.ds(pl.multiple_of(meta[i, 1] * BLOCK, BLOCK), BLOCK)
    a_kb[at, :] += left_t(low[1], qv)
    a_vb[at, :] += left_t(probs[1], dov)

    @pl.when(i == n_q - 1)
    def _():
        dkt[...] = (scale * a_kt[...]).astype(bf16)
        dvt[...] = a_vt[...].astype(bf16)
        dkb[...] = (scale * a_kb[...]).astype(bf16)
        dvb[...] = a_vb[...].astype(bf16)


def kv_specs(trunk_rows):
    trunk = pl.BlockSpec((trunk_rows, HD), lambda h, i, meta: (0, h))
    par = pl.BlockSpec((BLOCK, HD), lambda h, i, meta: (meta[i, 1], h))
    own = pl.BlockSpec((BLOCK, HD), lambda h, i, meta: (i, h))
    return [trunk, trunk, par, par, own, own]


def attend_forward(meta, q, kv):
    rows, width = q.shape
    trunk_rows = kv[0].shape[0]
    own = pl.BlockSpec((BLOCK, HD), lambda h, i, meta: (i, h))
    return pl.pallas_call(
        functools.partial(attn_fwd_kernel, trunk_rows),
        grid_spec=pltpu.PrefetchScalarGridSpec(
            num_scalar_prefetch=1,
            grid=(width // HD, rows // BLOCK),
            in_specs=[own] + kv_specs(trunk_rows),
            out_specs=[own, own],
        ),
        out_shape=[
            jax.ShapeDtypeStruct((rows, width), bf16),
            jax.ShapeDtypeStruct((rows, width), f32),
        ],
        compiler_params=pltpu.CompilerParams(vmem_limit_bytes=32 << 20),
        name="attend_forward",
    )(meta, q, *kv)


def attend_backward(meta, q, do, lse, kv):
    rows, width = q.shape
    trunk_rows = kv[0].shape[0]
    branch_rows = kv[2].shape[0]
    own = pl.BlockSpec((BLOCK, HD), lambda h, i, meta: (i, h))
    trunk = pl.BlockSpec((trunk_rows, HD), lambda h, i, meta: (0, h))
    branch = pl.BlockSpec((branch_rows, HD), lambda h, i, meta: (0, h))
    n_q = rows // BLOCK
    return pl.pallas_call(
        functools.partial(attn_bwd_kernel, trunk_rows, n_q),
        grid_spec=pltpu.PrefetchScalarGridSpec(
            num_scalar_prefetch=1,
            grid=(width // HD, n_q),
            in_specs=[own, own, own] + kv_specs(trunk_rows),
            out_specs=[own, own, own, trunk, trunk, branch, branch],
            scratch_shapes=[
                pltpu.VMEM((trunk_rows, HD), f32),
                pltpu.VMEM((trunk_rows, HD), f32),
                pltpu.VMEM((branch_rows, HD), f32),
                pltpu.VMEM((branch_rows, HD), f32),
            ],
        ),
        out_shape=[
            jax.ShapeDtypeStruct((rows, width), f32),
            jax.ShapeDtypeStruct((rows, width), f32),
            jax.ShapeDtypeStruct((rows, width), f32),
            jax.ShapeDtypeStruct((trunk_rows, width), bf16),
            jax.ShapeDtypeStruct((trunk_rows, width), bf16),
            jax.ShapeDtypeStruct((branch_rows, width), bf16),
            jax.ShapeDtypeStruct((branch_rows, width), bf16),
        ],
        compiler_params=pltpu.CompilerParams(vmem_limit_bytes=40 << 20),
        name="attend_backward",
    )(meta, q, do, lse, *kv)


def group_perm(n, k):
    half = n // 2
    return [(i, i // half * half + (i % half + k) % half) for i in range(n)]


def fetch_sources(block):
    n = lax.axis_size("seq")
    half = n // 2
    place = lax.axis_index("seq")
    spot = lax.rem(place, half)
    got = lax.ppermute(block, "seq", [(i, i + half) for i in range(half)])
    mine = jnp.where(place < half, block, got)
    parts = [mine] + [lax.ppermute(mine, "seq", group_perm(n, k)) for k in range(1, half)]
    out = []
    for source in range(half):
        pick = parts[0]
        for k in range(1, half):
            pick = jnp.where(lax.rem(spot - k + half, half) == source, parts[k], pick)
        out.append(pick)
    return jnp.concatenate(out, axis=0)


def return_to_sources(grads):
    n = lax.axis_size("seq")
    half = n // 2
    place = lax.axis_index("seq")
    spot = lax.rem(place, half)
    rows = grads.shape[0] // half
    pieces = [grads[s * rows : (s + 1) * rows] for s in range(half)]

    def piece(index):
        pick = pieces[0]
        for s in range(1, half):
            pick = jnp.where(index == s, pieces[s], pick)
        return pick

    total = piece(spot).astype(f32)
    for k in range(1, half):
        sent = piece(lax.rem(spot + k, half))
        total += lax.ppermute(sent, "seq", group_perm(n, k)).astype(f32)
    got = lax.ppermute(total.astype(bf16), "seq", [(i + half, i) for i in range(half)])
    return jnp.where(place < half, total + got.astype(f32), 0.0)


def gather_rows(item):
    return lax.all_gather(item, ("dp", "seq"), axis=0, tiled=True)


def gather_cols(item):
    return lax.all_gather(item, ("dp", "seq"), axis=1, tiled=True)


def scatter_rows(item):
    return lax.psum_scatter(
        item.astype(bf16), ("dp", "seq"), scatter_dimension=0, tiled=True
    ).astype(f32)


def scatter_cols(item):
    return lax.psum_scatter(
        item.astype(bf16), ("dp", "seq"), scatter_dimension=1, tiled=True
    ).astype(f32)


def all_reduce(parts):
    total = line_sum(jnp.concatenate([p.astype(bf16) for p in parts], axis=0)).astype(f32)
    rows = parts[0].shape[0]
    return [total[m * rows : (m + 1) * rows] for m in range(len(parts))]


def block_meta(parents, lengths, rows, n_blocks):
    seg_count = parents.shape[0]
    branches = (seg_count - 1) // 3
    trunk_blocks = n_blocks - 3 * branches
    blocks = lax.axis_index("seq") * (rows // BLOCK) + jnp.arange(rows // BLOCK, dtype=jnp.int32)
    seg = jnp.maximum(blocks - trunk_blocks + 1, 0)
    hit = seg[:, None] == jnp.arange(seg_count, dtype=jnp.int32)[None, :]
    parent = jnp.sum(jnp.where(hit, parents[None, :], 0), axis=1)
    own_len = jnp.sum(jnp.where(hit, lengths[None, :], 0), axis=1)
    hit = parent[:, None] == jnp.arange(seg_count, dtype=jnp.int32)[None, :]
    par_len = jnp.sum(jnp.where(hit, lengths[None, :], 0), axis=1)
    return jnp.stack(
        [
            blocks,
            jnp.maximum(parent - 1, 0),
            jnp.where(parent > 0, par_len, 0),
            jnp.where(blocks >= trunk_blocks, own_len, 0),
            jnp.broadcast_to(lengths[0], blocks.shape),
        ],
        axis=1,
    ).astype(jnp.int32)


def per_device(
    tokens, cotangent, w_query, w_key, w_value, w_out, w_gate, w_up, w_down,
    query_gain, key_gain, attn_gain, mlp_gain, parent_of, seg_length,
):
    micros, _, rows, width = tokens.shape
    n_blocks = rows // BLOCK * lax.axis_size("seq")
    heads = w_query.shape[1] // HD
    full_width = heads * HD * lax.axis_size("tensor")
    branches = (parent_of.shape[2] - 1) // 3
    trunk_rows = (n_blocks - 3 * branches) * BLOCK

    wq = gather_rows(w_query)
    wk = gather_rows(w_key)
    wv = gather_rows(w_value)
    q_gain = gather_cols(query_gain).reshape(-1).astype(f32)
    k_gain = gather_cols(key_gain).reshape(-1).astype(f32)
    wo = gather_cols(w_out)
    a_gain = gather_rows(attn_gain).astype(f32)
    m_gain = gather_rows(mlp_gain).astype(f32)
    wg = gather_rows(w_gate)
    wu = gather_rows(w_up)
    wd = gather_cols(w_down)

    saved = []
    for m in range(micros):
        x = tokens[m, 0]
        q_raw, k_raw, v_raw = matmul(x, wq), matmul(x, wk), matmul(x, wv)
        q_sq, k_sq = lax.psum(
            (jnp.sum(q_raw * q_raw, axis=1), jnp.sum(k_raw * k_raw, axis=1)), "tensor"
        )
        q_inv = lax.rsqrt(q_sq / full_width + norm_eps)[:, None]
        k_inv = lax.rsqrt(k_sq / full_width + norm_eps)[:, None]
        q_unit, k_unit = q_raw * q_inv, k_raw * k_inv
        q_low = (q_unit * q_gain).astype(bf16)
        k_low = (k_unit * k_gain).astype(bf16)
        v_low = v_raw.astype(bf16)
        sources = fetch_sources(jnp.concatenate([k_low, v_low], axis=1))
        cols = k_low.shape[1]
        kv = (
            sources[:trunk_rows, :cols],
            sources[:trunk_rows, cols:],
            sources[trunk_rows:, :cols],
            sources[trunk_rows:, cols:],
            k_low,
            v_low,
        )
        meta = block_meta(parent_of[m, 0], seg_length[m, 0], rows, n_blocks)
        attn_low, lse = attend_forward(meta, q_low, kv)
        saved.append(
            dict(x=x, q_inv=q_inv, k_inv=k_inv, q_unit=q_unit, k_unit=k_unit, q_low=q_low,
                 kv=kv, meta=meta, attn_low=attn_low, lse=lse)
        )

    outs = []
    projs = all_reduce([matmul(s["attn_low"], wo) for s in saved])
    for m in range(micros):
        s = saved[m]
        attn_proj = projs[m]
        attn_inv = lax.rsqrt(jnp.mean(attn_proj * attn_proj, axis=1, keepdims=True) + norm_eps)
        attn_unit = attn_proj * attn_inv
        hidden = s["x"].astype(f32) + attn_unit * a_gain
        hidden_low = hidden.astype(bf16)
        gate_pre = matmul(hidden_low, wg)
        up_pre = matmul(hidden_low, wu)
        sig = jax.nn.sigmoid(gate_pre)
        inner_low = (gate_pre * sig * up_pre).astype(bf16)
        s.update(attn_unit=attn_unit, attn_inv=attn_inv, hidden=hidden, hidden_low=hidden_low,
                 gate_pre=gate_pre.astype(bf16), up_pre=up_pre.astype(bf16), inner_low=inner_low)

    gm_grad = 0.0
    projs = all_reduce([matmul(s["inner_low"], wd) for s in saved])
    for m in range(micros):
        s = saved[m]
        mlp_proj = projs[m]
        mlp_inv = lax.rsqrt(jnp.mean(mlp_proj * mlp_proj, axis=1, keepdims=True) + norm_eps)
        mlp_unit = mlp_proj * mlp_inv
        outs.append((s["hidden"] + mlp_unit * m_gain).astype(bf16))
        c = cotangent[m, 0].astype(f32)
        gm_grad += jnp.sum(c * mlp_unit, axis=0)
        unit_grad = c * m_gain
        mlp_low = (
            mlp_inv * (unit_grad - mlp_unit * jnp.mean(unit_grad * mlp_unit, axis=1, keepdims=True))
        ).astype(bf16)
        inner_grad = right_t(mlp_low, wd)
        gate_pre, up_pre = s["gate_pre"].astype(f32), s["up_pre"].astype(f32)
        sig = jax.nn.sigmoid(gate_pre)
        gate_low = (inner_grad * up_pre * sig * (1.0 + gate_pre * (1.0 - sig))).astype(bf16)
        up_low = (inner_grad * gate_pre * sig).astype(bf16)
        s.update(c=c, mlp_low=mlp_low, gate_low=gate_low, up_low=up_low)

    def both(name):
        return jnp.concatenate([s[name] for s in saved], axis=0)

    g_down = scatter_cols(left_t(both("inner_low"), both("mlp_low")))
    hidden_low = both("hidden_low")
    g_gate = scatter_rows(left_t(hidden_low, both("gate_low")))
    g_up = scatter_rows(left_t(hidden_low, both("up_low")))

    ga_grad = 0.0
    backs = all_reduce([right_t(s["gate_low"], wg) + right_t(s["up_low"], wu) for s in saved])
    for m in range(micros):
        s = saved[m]
        hidden_grad = s["c"] + backs[m]
        ga_grad += jnp.sum(hidden_grad * s["attn_unit"], axis=0)
        unit_grad = hidden_grad * a_gain
        proj_low = (
            s["attn_inv"]
            * (unit_grad
               - s["attn_unit"] * jnp.mean(unit_grad * s["attn_unit"], axis=1, keepdims=True))
        ).astype(bf16)
        attn_grad = right_t(proj_low, wo).astype(bf16)
        dq, dko, dvo, dkt, dvt, dkb, dvb = attend_backward(
            s["meta"], s["q_low"], attn_grad, s["lse"], s["kv"]
        )
        returned = return_to_sources(
            jnp.concatenate(
                [jnp.concatenate([dkt, dvt], axis=1), jnp.concatenate([dkb, dvb], axis=1)], axis=0
            )
        )
        cols = dko.shape[1]
        dk = dko + returned[:, :cols]
        dv = dvo + returned[:, cols:]
        s.update(hidden_grad=hidden_grad, proj_low=proj_low, dq=dq, dk=dk, dv=dv)

    qg_grad = kg_grad = 0.0
    backs = []
    for m in range(micros):
        s = saved[m]
        q_unit, k_unit = s["q_unit"], s["k_unit"]
        qg_grad += jnp.sum(s["dq"] * q_unit, axis=0)
        kg_grad += jnp.sum(s["dk"] * k_unit, axis=0)
        q_scaled, k_scaled = s["dq"] * q_gain, s["dk"] * k_gain
        q_inner, k_inner = lax.psum(
            (jnp.sum(q_scaled * q_unit, axis=1), jnp.sum(k_scaled * k_unit, axis=1)), "tensor"
        )
        qr_low = (s["q_inv"] * (q_scaled - q_unit * (q_inner / full_width)[:, None])).astype(bf16)
        kr_low = (s["k_inv"] * (k_scaled - k_unit * (k_inner / full_width)[:, None])).astype(bf16)
        vr_low = s["dv"].astype(bf16)
        backs.append(right_t(qr_low, wq) + right_t(kr_low, wk) + right_t(vr_low, wv))
        s.update(qr_low=qr_low, kr_low=kr_low, vr_low=vr_low)

    grads = [s["hidden_grad"] + back for s, back in zip(saved, all_reduce(backs))]
    x = both("x")
    g_out = scatter_cols(left_t(both("attn_low"), both("proj_low")))
    g_query = scatter_rows(left_t(x, both("qr_low")))
    g_key = scatter_rows(left_t(x, both("kr_low")))
    g_value = scatter_rows(left_t(x, both("vr_low")))
    return (
        jnp.stack(outs)[:, None],
        jnp.stack(grads)[:, None],
        g_query,
        g_key,
        g_value,
        g_out,
        g_gate,
        g_up,
        g_down,
        scatter_cols(qg_grad.reshape(heads, HD)),
        scatter_cols(kg_grad.reshape(heads, HD)),
        scatter_rows(ga_grad),
        scatter_rows(gm_grad),
    )


def solution(mesh):
    rows = P(None, "dp", "seq", None)
    by_row = P(("dp", "seq"), "tensor")
    by_col = P("tensor", ("dp", "seq"))
    gain = P(("dp", "seq"))
    tree = P(None, "dp", None)
    weights = (by_row, by_row, by_row, by_col, by_row, by_row, by_col, by_col, by_col, gain, gain)
    return jax.shard_map(
        per_device,
        mesh=mesh,
        in_specs=(rows, rows) + weights + (tree, tree),
        out_specs=(rows, rows) + weights,
        check_vma=False,
    )
```

```python
import functools
import math

import jax
import jax.numpy as jnp
from jax import lax
from jax.experimental import pallas as pl
from jax.experimental.pallas import tpu as pltpu
from jax.sharding import PartitionSpec as P

HD = 128
BLOCK = 256

norm_eps = 1e-06
masked_score = -1e30
f32 = jnp.float32
bf16 = jnp.bfloat16


def matmul(left, right):
    return jnp.dot(left, right, preferred_element_type=f32)


def left_t(left, right):
    return lax.dot_general(left, right, (((0,), (0,)), ((), ())), preferred_element_type=f32)


def right_t(left, right):
    return lax.dot_general(left, right, (((1,), (1,)), ((), ())), preferred_element_type=f32)


MESH = pl.DeviceIdType.MESH


def cost(us):
    return pl.CostEstimate(flops=int(us * 1.1e9), bytes_accessed=0, transcendentals=0)


def after(value, *earlier):
    hbm = pl.BlockSpec(memory_space=pl.ANY)
    return pl.pallas_call(
        lambda *refs: None,
        in_specs=[hbm] * (1 + len(earlier)),
        out_specs=hbm,
        out_shape=jax.ShapeDtypeStruct(value.shape, value.dtype),
        input_output_aliases={0: 0},
        name="after",
    )(value, *earlier)


class Line:
    def __init__(self, n, chunks, rows, part, out, s, land, res, sems):
        self.chunks, self.rows = chunks, rows
        self.part, self.out, self.s, self.land, self.res = part, out, s, land, res
        (
            self.load_sem,
            self.in_send,
            self.in_recv,
            self.out_send,
            self.out_recv,
            self.store_sem,
        ) = sems
        i = lax.axis_index("tensor")
        half = n // 2
        left = i < half
        self.inward = jnp.where(left, i + 1, i - 1)
        self.outward = jnp.where(left, i - 1, i + 1)
        self.relay = (i > 0) & (i < n - 1)
        self.mid = (i == half - 1) | (i == half)
        self.slot = jnp.where(self.mid, 1, 0)

    def at(self, c):
        return pl.ds(pl.multiple_of(c * self.rows, self.rows), self.rows)

    def load(self):
        return pltpu.make_async_copy(self.part, self.s, self.load_sem)

    def inward_copy(self, c, slot):
        return pltpu.make_async_remote_copy(
            src_ref=self.s.at[self.at(c)],
            dst_ref=self.land.at[slot, self.at(c)],
            send_sem=self.in_send.at[c],
            recv_sem=self.in_recv.at[slot, c],
            device_id={"tensor": self.inward},
            device_id_type=MESH,
        )

    def outward_copy(self, c):
        return pltpu.make_async_remote_copy(
            src_ref=self.res.at[self.at(c)],
            dst_ref=self.res.at[self.at(c)],
            send_sem=self.out_send.at[c],
            recv_sem=self.out_recv.at[c],
            device_id={"tensor": self.outward},
            device_id_type=MESH,
        )

    def store(self, c):
        return pltpu.make_async_copy(
            self.res.at[self.at(c)], self.out.at[self.at(c)], self.store_sem.at[c]
        )

    def begin(self):
        self.load().start()
        barrier = pltpu.get_barrier_semaphore()
        pl.semaphore_signal(
            barrier, inc=1, device_id={"tensor": self.inward}, device_id_type=MESH
        )

        @pl.when(self.relay)
        def _():
            pl.semaphore_signal(
                barrier, inc=1, device_id={"tensor": self.outward}, device_id_type=MESH
            )

        pl.semaphore_wait(barrier, jnp.where(self.relay, 2, 1))
        self.load().wait()

        @pl.when(~self.relay)
        def _():
            def one(c, carry):
                self.inward_copy(c, self.slot).start()
                return carry

            lax.fori_loop(0, self.chunks, one, 0)

    def reduce(self, c):
        @pl.when(self.relay)
        def _():
            self.inward_copy(c, 0).wait_recv()
            a = self.at(c)
            self.s[a, :] = (self.s[a, :].astype(f32) + self.land[0, a, :].astype(f32)).astype(bf16)
            self.inward_copy(c, self.slot).start()

    def spread(self, c):
        a = self.at(c)

        @pl.when(self.mid)
        def _():
            self.inward_copy(c, 1).wait_recv()
            self.res[a, :] = (
                self.s[a, :].astype(f32) + self.land[1, a, :].astype(f32)
            ).astype(bf16)

        @pl.when(~self.mid)
        def _():
            self.outward_copy(c).wait_recv()

        @pl.when(self.relay)
        def _():
            self.outward_copy(c).start()

        self.store(c).start()

    def end(self):
        def one(c, carry):
            self.inward_copy(c, self.slot).wait_send()

            @pl.when(self.relay)
            def _():
                self.outward_copy(c).wait_send()

            self.store(c).wait()
            return carry

        lax.fori_loop(0, self.chunks, one, 0)


def line_scratch(rows, width, chunks):
    dma = pltpu.SemaphoreType.DMA
    return [
        pltpu.VMEM((rows, width), bf16),
        pltpu.VMEM((2, rows, width), bf16),
        pltpu.VMEM((rows, width), bf16),
        dma(()),
        dma((chunks,)),
        dma((2, chunks)),
        dma((chunks,)),
        dma((chunks,)),
        dma((chunks,)),
    ]


def line_kernel(n, chunks, part, out, s, land, res, *sems):
    line = Line(n, chunks, part.shape[0] // chunks, part, out, s, land, res, sems)
    line.begin()

    def step(c, carry):
        line.reduce(c)

        @pl.when(c > 0)
        def _():
            line.spread(c - 1)

        return carry

    lax.fori_loop(0, chunks, step, 0)
    line.spread(chunks - 1)
    line.end()


def line_sum(part, collective_id):
    rows, width = part.shape
    n = lax.axis_size("tensor")
    chunks = rows // 48
    return pl.pallas_call(
        functools.partial(line_kernel, n, chunks),
        in_specs=[pl.BlockSpec(memory_space=pl.ANY)],
        out_specs=pl.BlockSpec(memory_space=pl.ANY),
        out_shape=jax.ShapeDtypeStruct(part.shape, bf16),
        scratch_shapes=line_scratch(rows, width, chunks),
        compiler_params=pltpu.CompilerParams(
            collective_id=collective_id, has_side_effects=True, vmem_limit_bytes=48 << 20
        ),
        cost_estimate=cost(rows // 9),
        name="line_sum",
    )(part)


def small_kernel(n, x, out, land, send, recv):
    me = lax.axis_index("tensor")
    barrier = pltpu.get_barrier_semaphore()
    peers = [lax.rem(me + d, n) for d in range(1, n)]
    for peer in peers:
        pl.semaphore_signal(barrier, inc=1, device_id={"tensor": peer}, device_id_type=MESH)
    land[me] = x[...]
    pl.semaphore_wait(barrier, n - 1)
    copies = [
        pltpu.make_async_remote_copy(
            src_ref=x,
            dst_ref=land.at[me],
            send_sem=send.at[d],
            recv_sem=recv.at[me],
            device_id={"tensor": peer},
            device_id_type=MESH,
        )
        for d, peer in enumerate(peers)
    ]
    for copy in copies:
        copy.start()
    for d, peer in enumerate(peers):
        pltpu.make_async_remote_copy(
            src_ref=x,
            dst_ref=land.at[peer],
            send_sem=send.at[d],
            recv_sem=recv.at[peer],
            device_id={"tensor": peer},
            device_id_type=MESH,
        ).wait_recv()
    total = land[0]
    for place in range(1, n):
        total += land[place]
    out[...] = total
    for copy in copies:
        copy.wait_send()


def small_sum(x, collective_id):
    n = lax.axis_size("tensor")
    flat = x.reshape(-1, 128)
    dma = pltpu.SemaphoreType.DMA
    vmem = pl.BlockSpec(memory_space=pltpu.VMEM)
    return pl.pallas_call(
        functools.partial(small_kernel, n),
        in_specs=[vmem],
        out_specs=vmem,
        out_shape=jax.ShapeDtypeStruct(flat.shape, f32),
        scratch_shapes=[pltpu.VMEM((n,) + flat.shape, f32), dma((n - 1,)), dma((n,))],
        compiler_params=pltpu.CompilerParams(
            collective_id=collective_id, has_side_effects=True
        ),
        cost_estimate=cost(7),
        name="small_sum",
    )(flat).reshape(x.shape)


LINE_ROWS = 48
LAG = 3
TILE = 256
NAMES = (
    "part", "x", "cot", "w", "ga", "gm", "first", "proj", "hidden", "inner", "layer", "low",
    "gu", "back", "pre", "grads", "gm_grad", "s", "land", "swap", "res", "acc", "h", "xin", "cin",
    "wgt", "wut", "wdt", "gt", "ut", "it", "jt", "stage", "load_sem", "in_send", "in_recv", "swap_recv",
    "out_send", "out_recv", "store_sem", "w_sem", "x_sem", "c_sem", "h_sem", "y_sem", "t_sem",
    "r_sem", "g_sem",
)


class Mlp:
    def __init__(self, n, micros, rows, *refs):
        for name, ref in zip(NAMES, refs):
            setattr(self, name, ref)
        self.micros, self.rows = micros, rows
        self.chunks = rows // LINE_ROWS
        self.hidden_units = self.w.shape[1] // 3
        self.tiles = self.hidden_units // TILE
        i = lax.axis_index("tensor")
        half = n // 2
        left = i < half
        self.inward = jnp.where(left, i + 1, i - 1)
        self.outward = jnp.where(left, i - 1, i + 1)
        self.relay = (i > 0) & (i < n - 1)
        self.mid = (i == half - 1) | (i == half)

    def at(self, m, c):
        start = pl.multiple_of((m * self.chunks + c) * LINE_ROWS, LINE_ROWS)
        return pl.ds(start, LINE_ROWS)

    def micro(self, m):
        return pl.ds(pl.multiple_of(m * self.rows, self.rows), self.rows)

    def move_in(self, m, c):
        return pltpu.make_async_remote_copy(
            src_ref=self.s.at[self.at(m, c)],
            dst_ref=self.land.at[self.at(m, c)],
            send_sem=self.in_send.at[m, c],
            recv_sem=self.in_recv.at[m, c],
            device_id={"tensor": self.inward},
            device_id_type=MESH,
        )

    def move_swap(self, m, c):
        return pltpu.make_async_remote_copy(
            src_ref=self.s.at[self.at(m, c)],
            dst_ref=self.swap.at[self.at(m, c)],
            send_sem=self.in_send.at[m, c],
            recv_sem=self.swap_recv.at[m, c],
            device_id={"tensor": self.inward},
            device_id_type=MESH,
        )

    def move_out(self, m, c):
        return pltpu.make_async_remote_copy(
            src_ref=self.res.at[self.at(m, c)],
            dst_ref=self.res.at[self.at(m, c)],
            send_sem=self.out_send.at[m, c],
            recv_sem=self.out_recv.at[m, c],
            device_id={"tensor": self.outward},
            device_id_type=MESH,
        )

    def send_in(self, m, c):
        @pl.when(self.mid)
        def _():
            self.move_swap(m, c).start()

        @pl.when(~self.mid)
        def _():
            self.move_in(m, c).start()

    def each_chunk(self, body):
        def one(c, carry):
            body(c)
            return carry

        lax.fori_loop(0, self.chunks, one, 0)

    def launch(self, m):
        @pl.when(~self.relay)
        def _():
            self.each_chunk(lambda c: self.send_in(m, c))

    def settle(self, m):
        def one(c):
            self.move_in(m, c).wait_send()

            @pl.when(self.relay)
            def _():
                self.move_out(m, c).wait_send()

        self.each_chunk(one)

    def begin(self):
        load = pltpu.make_async_copy(self.part, self.s, self.load_sem)
        load.start()
        rest = self.micro(0)
        done = pltpu.make_async_copy(self.first, self.res.at[rest], self.y_sem)
        done.start()
        self.load_x(0, self.x).start()
        for copy in self.load_w(0, 0):
            copy.start()
        barrier = pltpu.get_barrier_semaphore()
        pl.semaphore_signal(
            barrier, inc=1, device_id={"tensor": self.inward}, device_id_type=MESH
        )

        @pl.when(self.relay)
        def _():
            pl.semaphore_signal(
                barrier, inc=1, device_id={"tensor": self.outward}, device_id_type=MESH
            )

        pl.semaphore_wait(barrier, jnp.where(self.relay, 2, 1))
        load.wait()
        done.wait()
        for m in range(1, self.micros):
            self.launch(m)
        self.gm_grad[...] = jnp.zeros_like(self.gm_grad)

    def reduce(self, m, c):
        @pl.when(self.relay)
        def _():
            self.move_in(m, c).wait_recv()
            a = self.at(m, c)
            self.s[a, :] = (self.s[a, :].astype(f32) + self.land[a, :].astype(f32)).astype(bf16)
            self.send_in(m, c)

    def store(self, m, c, to):
        a = self.at(m, c)
        return pltpu.make_async_copy(self.res.at[a], to.at[a], self.store_sem.at[m, c])

    def spread(self, which, m, c):
        a = self.at(m, c)

        @pl.when(self.mid)
        def _():
            self.move_swap(m, c).wait_recv()
            self.res[a, :] = (self.s[a, :].astype(f32) + self.swap[a, :].astype(f32)).astype(bf16)

        @pl.when(~self.mid)
        def _():
            self.move_out(m, c).wait_recv()

        @pl.when(self.relay)
        def _():
            self.move_out(m, c).start()

        @pl.when(which == 0)
        def _():
            self.store(m, c, self.proj).start()

        @pl.when(which == 2)
        def _():
            self.store(m, c, self.back).start()

    def load_x(self, m, source):
        return pltpu.make_async_copy(source.at[self.micro(m)], self.xin, self.x_sem)

    def load_c(self, m):
        return pltpu.make_async_copy(self.cot.at[self.micro(m)], self.cin, self.c_sem)

    def store_h(self, m, to):
        return pltpu.make_async_copy(self.h, to.at[self.micro(m)], self.h_sem)

    def store_layer(self, m):
        return pltpu.make_async_copy(self.xin, self.layer.at[self.micro(m)], self.y_sem)

    def cols(self, t, which=0):
        return pl.ds(pl.multiple_of(which * self.hidden_units + t * TILE, TILE), TILE)

    def load_w(self, t, slot):
        return [
            pltpu.make_async_copy(
                self.w.at[:, self.cols(t, which)], to.at[slot], self.w_sem.at[which, slot]
            )
            for which, to in enumerate((self.wgt, self.wut, self.wdt))
        ]

    def load_pre(self, m, t, slot):
        return [
            pltpu.make_async_copy(
                self.pre.at[self.micro(m), self.cols(t, which)],
                to.at[slot],
                self.r_sem.at[which, slot],
            )
            for which, to in enumerate((self.gt, self.ut))
        ]

    def store_tile(self, which, source, to, m, at, slot):
        return pltpu.make_async_copy(
            source.at[slot], to.at[self.micro(m), at], self.t_sem.at[which, slot]
        )

    def store_pre(self, m, t, slot):
        return (
            self.store_tile(0, self.gt, self.pre, m, self.cols(t, 0), slot),
            self.store_tile(1, self.ut, self.pre, m, self.cols(t, 1), slot),
            self.store_tile(2, self.it, self.inner, m, self.cols(t), slot),
        )

    def store_low(self, m, t, slot):
        return (
            self.store_tile(2, self.it, self.gu, m, self.cols(t, 0), slot),
            self.store_tile(3, self.jt, self.gu, m, self.cols(t, 1), slot),
        )

    def row_groups(self, body):
        step = 16

        def one(r, carry):
            body(pl.ds(pl.multiple_of(r * step, step), step), r * step)
            return carry

        lax.fori_loop(0, self.rows // step, one, 0)

    def forward_start(self, m):
        @pl.when(m > 0)
        def _():
            self.each_chunk(lambda c: self.store(m, c, self.proj).wait())

        self.load_x(m, self.x).wait()
        base = m * self.rows
        gain = self.ga[...]

        def one(at, r):
            total = self.res[pl.ds(pl.multiple_of(base + r, 16), 16), :].astype(f32)
            inv = lax.rsqrt(jnp.mean(total * total, axis=1, keepdims=True) + norm_eps)
            self.h[at, :] = (self.xin[at, :].astype(f32) + total * inv * gain).astype(bf16)

        self.row_groups(one)
        self.store_h(m, self.hidden).start()

    def backward_start(self, m):
        for copy in self.load_pre(m, 0, 0):
            copy.start()
        self.load_x(m, self.hidden).wait()
        self.load_c(m).wait()
        base = m * self.rows
        gain = self.gm[...]

        def one(at, r):
            total = self.res[pl.ds(pl.multiple_of(base + r, 16), 16), :].astype(f32)
            inv = lax.rsqrt(jnp.mean(total * total, axis=1, keepdims=True) + norm_eps)
            unit = total * inv
            c = self.cin[at, :].astype(f32)
            self.xin[at, :] = (self.xin[at, :].astype(f32) + unit * gain).astype(bf16)
            hit = c * unit
            self.gm_grad[...] += hit[0:8, :] + hit[8:16, :]
            dy = c * gain
            inner = jnp.mean(hit * gain, axis=1, keepdims=True)
            self.h[at, :] = (inv * (dy - unit * inner)).astype(bf16)

        self.row_groups(one)
        self.store_layer(m).start()
        self.store_h(m, self.low).start()

    def tile_weights(self, t, slot, last):
        for copy in self.load_w(t, slot):
            copy.wait()

        @pl.when(jnp.logical_not(last))
        def _():
            for copy in self.load_w(lax.rem(t + 1, self.tiles), 1 - slot):
                copy.start()

    def add(self, t, at, value):
        @pl.when(t == 0)
        def _():
            self.acc[:, at] = value

        @pl.when(t > 0)
        def _():
            self.acc[:, at] += value

    def forward_tile(self, m, t):
        slot = lax.rem(t, 2)
        self.tile_weights(t, slot, False)

        @pl.when(t >= 2)
        def _():
            for copy in self.store_pre(m, t - 2, slot):
                copy.wait()

        gate = matmul(self.h[...], self.wgt[slot])
        up = matmul(self.h[...], self.wut[slot])
        self.gt[slot] = gate.astype(bf16)
        self.ut[slot] = up.astype(bf16)
        self.it[slot] = (gate * jax.nn.sigmoid(gate) * up).astype(bf16)
        for copy in self.store_pre(m, t, slot):
            copy.start()
        wide = self.acc.shape[1]
        step = math.gcd(wide, 512)
        for k in range(0, wide, step):
            self.add(t, slice(k, k + step), right_t(self.it[slot], self.wdt[slot, k : k + step, :]))

        @pl.when(t == self.tiles - 1)
        def _():
            for back in range(min(2, self.tiles)):
                at = self.tiles - 1 - back
                for copy in self.store_pre(m, at, at % 2):
                    copy.wait()
            self.store_h(m, self.hidden).wait()
            self.finish(m, m > 0)

    def backward_tile(self, m, t, last):
        slot = lax.rem(t, 2)
        self.tile_weights(t, slot, last & (t == self.tiles - 1))
        for copy in self.load_pre(m, t, slot):
            copy.wait()

        @pl.when(t < self.tiles - 1)
        def _():
            for copy in self.load_pre(m, t + 1, 1 - slot):
                copy.start()

        @pl.when(t >= 2)
        def _():
            for copy in self.store_low(m, t - 2, slot):
                copy.wait()

        grad = matmul(self.h[...], self.wdt[slot])
        gate = self.gt[slot].astype(f32)
        sig = jax.nn.sigmoid(gate)
        act = grad * sig
        self.jt[slot] = (act * gate).astype(bf16)
        self.it[slot] = (
            act * self.ut[slot].astype(f32) * (1.0 + gate * (1.0 - sig))
        ).astype(bf16)
        for copy in self.store_low(m, t, slot):
            copy.start()
        wide = self.acc.shape[1]
        step = math.gcd(wide, 512)
        for k in range(0, wide, step):
            self.add(
                t,
                slice(k, k + step),
                right_t(self.it[slot], self.wgt[slot, k : k + step, :])
                + right_t(self.jt[slot], self.wut[slot, k : k + step, :]),
            )

        @pl.when(t == self.tiles - 1)
        def _():
            for back in range(min(2, self.tiles)):
                at = self.tiles - 1 - back
                for copy in self.store_low(m, at, at % 2):
                    copy.wait()
            self.store_h(m, self.low).wait()
            self.store_layer(m).wait()
            self.finish(m, True)

    def load_bigs(self, source):
        return (
            pltpu.make_async_copy(source.at[self.micro(0)], self.xin, self.x_sem),
            pltpu.make_async_copy(source.at[self.micro(1)], self.cin, self.c_sem),
        )

    def load_units(self, source, w, slot):
        return [
            pltpu.make_async_copy(
                source.at[self.micro(m), self.cols(w)], to.at[slot], self.r_sem.at[m, slot]
            )
            for m, to in enumerate((self.gt, self.ut))
        ]

    def start_units(self, w, slot):
        split = 2 * self.tiles

        @pl.when(w < split)
        def _():
            for copy in self.load_units(self.gu, w, slot):
                copy.start()

        @pl.when((w >= split) & (w < 3 * self.tiles))
        def _():
            for copy in self.load_units(self.inner, w - split, slot):
                copy.start()

    def store_grads(self, w, slot):
        return pltpu.make_async_copy(
            self.stage.at[slot], self.grads.at[:, self.cols(w), :], self.g_sem.at[slot]
        )

    def grad_tile(self, w):
        slot = lax.rem(w, 2)
        split = 2 * self.tiles

        @pl.when((w == 0) | (w == split))
        def _():
            for copy in self.load_bigs(self.hidden):
                copy.wait()

        for copy in self.load_units(self.gu, 0, slot):
            copy.wait()
        self.start_units(w + 1, 1 - slot)

        @pl.when(w >= 2)
        def _():
            self.store_grads(w - 2, slot).wait()

        value = left_t(self.gt[slot], self.xin[...]) + left_t(self.ut[slot], self.cin[...])
        owners, _, wide = self.stage.shape[1:]
        for owner in range(owners):
            self.stage[slot, owner] = value[:, owner * wide : (owner + 1) * wide].astype(bf16)
        self.store_grads(w, slot).start()

        @pl.when(w == split - 1)
        def _():
            for copy in self.load_bigs(self.low):
                copy.start()

        @pl.when(w == 3 * self.tiles - 1)
        def _():
            self.store_grads(w - 1, 1 - slot).wait()
            self.store_grads(w, slot).wait()

    def finish(self, m, sent):
        @pl.when(sent)
        def _():
            self.settle(m)

        base = m * self.rows

        def one(at, r):
            self.s[pl.ds(pl.multiple_of(base + r, 16), 16), :] = self.acc[at, :].astype(bf16)

        self.row_groups(one)
        self.launch(m)

    def job(self, index, step):
        micros = self.micros
        m = lax.rem(index, micros)
        forward = index < micros
        last = index == 2 * micros - 1

        @pl.when(forward & (step == 0))
        def _():
            self.forward_start(m)

        @pl.when(jnp.logical_not(forward) & (step == 0))
        def _():
            self.backward_start(m)

        tiled = (step >= 1) & (step <= self.tiles)

        @pl.when(forward & tiled)
        def _():
            self.forward_tile(m, step - 1)

        @pl.when(jnp.logical_not(forward) & tiled)
        def _():
            self.backward_tile(m, step - 1, last)

        done = step == self.tiles

        @pl.when(done & (index < micros - 1))
        def _():
            self.load_x(index + 1, self.x).start()

        @pl.when(done & (index >= micros - 1) & jnp.logical_not(last))
        def _():
            self.load_x(index + 1 - micros, self.hidden).start()
            self.load_c(index + 1 - micros).start()

        @pl.when(done & last)
        def _():
            for copy in self.load_bigs(self.hidden):
                copy.start()
            self.start_units(0, 0)

    def run(self):
        n, micros = self.chunks, self.micros
        total = 3 * micros * n
        self.begin()

        def clock(k, carry):
            @pl.when(k < total)
            def _():
                self.reduce(lax.rem(k // n, micros), lax.rem(k, n))

            back = k - LAG

            @pl.when((back >= n) & (back < total))
            def _():
                sum_index = back // n
                self.spread(sum_index // micros, lax.rem(sum_index, micros), lax.rem(back, n))

            turn = back - n

            @pl.when((turn >= 0) & (turn < 2 * micros * n))
            def _():
                self.job(turn // n, lax.rem(turn, n))

            turn = turn - 2 * micros * n + n - self.tiles - 1

            @pl.when((turn >= 0) & (turn < 3 * self.tiles))
            def _():
                self.grad_tile(turn)

            return carry

        grads_at = 2 * micros * n + LAG + self.tiles + 1
        lax.fori_loop(n, max(total + LAG, grads_at + 3 * self.tiles), clock, 0)
        for m in range(micros):
            self.settle(m)
            self.each_chunk(lambda c: self.store(m, c, self.back).wait())


def mlp_kernel(n, micros, rows, *refs):
    Mlp(n, micros, rows, *refs).run()


def feed_forward(part, x, cot, w, ga, gm, first, micros, owners):
    assert micros == 2
    both, width = x.shape
    hidden = w.shape[1] // 3
    rows = both // micros
    chunks = rows // LINE_ROWS
    dma = pltpu.SemaphoreType.DMA
    hbm = pl.BlockSpec(memory_space=pl.ANY)
    vmem = pl.BlockSpec(memory_space=pltpu.VMEM)
    wide = jax.ShapeDtypeStruct((both, width), bf16)
    unit = jax.ShapeDtypeStruct((both, hidden), bf16)
    two = jax.ShapeDtypeStruct((both, 2 * hidden), bf16)
    return pl.pallas_call(
        functools.partial(mlp_kernel, lax.axis_size("tensor"), micros, rows),
        in_specs=[hbm] * 4 + [vmem] * 2 + [hbm],
        out_specs=[hbm] * 9 + [vmem],
        out_shape=[wide, wide, unit, wide, wide, two, wide, two]
        + [jax.ShapeDtypeStruct((owners, 3 * hidden, width // owners), bf16)]
        + [jax.ShapeDtypeStruct((8, width), f32)],
        scratch_shapes=[
            pltpu.VMEM((both, width), bf16),
            pltpu.VMEM((both, width), bf16),
            pltpu.VMEM((both, width), bf16),
            pltpu.VMEM((both, width), bf16),
            pltpu.VMEM((rows, width), f32),
            pltpu.VMEM((rows, width), bf16),
            pltpu.VMEM((rows, width), bf16),
            pltpu.VMEM((rows, width), bf16),
            pltpu.VMEM((2, width, TILE), bf16),
            pltpu.VMEM((2, width, TILE), bf16),
            pltpu.VMEM((2, width, TILE), bf16),
            pltpu.VMEM((2, rows, TILE), bf16),
            pltpu.VMEM((2, rows, TILE), bf16),
            pltpu.VMEM((2, rows, TILE), bf16),
            pltpu.VMEM((2, rows, TILE), bf16),
            pltpu.VMEM((2, owners, TILE, width // owners), bf16),
            dma(()),
            dma((micros, chunks)),
            dma((micros, chunks)),
            dma((micros, chunks)),
            dma((micros, chunks)),
            dma((micros, chunks)),
            dma((micros, chunks)),
            dma((3, 2)),
            dma(()),
            dma(()),
            dma(()),
            dma(()),
            dma((4, 2)),
            dma((2, 2)),
            dma((2,)),
        ],
        compiler_params=pltpu.CompilerParams(
            collective_id=1, has_side_effects=True, vmem_limit_bytes=60 << 20
        ),
        cost_estimate=cost(both // 4),
        name="feed_forward",
    )(part, x, cot, w, ga, gm, first)


def attn_scores(meta, i, trunk_rows, q, kt, kp, ko):
    scale = HD ** (-0.5)
    block = meta[i, 0]
    n_par = meta[i, 2]
    n_own = meta[i, 3]
    n_trunk = meta[i, 4]
    st = right_t(q, kt) * scale
    sp = right_t(q, kp) * scale
    so = right_t(q, ko) * scale
    row = lax.broadcasted_iota(jnp.int32, (BLOCK, trunk_rows), 0) + block * BLOCK
    col = lax.broadcasted_iota(jnp.int32, (BLOCK, trunk_rows), 1)
    st = jnp.where((col < n_trunk) & (col <= row), st, masked_score)
    row = lax.broadcasted_iota(jnp.int32, (BLOCK, BLOCK), 0)
    col = lax.broadcasted_iota(jnp.int32, (BLOCK, BLOCK), 1)
    sp = jnp.where(col < n_par, sp, masked_score)
    so = jnp.where((col < n_own) & (col <= row), so, masked_score)
    return st, sp, so


def attn_fwd_kernel(trunk_rows, meta, q, kt, vt, kp, vp, ko, vo, out, lse):
    i = pl.program_id(1)
    st, sp, so = attn_scores(meta, i, trunk_rows, q[...], kt[...], kp[...], ko[...])
    top = jnp.maximum(
        jnp.max(st, axis=1, keepdims=True),
        jnp.maximum(jnp.max(sp, axis=1, keepdims=True), jnp.max(so, axis=1, keepdims=True)),
    )
    et, ep, eo = jnp.exp(st - top), jnp.exp(sp - top), jnp.exp(so - top)
    total = (
        jnp.sum(et, axis=1, keepdims=True)
        + jnp.sum(ep, axis=1, keepdims=True)
        + jnp.sum(eo, axis=1, keepdims=True)
    )
    acc = matmul(et.astype(bf16), vt[...])
    acc += matmul(ep.astype(bf16), vp[...])
    acc += matmul(eo.astype(bf16), vo[...])
    out[...] = (acc / total).astype(bf16)
    lse[...] = jnp.broadcast_to(top + jnp.log(total), (BLOCK, HD))


def attn_bwd_kernel(
    trunk_rows, n_q, meta, q, do, lse, kt, vt, kp, vp, ko, vo,
    dq, dko, dvo, dkt, dvt, dkb, dvb, a_kt, a_vt, a_kb, a_vb,
):
    i = pl.program_id(1)

    @pl.when(i == 0)
    def _():
        for acc in (a_kt, a_vt, a_kb, a_vb):
            acc[...] = jnp.zeros_like(acc)

    scale = HD ** (-0.5)
    qv, dov = q[...], do[...]
    scores = attn_scores(meta, i, trunk_rows, qv, kt[...], kp[...], ko[...])
    top = lse[:, 0:1]
    probs = [jnp.exp(s - top) for s in scores]
    grads = [right_t(dov, v[...]) for v in (vt, vp, vo)]
    inner = sum(jnp.sum(p * g, axis=1, keepdims=True) for p, g in zip(probs, grads))
    low = [(p * (g - inner)).astype(bf16) for p, g in zip(probs, grads)]
    probs = [p.astype(bf16) for p in probs]
    dq[...] = scale * (
        matmul(low[0], kt[...]) + matmul(low[1], kp[...]) + matmul(low[2], ko[...])
    )
    a_kt[...] += left_t(low[0], qv)
    a_vt[...] += left_t(probs[0], dov)
    dko[...] = scale * left_t(low[2], qv)
    dvo[...] = left_t(probs[2], dov)
    at = pl.ds(pl.multiple_of(meta[i, 1] * BLOCK, BLOCK), BLOCK)
    a_kb[at, :] += left_t(low[1], qv)
    a_vb[at, :] += left_t(probs[1], dov)

    @pl.when(i == n_q - 1)
    def _():
        dkt[...] = (scale * a_kt[...]).astype(bf16)
        dvt[...] = a_vt[...].astype(bf16)
        dkb[...] = (scale * a_kb[...]).astype(bf16)
        dvb[...] = a_vb[...].astype(bf16)


def kv_specs(trunk_rows):
    trunk = pl.BlockSpec((trunk_rows, HD), lambda h, i, meta: (0, h))
    par = pl.BlockSpec((BLOCK, HD), lambda h, i, meta: (meta[i, 1], h))
    own = pl.BlockSpec((BLOCK, HD), lambda h, i, meta: (i, h))
    return [trunk, trunk, par, par, own, own]


def attend_forward(meta, q, kv):
    rows, width = q.shape
    trunk_rows = kv[0].shape[0]
    own = pl.BlockSpec((BLOCK, HD), lambda h, i, meta: (i, h))
    return pl.pallas_call(
        functools.partial(attn_fwd_kernel, trunk_rows),
        grid_spec=pltpu.PrefetchScalarGridSpec(
            num_scalar_prefetch=1,
            grid=(width // HD, rows // BLOCK),
            in_specs=[own] + kv_specs(trunk_rows),
            out_specs=[own, own],
        ),
        out_shape=[
            jax.ShapeDtypeStruct((rows, width), bf16),
            jax.ShapeDtypeStruct((rows, width), f32),
        ],
        compiler_params=pltpu.CompilerParams(vmem_limit_bytes=32 << 20),
        cost_estimate=cost(12),
        name="attend_forward",
    )(meta, q, *kv)


def attend_backward(meta, q, do, lse, kv):
    rows, width = q.shape
    trunk_rows = kv[0].shape[0]
    branch_rows = kv[2].shape[0]
    own = pl.BlockSpec((BLOCK, HD), lambda h, i, meta: (i, h))
    trunk = pl.BlockSpec((trunk_rows, HD), lambda h, i, meta: (0, h))
    branch = pl.BlockSpec((branch_rows, HD), lambda h, i, meta: (0, h))
    n_q = rows // BLOCK
    return pl.pallas_call(
        functools.partial(attn_bwd_kernel, trunk_rows, n_q),
        grid_spec=pltpu.PrefetchScalarGridSpec(
            num_scalar_prefetch=1,
            grid=(width // HD, n_q),
            in_specs=[own, own, own] + kv_specs(trunk_rows),
            out_specs=[own, own, own, trunk, trunk, branch, branch],
            scratch_shapes=[
                pltpu.VMEM((trunk_rows, HD), f32),
                pltpu.VMEM((trunk_rows, HD), f32),
                pltpu.VMEM((branch_rows, HD), f32),
                pltpu.VMEM((branch_rows, HD), f32),
            ],
        ),
        out_shape=[
            jax.ShapeDtypeStruct((rows, width), f32),
            jax.ShapeDtypeStruct((rows, width), f32),
            jax.ShapeDtypeStruct((rows, width), f32),
            jax.ShapeDtypeStruct((trunk_rows, width), bf16),
            jax.ShapeDtypeStruct((trunk_rows, width), bf16),
            jax.ShapeDtypeStruct((branch_rows, width), bf16),
            jax.ShapeDtypeStruct((branch_rows, width), bf16),
        ],
        compiler_params=pltpu.CompilerParams(vmem_limit_bytes=40 << 20),
        cost_estimate=cost(22),
        name="attend_backward",
    )(meta, q, do, lse, *kv)


def group_perm(n, k):
    half = n // 2
    return [(i, i // half * half + (i % half + k) % half) for i in range(n)]


def fetch_sources(block, hold):
    n = lax.axis_size("seq")
    half = n // 2
    place = lax.axis_index("seq")
    spot = lax.rem(place, half)
    got = lax.ppermute(block, "seq", [(i, i + half) for i in range(half)])
    mine = jnp.where(place < half, block, got if hold is None else after(got, hold))
    parts = [mine] + [lax.ppermute(mine, "seq", group_perm(n, k)) for k in range(1, half)]
    out = []
    for source in range(half):
        pick = parts[0]
        for k in range(1, half):
            pick = jnp.where(lax.rem(spot - k + half, half) == source, parts[k], pick)
        out.append(pick)
    return jnp.concatenate(out, axis=0)


def sum_over_group(grads):
    n = lax.axis_size("seq")
    half = n // 2
    spot = lax.rem(lax.axis_index("seq"), half)
    rows = grads.shape[0] // half
    pieces = [grads[s * rows : (s + 1) * rows] for s in range(half)]

    def piece(index):
        pick = pieces[0]
        for s in range(1, half):
            pick = jnp.where(index == s, pieces[s], pick)
        return pick

    total = piece(spot).astype(f32)
    for k in range(1, half):
        sent = piece(lax.rem(spot + k, half))
        total += lax.ppermute(sent, "seq", group_perm(n, k)).astype(f32)
    return total.astype(bf16)


def return_to_sources(total):
    n = lax.axis_size("seq")
    half = n // 2
    got = lax.ppermute(total, "seq", [(i + half, i) for i in range(half)])
    both = total.astype(f32) + got.astype(f32)
    return jnp.where(lax.axis_index("seq") < half, both, 0.0)


def gather_rows(item):
    return lax.all_gather(item, ("dp", "seq"), axis=0, tiled=True)


def scatter_rows(item):
    return lax.psum_scatter(
        item.astype(bf16), ("dp", "seq"), scatter_dimension=0, tiled=True
    ).astype(f32)


def block_meta(parents, lengths, rows, n_blocks):
    seg_count = parents.shape[0]
    branches = (seg_count - 1) // 3
    trunk_blocks = n_blocks - 3 * branches
    blocks = lax.axis_index("seq") * (rows // BLOCK) + jnp.arange(rows // BLOCK, dtype=jnp.int32)
    seg = jnp.maximum(blocks - trunk_blocks + 1, 0)
    hit = seg[:, None] == jnp.arange(seg_count, dtype=jnp.int32)[None, :]
    parent = jnp.sum(jnp.where(hit, parents[None, :], 0), axis=1)
    own_len = jnp.sum(jnp.where(hit, lengths[None, :], 0), axis=1)
    hit = parent[:, None] == jnp.arange(seg_count, dtype=jnp.int32)[None, :]
    par_len = jnp.sum(jnp.where(hit, lengths[None, :], 0), axis=1)
    return jnp.stack(
        [
            blocks,
            jnp.maximum(parent - 1, 0),
            jnp.where(parent > 0, par_len, 0),
            jnp.where(blocks >= trunk_blocks, own_len, 0),
            jnp.broadcast_to(lengths[0], blocks.shape),
        ],
        axis=1,
    ).astype(jnp.int32)


def per_device(
    tokens, cotangent, w_query, w_key, w_value, w_out, w_gate, w_up, w_down,
    query_gain, key_gain, attn_gain, mlp_gain, parent_of, seg_length,
):
    micros, _, rows, width = tokens.shape
    n_blocks = rows // BLOCK * lax.axis_size("seq")
    heads = w_query.shape[1] // HD
    full_width = heads * HD * lax.axis_size("tensor")
    branches = (parent_of.shape[2] - 1) // 3
    trunk_rows = (n_blocks - 3 * branches) * BLOCK

    cols = w_query.shape[1]
    owners = lax.axis_size("dp") * lax.axis_size("seq")
    w_attn = gather_rows(jnp.concatenate([w_query, w_key, w_value, w_out.T], axis=1))
    gains = [query_gain.reshape(-1), key_gain.reshape(-1), attn_gain, mlp_gain]
    gains = lax.all_gather(jnp.concatenate(gains), ("dp", "seq"), axis=0, tiled=False)
    own = query_gain.size

    def head_gain(block):
        block = block.reshape(owners, heads, HD // owners)
        return jnp.swapaxes(block, 0, 1).reshape(-1).astype(f32)

    q_gain = head_gain(gains[:, :own])
    k_gain = head_gain(gains[:, own : 2 * own])
    a_gain = gains[:, 2 * own : 2 * own + attn_gain.size].reshape(-1).astype(f32)
    m_gain = gains[:, 2 * own + attn_gain.size :].reshape(-1).astype(f32)
    wq, wk, wv = (w_attn[:, k * cols : (k + 1) * cols] for k in range(3))
    wo_t = w_attn[:, 3 * cols :]

    def part_of(array, m):
        return array[m * rows : (m + 1) * rows]

    x = tokens.reshape(micros * rows, width)
    cot = cotangent.reshape(micros * rows, width)
    q_raw, k_raw, v_raw = matmul(x, wq), matmul(x, wk), matmul(x, wv)
    q_sq, k_sq = small_sum(
        jnp.stack([jnp.sum(q_raw * q_raw, axis=1), jnp.sum(k_raw * k_raw, axis=1)]), 2
    )
    q_inv = lax.rsqrt(q_sq / full_width + norm_eps)[:, None]
    k_inv = lax.rsqrt(k_sq / full_width + norm_eps)[:, None]
    q_unit, k_unit = q_raw * q_inv, k_raw * k_inv
    q_low = (q_unit * q_gain).astype(bf16)
    k_low = (k_unit * k_gain).astype(bf16)
    v_low = v_raw.astype(bf16)

    kvs, metas, attn_lows, lses, parts, first = [], [], [], [], [], None
    for m in range(micros):
        k_own, v_own = part_of(k_low, m), part_of(v_low, m)
        sources = fetch_sources(jnp.concatenate([k_own, v_own], axis=1), first)
        kvs.append(
            (
                sources[:trunk_rows, :cols],
                sources[:trunk_rows, cols:],
                sources[trunk_rows:, :cols],
                sources[trunk_rows:, cols:],
                k_own,
                v_own,
            )
        )
        metas.append(block_meta(parent_of[m, 0], seg_length[m, 0], rows, n_blocks))
        attn_low, lse = attend_forward(metas[m], part_of(q_low, m), kvs[m])
        attn_lows.append(attn_low)
        lses.append(lse)
        parts.append(right_t(attn_low, wo_t).astype(bf16))
        if m == 0:
            first = line_sum(parts[0], 0)
            w_own = jnp.concatenate([w_gate, w_up, w_down.T], axis=1)
            w_mlp = gather_rows(after(w_own, sources))
    proj, _, _, layer_out, _, _, back, _, mlp_grads, gm_grad = feed_forward(
        jnp.concatenate(parts, axis=0), x, cot, w_mlp, a_gain[None], m_gain[None], first,
        micros, owners,
    )
    units = w_gate.shape[1]
    ga_grad = 0.0
    proj_lows, dqs, owns, sums = [], [], [], []
    for m in range(micros):
        attn_proj = (first if m == 0 else part_of(proj, m)).astype(f32)
        attn_inv = lax.rsqrt(jnp.mean(attn_proj * attn_proj, axis=1, keepdims=True) + norm_eps)
        attn_unit = attn_proj * attn_inv
        hidden_grad = part_of(cot, m).astype(f32) + part_of(back, m).astype(f32)
        ga_grad += jnp.sum(hidden_grad * attn_unit, axis=0)
        unit_grad = hidden_grad * a_gain
        proj_low = (
            attn_inv
            * (unit_grad - attn_unit * jnp.mean(unit_grad * attn_unit, axis=1, keepdims=True))
        ).astype(bf16)
        attn_grad = matmul(proj_low, wo_t).astype(bf16)
        if m > 0:
            attn_grad = after(attn_grad, sums[-1])
        dq, dko, dvo, dkt, dvt, dkb, dvb = attend_backward(
            metas[m], part_of(q_low, m), attn_grad, lses[m], kvs[m]
        )
        sums.append(
            sum_over_group(
                jnp.concatenate(
                    [jnp.concatenate([dkt, dvt], axis=1), jnp.concatenate([dkb, dvb], axis=1)],
                    axis=0,
                )
            )
        )
        proj_lows.append(proj_low)
        dqs.append(dq)
        owns.append((dko, dvo))

    qkv_lows, lasts = [], []
    qg_grad = kg_grad = g_qkv = 0.0
    for m in range(micros):
        got = return_to_sources(sums[m])
        if m > 0:
            got = after(got, lasts[-1])
        else:
            got = after(got, dqs[-1])
            mlp_grads = after(mlp_grads.reshape(-1, mlp_grads.shape[2]), got)
            mlp_grads = scatter_rows(mlp_grads)
        dq, dk, dv = dqs[m], owns[m][0] + got[:, :cols], owns[m][1] + got[:, cols:]
        q_u, k_u = part_of(q_unit, m), part_of(k_unit, m)
        qg_grad += jnp.sum(dq * q_u, axis=0)
        kg_grad += jnp.sum(dk * k_u, axis=0)
        q_scaled, k_scaled = dq * q_gain, dk * k_gain
        q_inner, k_inner = small_sum(
            jnp.stack([jnp.sum(q_scaled * q_u, axis=1), jnp.sum(k_scaled * k_u, axis=1)]), 4
        )
        q_inner, k_inner = q_inner[:, None] / full_width, k_inner[:, None] / full_width
        qr_low = (part_of(q_inv, m) * (q_scaled - q_u * q_inner)).astype(bf16)
        kr_low = (part_of(k_inv, m) * (k_scaled - k_u * k_inner)).astype(bf16)
        qkv_lows.append(jnp.concatenate([qr_low, kr_low, dv.astype(bf16)], axis=1))
        part = right_t(qkv_lows[m], w_attn[:, : 3 * cols]).astype(bf16)
        g_qkv += left_t(part_of(x, m), qkv_lows[m])
        if m > 0:
            g_qkv = g_qkv.astype(bf16)
            part = after(part, g_qkv)
        lasts.append(line_sum(part, 3))
    g_qkv = scatter_rows(g_qkv)
    last = jnp.concatenate(lasts, axis=0)

    def head_grad(value):
        return jnp.swapaxes(value.reshape(heads, owners, HD // owners), 0, 1).reshape(owners, -1)

    gain_grads = jnp.concatenate(
        [
            head_grad(qg_grad),
            head_grad(kg_grad),
            ga_grad.reshape(owners, -1),
            jnp.sum(gm_grad, axis=0).reshape(owners, -1),
        ],
        axis=1,
    )
    count = gain_grads.shape[1]
    lines = -(-count // 128)
    gain_grads = jnp.pad(gain_grads, ((0, 0), (0, lines * 128 - count)))
    gain_grads = gain_grads.reshape(owners, lines, 128)
    gain_grads = jnp.pad(gain_grads, ((0, 0), (0, width // owners - lines), (0, 0)))
    proj_low = after(jnp.concatenate(proj_lows, axis=0), lasts[0])
    g_out = left_t(proj_low, jnp.concatenate(attn_lows, axis=0))
    g_out = jnp.concatenate([g_out, gain_grads.reshape(width, 128)], axis=1).astype(bf16)
    g_out = scatter_rows(after(g_out, mlp_grads))
    gain_grads = g_out[:lines, cols:].reshape(-1)
    input_grad = cot.astype(f32) + back.astype(f32) + last.astype(f32)
    return (
        layer_out.reshape(tokens.shape),
        input_grad.reshape(tokens.shape),
        g_qkv[:, :cols],
        g_qkv[:, cols : 2 * cols],
        g_qkv[:, 2 * cols :],
        g_out[:, :cols].T,
        mlp_grads[:units].T,
        mlp_grads[units : 2 * units].T,
        mlp_grads[2 * units :],
        gain_grads[:own].reshape(query_gain.shape),
        gain_grads[own : 2 * own].reshape(key_gain.shape),
        gain_grads[2 * own : 2 * own + attn_gain.size],
        gain_grads[2 * own + attn_gain.size : count],
    )


def solution(mesh):
    rows = P(None, "dp", "seq", None)
    by_row = P(("dp", "seq"), "tensor")
    by_col = P("tensor", ("dp", "seq"))
    gain = P(("dp", "seq"))
    tree = P(None, "dp", None)
    weights = (by_row, by_row, by_row, by_col, by_row, by_row, by_col, by_col, by_col, gain, gain)
    return jax.shard_map(
        per_device,
        mesh=mesh,
        in_specs=(rows, rows) + weights + (tree, tree),
        out_specs=(rows, rows) + weights,
        check_vma=False,
    )
```

```python
import functools
import math

import jax
import jax.numpy as jnp
from jax import lax
from jax.experimental import pallas as pl
from jax.experimental.pallas import tpu as pltpu
from jax.sharding import PartitionSpec as P

HD = 128
BLOCK = 256

norm_eps = 1e-06
masked_score = -1e30
f32 = jnp.float32
bf16 = jnp.bfloat16


def matmul(left, right):
    return jnp.dot(left, right, preferred_element_type=f32)


def left_t(left, right):
    return lax.dot_general(left, right, (((0,), (0,)), ((), ())), preferred_element_type=f32)


def right_t(left, right):
    return lax.dot_general(left, right, (((1,), (1,)), ((), ())), preferred_element_type=f32)


MESH = pl.DeviceIdType.MESH


def cost(us):
    return pl.CostEstimate(flops=int(us * 1.1e9), bytes_accessed=0, transcendentals=0)


def fold(rows):
    total = rows[0:8]
    for j in range(8, rows.shape[0], 8):
        total += rows[j : j + 8]
    return total


def after(value, *earlier):
    hbm = pl.BlockSpec(memory_space=pl.ANY)
    return pl.pallas_call(
        lambda *refs: None,
        in_specs=[hbm] * (1 + len(earlier)),
        out_specs=hbm,
        out_shape=jax.ShapeDtypeStruct(value.shape, value.dtype),
        input_output_aliases={0: 0},
        name="after",
    )(value, *earlier)


class Line:
    def __init__(self, n, chunks, rows, part, out, s, land, res, sems):
        self.chunks, self.rows = chunks, rows
        self.part, self.out, self.s, self.land, self.res = part, out, s, land, res
        (
            self.load_sem,
            self.in_send,
            self.in_recv,
            self.out_send,
            self.out_recv,
            self.store_sem,
        ) = sems
        i = lax.axis_index("tensor")
        half = n // 2
        left = i < half
        self.inward = jnp.where(left, i + 1, i - 1)
        self.outward = jnp.where(left, i - 1, i + 1)
        self.relay = (i > 0) & (i < n - 1)
        self.mid = (i == half - 1) | (i == half)
        self.slot = jnp.where(self.mid, 1, 0)

    def at(self, c):
        return pl.ds(pl.multiple_of(c * self.rows, self.rows), self.rows)

    def load(self):
        return pltpu.make_async_copy(self.part, self.s, self.load_sem)

    def inward_copy(self, c, slot):
        return pltpu.make_async_remote_copy(
            src_ref=self.s.at[self.at(c)],
            dst_ref=self.land.at[slot, self.at(c)],
            send_sem=self.in_send.at[c],
            recv_sem=self.in_recv.at[slot, c],
            device_id={"tensor": self.inward},
            device_id_type=MESH,
        )

    def outward_copy(self, c):
        return pltpu.make_async_remote_copy(
            src_ref=self.res.at[self.at(c)],
            dst_ref=self.res.at[self.at(c)],
            send_sem=self.out_send.at[c],
            recv_sem=self.out_recv.at[c],
            device_id={"tensor": self.outward},
            device_id_type=MESH,
        )

    def store(self, c):
        return pltpu.make_async_copy(
            self.res.at[self.at(c)], self.out.at[self.at(c)], self.store_sem.at[c]
        )

    def begin(self):
        self.load().start()
        barrier = pltpu.get_barrier_semaphore()
        pl.semaphore_signal(
            barrier, inc=1, device_id={"tensor": self.inward}, device_id_type=MESH
        )

        @pl.when(self.relay)
        def _():
            pl.semaphore_signal(
                barrier, inc=1, device_id={"tensor": self.outward}, device_id_type=MESH
            )

        pl.semaphore_wait(barrier, jnp.where(self.relay, 2, 1))
        self.load().wait()
        self.launch(0, self.chunks)

    def launch(self, first, last):
        @pl.when(~self.relay)
        def _():
            def one(c, carry):
                self.inward_copy(c, self.slot).start()
                return carry

            lax.fori_loop(first, last, one, 0)

    def stream(self, job=None):
        def step(c, carry):
            if job is not None:
                job(c)
            self.reduce(c)

            @pl.when(c > 0)
            def _():
                self.spread(c - 1)

            return carry

        lax.fori_loop(0, self.chunks, step, 0)
        self.spread(self.chunks - 1)
        self.end()

    def reduce(self, c):
        @pl.when(self.relay)
        def _():
            self.inward_copy(c, 0).wait_recv()
            a = self.at(c)
            self.s[a, :] = (self.s[a, :].astype(f32) + self.land[0, a, :].astype(f32)).astype(bf16)
            self.inward_copy(c, self.slot).start()

    def spread(self, c):
        a = self.at(c)

        @pl.when(self.mid)
        def _():
            self.inward_copy(c, 1).wait_recv()
            self.res[a, :] = (
                self.s[a, :].astype(f32) + self.land[1, a, :].astype(f32)
            ).astype(bf16)

        @pl.when(~self.mid)
        def _():
            self.outward_copy(c).wait_recv()

        @pl.when(self.relay)
        def _():
            self.outward_copy(c).start()

        self.store(c).start()

    def end(self):
        def one(c, carry):
            self.inward_copy(c, self.slot).wait_send()

            @pl.when(self.relay)
            def _():
                self.outward_copy(c).wait_send()

            self.store(c).wait()
            return carry

        lax.fori_loop(0, self.chunks, one, 0)


def line_scratch(rows, width, chunks):
    dma = pltpu.SemaphoreType.DMA
    return [
        pltpu.VMEM((rows, width), bf16),
        pltpu.VMEM((2, rows, width), bf16),
        pltpu.VMEM((rows, width), bf16),
        dma(()),
        dma((chunks,)),
        dma((2, chunks)),
        dma((chunks,)),
        dma((chunks,)),
        dma((chunks,)),
    ]


def line_kernel(n, chunks, part, out, s, land, res, *sems):
    line = Line(n, chunks, part.shape[0] // chunks, part, out, s, land, res, sems)
    line.begin()
    line.stream()


def line_sum(part, collective_id):
    rows, width = part.shape
    n = lax.axis_size("tensor")
    chunks = rows // 48
    return pl.pallas_call(
        functools.partial(line_kernel, n, chunks),
        in_specs=[pl.BlockSpec(memory_space=pl.ANY)],
        out_specs=pl.BlockSpec(memory_space=pl.ANY),
        out_shape=jax.ShapeDtypeStruct(part.shape, bf16),
        scratch_shapes=line_scratch(rows, width, chunks),
        compiler_params=pltpu.CompilerParams(
            collective_id=collective_id, has_side_effects=True, vmem_limit_bytes=60 << 20
        ),
        cost_estimate=cost(rows // 9),
        name="line_sum",
    )(part)


LANES = 128


def diagonal():
    shape = (LANES, LANES)
    return lax.broadcasted_iota(jnp.int32, shape, 0) == lax.broadcasted_iota(jnp.int32, shape, 1)


def to_line(column):
    return jnp.sum(jnp.where(diagonal(), column, 0.0), axis=0, keepdims=True)


def to_column(line):
    return jnp.sum(jnp.where(diagonal(), line, 0.0), axis=1, keepdims=True)


class Exchange:
    def __init__(self, n, lines, land, send, recv):
        self.n, self.lines, self.land, self.send, self.recv = n, lines, land, send, recv
        self.me = lax.axis_index("tensor")
        self.peers = [lax.rem(self.me + d, n) for d in range(1, n)]

    def greet(self):
        barrier = pltpu.get_barrier_semaphore()
        for peer in self.peers:
            pl.semaphore_signal(barrier, inc=1, device_id={"tensor": peer}, device_id_type=MESH)

    def met(self):
        pl.semaphore_wait(pltpu.get_barrier_semaphore(), self.n - 1)

    def copy(self, d, peer, slot):
        return pltpu.make_async_remote_copy(
            src_ref=self.lines,
            dst_ref=self.land.at[slot],
            send_sem=self.send.at[d],
            recv_sem=self.recv.at[slot],
            device_id={"tensor": peer},
            device_id_type=MESH,
        )

    def total(self):
        self.land[self.me] = self.lines[...]
        for d, peer in enumerate(self.peers):
            self.copy(d, peer, self.me).start()
        for d, peer in enumerate(self.peers):
            self.copy(d, peer, peer).wait_recv()
        total = self.land[0]
        for place in range(1, self.n):
            total += self.land[place]
        for d, peer in enumerate(self.peers):
            self.copy(d, peer, self.me).wait_send()
        return total


def exchange_scratch(n, lines):
    dma = pltpu.SemaphoreType.DMA
    return [
        pltpu.VMEM((2 * lines, LANES), f32),
        pltpu.VMEM((n, 2 * lines, LANES), f32),
        dma((n - 1,)),
        dma((n,)),
    ]


def line_count(rows):
    return -(-rows // LANES // 8) * 8


def qkv_kernel(n, rows, cols, x, w, qg, kg, q_low, kv_low, units, squares, raw, *net):
    swap = Exchange(n, *net)
    swap.greet()
    lines = swap.lines.shape[0] // 2
    swap.lines[...] = jnp.zeros_like(swap.lines)
    step = math.gcd(rows, 384)
    for r in range(0, rows, step):
        at = slice(r, r + step)
        for k in range(2):
            value = matmul(x[at, :], w[:, k * cols : (k + 1) * cols])
            raw[k, at, :] = value
            square = jnp.sum(value * value, axis=1, keepdims=True)
            for j in range(0, step, LANES):
                spot = k * lines + (r + j) // LANES
                swap.lines[spot : spot + 1, :] = to_line(square[j : j + LANES])
    swap.met()
    for r in range(0, rows, step):
        at = slice(r, r + step)
        kv_low[1, at, :] = matmul(x[at, :], w[:, 2 * cols : 3 * cols]).astype(bf16)
    total = swap.total()
    squares[...] = total
    width = n * cols
    for r in range(0, rows, LANES):
        at = slice(r, r + LANES)
        for k, gain in enumerate((qg, kg)):
            spot = k * lines + r // LANES
            square = to_column(total[spot : spot + 1, :])
            unit = raw[k, at, :] * lax.rsqrt(square / width + norm_eps)
            units[k, at, :] = unit
            low = (unit * gain[...]).astype(bf16)
            if k == 0:
                q_low[at, :] = low
            else:
                kv_low[0, at, :] = low


def qkv(x, w, qg, kg, m, rows, collective_id):
    n = lax.axis_size("tensor")
    width = x.shape[1]
    cols = qg.shape[1]
    lines = line_count(rows)
    vmem = pl.BlockSpec(memory_space=pltpu.VMEM)
    return pl.pallas_call(
        functools.partial(qkv_kernel, n, rows, cols),
        grid=(1,),
        in_specs=[
            pl.BlockSpec((rows, width), lambda i: (m, 0)),
            pl.BlockSpec((width, 3 * cols), lambda i: (0, 0)),
            vmem,
            vmem,
        ],
        out_specs=[vmem] * 4,
        out_shape=[
            jax.ShapeDtypeStruct((rows, cols), bf16),
            jax.ShapeDtypeStruct((2, rows, cols), bf16),
            jax.ShapeDtypeStruct((2, rows, cols), f32),
            jax.ShapeDtypeStruct((2 * lines, LANES), f32),
        ],
        scratch_shapes=[pltpu.VMEM((2, rows, cols), f32)] + exchange_scratch(n, lines),
        compiler_params=pltpu.CompilerParams(
            collective_id=collective_id, has_side_effects=True, vmem_limit_bytes=60 << 20
        ),
        cost_estimate=cost(15),
        name="qkv",
    )(x, w, qg, kg)


def proj_kernel(cot, back, proj, gain, wo_t, layer, *refs):
    low, grad, gain_grad, layer_out = refs[-4:]
    layer_out[...] = layer[...]

    @pl.when(pl.program_id(0) == 0)
    def _():
        gain_grad[...] = jnp.zeros_like(gain_grad)

    step = ROW_STEP

    def one(r, carry):
        at = pl.ds(pl.multiple_of(r * step, step), step)
        value = proj[at, :].astype(f32)
        inv = lax.rsqrt(jnp.mean(value * value, axis=1, keepdims=True) + norm_eps)
        unit = value * inv
        hidden = cot[at, :].astype(f32) + back[at, :].astype(f32)
        hit = hidden * unit
        gain_grad[...] += fold(hit)
        inner = jnp.mean(hit * gain[...], axis=1, keepdims=True)
        low[at, :] = (inv * (hidden * gain[...] - unit * inner)).astype(bf16)
        return carry

    lax.fori_loop(0, low.shape[0] // step, one, 0)
    grad[...] = matmul(low[...], wo_t[...]).astype(bf16)


def proj_backward(cot, back, proj, gain, w, layer, layer_out, cols, m, rows, proj_m):
    width = cot.shape[1]
    step = BLOCK
    blocks = rows // step

    earlier = [] if layer_out is None else [layer_out]

    def whole(first):
        return pl.BlockSpec((step, width), lambda i: (first * blocks + i, 0))

    return pl.pallas_call(
        proj_kernel,
        grid=(blocks,),
        in_specs=[
            whole(m),
            whole(m),
            whole(proj_m),
            pl.BlockSpec((1, width), lambda i: (0, 0)),
            pl.BlockSpec((width, cols), lambda i: (0, 3)),
            whole(m),
        ]
        + [pl.BlockSpec(memory_space=pl.ANY)] * len(earlier),
        out_specs=[
            whole(0),
            pl.BlockSpec((step, cols), lambda i: (i, 0)),
            pl.BlockSpec((8, width), lambda i: (0, 0)),
            whole(m),
        ],
        out_shape=[
            jax.ShapeDtypeStruct((rows, width), bf16),
            jax.ShapeDtypeStruct((rows, cols), bf16),
            jax.ShapeDtypeStruct((8, width), f32),
            jax.ShapeDtypeStruct(cot.shape, bf16),
        ],
        input_output_aliases={6: 3} if earlier else {},
        compiler_params=pltpu.CompilerParams(vmem_limit_bytes=60 << 20),
        cost_estimate=cost(10),
        name="proj_backward",
    )(cot, back, proj, gain, w, layer, *earlier)


class Grads:
    def __init__(self, to, stage, sem):
        self.to, self.stage, self.sem = to, stage, sem
        self.wide = stage.shape[1]

    def at(self, owner):
        return pl.ds(pl.multiple_of(owner * self.wide, self.wide), self.wide)

    def store(self, owner, slot):
        width = self.stage.shape[2]
        return pltpu.make_async_copy(
            self.stage.at[slot], self.to.at[self.at(owner), pl.ds(0, width)], self.sem.at[slot]
        )


def last_kernel(
    n, rows, cols, sources, stream, dq, own, mine, got, units, squares, qg, kg, x, proj, attn,
    before, others, w, low, out, gain_grad, g_attn, *scratch,
):
    swap = Exchange(n, *scratch[:4])
    swap.greet()
    xin, x_sem, stage, g_sem = scratch[4:8]
    load_x = pltpu.make_async_copy(x.at[0 if stream else 1], xin, x_sem)
    load_x.start()
    grads = Grads(g_attn, stage, g_sem)
    owners = xin.shape[1] // grads.wide
    if stream:
        s, land, res, pin, p_sem = scratch[8:13]
        loads = [pltpu.make_async_copy(proj[m], pin.at[m], p_sem.at[m]) for m in range(2)]
        for load in loads:
            load.start()
    else:
        s = out
        had, b_sem, gains, n_sem = scratch[8:12]

        def load_before(owner, slot):
            return pltpu.make_async_copy(
                before.at[grads.at(owner), pl.ds(0, 3 * cols)], had.at[slot], b_sem.at[slot]
            )

        load_before(0, 0).start()
    lines = swap.lines.shape[0] // 2
    swap.lines[...] = jnp.zeros_like(swap.lines)
    gain_grad[...] = jnp.zeros_like(gain_grad)
    scale = jnp.where(sources, 1.0, 0.0).astype(f32)
    width = n * cols

    def gathered(k, at):
        both = mine[k, at, :].astype(f32) + got[k, at, :].astype(f32)
        return own[k, at, :] + scale * both

    for r in range(0, rows, LANES):
        at = slice(r, r + LANES)
        for k, gain in enumerate((qg, kg)):
            grad = dq[at, :] if k == 0 else gathered(0, at)
            hit = grad * units[k, at, :]
            gain_grad[8 * k : 8 * k + 8, :] += fold(hit)
            spot = k * lines + r // LANES
            swap.lines[spot : spot + 1, :] = to_line(
                jnp.sum(hit * gain[...], axis=1, keepdims=True)
            )
    swap.met()
    total = swap.total()
    for r in range(0, rows, LANES):
        at = slice(r, r + LANES)
        for k, gain in enumerate((qg, kg)):
            spot = k * lines + r // LANES
            inner = to_column(total[spot : spot + 1, :]) / width
            inv = lax.rsqrt(to_column(squares[spot : spot + 1, :]) / width + norm_eps)
            grad = dq[at, :] if k == 0 else gathered(0, at)
            value = inv * (grad * gain[...] - units[k, at, :] * inner)
            low[at, k * cols : (k + 1) * cols] = value.astype(bf16)
        low[at, 2 * cols :] = gathered(1, at).astype(bf16)
    if stream:
        line = Line(n, out.shape[0] // 48, 48, None, out, s, land, res, scratch[13:])
    step = math.gcd(rows, 384)
    piece = math.gcd(s.shape[1], 512)
    for r in range(0, rows, step):
        at = slice(r, r + step)
        for c in range(0, s.shape[1], piece):
            s[at, c : c + piece] = right_t(low[at, :], w[c : c + piece, :]).astype(bf16)
        if stream:
            line.launch(r // 48, (r + step) // 48)

    def narrow(array, owner, small):
        return left_t(array[:, grads.at(owner)], small)

    def drain():
        for owner in range(max(owners - 2, 0), owners):
            grads.store(owner, owner % 2).wait()

    if stream:

        def job(owner):
            slot = lax.rem(owner, 2)

            @pl.when(owner == 0)
            def _():
                load_x.wait()
                for load in loads:
                    load.wait()

            @pl.when((owner >= 2) & (owner < owners))
            def _():
                grads.store(owner - 2, slot).wait()

            @pl.when(owner < owners)
            def _():
                stage[slot, :, : 3 * cols] = narrow(xin, owner, low[...]).astype(bf16)
                stage[slot, :, 3 * cols :] = (
                    narrow(pin.at[0], owner, attn[0][...])
                    + narrow(pin.at[1], owner, attn[1][...])
                ).astype(bf16)
                grads.store(owner, slot).start()

        assert owners <= rows // 48
        line.stream(job)
        drain()
    else:
        load_x.wait()

        def one(owner, carry):
            slot = lax.rem(owner, 2)
            load_before(owner, slot).wait()

            @pl.when(owner < owners - 1)
            def _():
                load_before(owner + 1, 1 - slot).start()

            @pl.when(owner >= 2)
            def _():
                grads.store(owner - 2, slot).wait()

            value = narrow(xin, owner, low[...]) + had[slot].astype(f32)
            stage[slot] = value.astype(bf16)
            grads.store(owner, slot).start()
            return carry

        lax.fori_loop(0, owners, one, 0)
        heads = cols // HD
        parts = grads.wide // LANES
        gains[...] = jnp.zeros_like(gains)
        first = others[0][...]
        for k in range(2):
            both = gain_grad[8 * k : 8 * k + 8, :] + first[8 * k : 8 * k + 8, :]
            total = jnp.sum(both, axis=0, keepdims=True)
            for owner in range(owners):
                for h in range(heads):
                    gains[owner, k * heads + h, :] = total[0, h * HD : (h + 1) * HD]
        for k, items in enumerate((others[1:3], others[3:])):
            total = sum(jnp.sum(item[...], axis=0, keepdims=True) for item in items)
            for owner in range(owners):
                for j in range(parts):
                    at = (owner * parts + j) * LANES
                    gains[owner, 2 * heads + k * parts + j, :] = total[0, at : at + LANES]
        low_gains, stores = scratch[12], []
        low_gains[...] = gains[...].astype(bf16)
        for owner in range(owners):
            at = pl.ds(owner * grads.wide, low_gains.shape[1])
            to = g_attn.at[at, pl.ds(4 * cols, LANES)]
            stores.append(pltpu.make_async_copy(low_gains.at[owner], to, n_sem.at[owner]))
        for store in stores:
            store.start()
        for store in stores:
            store.wait()
        drain()


def last_sum(
    dq, own, mine, got, units, squares, qg, kg, x, extra, before, w, owners, collective_id
):
    stream = before is None
    n = lax.axis_size("tensor")
    rows, cols = dq.shape
    width = w.shape[0]
    lines = line_count(rows)
    vmem = pl.BlockSpec(memory_space=pltpu.VMEM)
    hbm = pl.BlockSpec(memory_space=pl.ANY)
    dma = pltpu.SemaphoreType.DMA
    wide = width // owners
    weights = pl.BlockSpec((width, 3 * cols), lambda i: (0, 0))

    def kernel(*refs):
        sources = lax.axis_index("seq") < lax.axis_size("seq") // 2
        args = [n, rows, cols, sources, stream, *refs[:9]]
        if stream:
            args += [refs[9:11], refs[11:13], None, None, *refs[13:]]
        else:
            args += [None, None, refs[9], refs[10:14], *refs[14:]]
        last_kernel(*args)

    if stream:
        extra_specs = [hbm, hbm, vmem, vmem]
    else:
        extra, extra_specs = [before, *extra], [hbm] + [vmem] * 4
    shapes = [
        jax.ShapeDtypeStruct((rows, 3 * cols), bf16),
        jax.ShapeDtypeStruct((rows, width), bf16),
        jax.ShapeDtypeStruct((16, cols), f32),
        jax.ShapeDtypeStruct((width, 4 * cols + LANES), bf16),
    ]
    scratch = exchange_scratch(n, lines) + [
        pltpu.VMEM((rows, width), bf16),
        dma(()),
        pltpu.VMEM((2, wide, (4 if stream else 3) * cols), bf16),
        dma((2,)),
    ]
    if stream:
        line = line_scratch(rows, width, rows // 48)
        scratch += line[:3] + [pltpu.VMEM((2, rows, width), bf16), dma((2,))] + line[3:]
    else:
        scratch += [
            pltpu.VMEM((2, wide, 3 * cols), bf16),
            dma((2,)),
            pltpu.VMEM((owners, 16, LANES), f32),
            dma((owners,)),
            pltpu.VMEM((owners, 16, LANES), bf16),
        ]
    return pl.pallas_call(
        kernel,
        grid=(1,),
        in_specs=[vmem] * 8 + [hbm] + extra_specs + [weights],
        out_specs=[vmem, hbm if stream else vmem, vmem, hbm],
        out_shape=shapes,
        scratch_shapes=scratch,
        input_output_aliases={} if stream else {9: 3},
        compiler_params=pltpu.CompilerParams(
            collective_id=collective_id, has_side_effects=True, vmem_limit_bytes=60 << 20
        ),
        cost_estimate=cost(100 if stream else 25),
        name="last_sum" if stream else "last_part",
    )(dq, own, mine, got, units, squares, qg, kg, x, *extra, w)


LINE_ROWS = 48
ROW_STEP = 32
LAG = 3
TILE = 256
NAMES = (
    "part", "x", "cot", "w", "ga", "gm", "first", "proj", "hidden", "inner", "layer", "low",
    "gu", "back", "pre", "grads", "gm_grad", "s", "land", "swap", "res", "acc", "h", "xin", "cin",
    "wgt", "wut", "wdt", "gt", "ut", "it", "jt", "stage", "load_sem", "in_send", "in_recv", "swap_recv",
    "out_send", "out_recv", "store_sem", "w_sem", "x_sem", "c_sem", "h_sem", "y_sem", "t_sem",
    "r_sem", "g_sem",
)


class Mlp:
    def __init__(self, n, micros, rows, *refs):
        for name, ref in zip(NAMES, refs):
            setattr(self, name, ref)
        self.micros, self.rows = micros, rows
        self.chunks = rows // LINE_ROWS
        self.hidden_units = self.w.shape[1] // 3
        self.tiles = self.hidden_units // TILE
        i = lax.axis_index("tensor")
        half = n // 2
        left = i < half
        self.inward = jnp.where(left, i + 1, i - 1)
        self.outward = jnp.where(left, i - 1, i + 1)
        self.relay = (i > 0) & (i < n - 1)
        self.mid = (i == half - 1) | (i == half)

    def at(self, m, c):
        start = pl.multiple_of((m * self.chunks + c) * LINE_ROWS, LINE_ROWS)
        return pl.ds(start, LINE_ROWS)

    def micro(self, m):
        return pl.ds(pl.multiple_of(m * self.rows, self.rows), self.rows)

    def move_in(self, m, c):
        return pltpu.make_async_remote_copy(
            src_ref=self.s.at[self.at(m, c)],
            dst_ref=self.land.at[self.at(m, c)],
            send_sem=self.in_send.at[m, c],
            recv_sem=self.in_recv.at[m, c],
            device_id={"tensor": self.inward},
            device_id_type=MESH,
        )

    def move_swap(self, m, c):
        return pltpu.make_async_remote_copy(
            src_ref=self.s.at[self.at(m, c)],
            dst_ref=self.swap.at[self.at(m, c)],
            send_sem=self.in_send.at[m, c],
            recv_sem=self.swap_recv.at[m, c],
            device_id={"tensor": self.inward},
            device_id_type=MESH,
        )

    def move_out(self, m, c):
        return pltpu.make_async_remote_copy(
            src_ref=self.res.at[self.at(m, c)],
            dst_ref=self.res.at[self.at(m, c)],
            send_sem=self.out_send.at[m, c],
            recv_sem=self.out_recv.at[m, c],
            device_id={"tensor": self.outward},
            device_id_type=MESH,
        )

    def send_in(self, m, c):
        @pl.when(self.mid)
        def _():
            self.move_swap(m, c).start()

        @pl.when(~self.mid)
        def _():
            self.move_in(m, c).start()

    def each_chunk(self, body):
        def one(c, carry):
            body(c)
            return carry

        lax.fori_loop(0, self.chunks, one, 0)

    def launch(self, m):
        @pl.when(~self.relay)
        def _():
            self.each_chunk(lambda c: self.send_in(m, c))

    def settle(self, m):
        def one(c):
            self.move_in(m, c).wait_send()

            @pl.when(self.relay)
            def _():
                self.move_out(m, c).wait_send()

        self.each_chunk(one)

    def begin(self):
        others = pl.ds(self.rows, (self.micros - 1) * self.rows)
        load = pltpu.make_async_copy(self.part, self.s.at[others], self.load_sem)
        load.start()
        rest = self.micro(0)
        done = pltpu.make_async_copy(self.first, self.res.at[rest], self.y_sem)
        done.start()
        self.load_x(0, self.x).start()
        for copy in self.load_w(0, 0):
            copy.start()
        barrier = pltpu.get_barrier_semaphore()
        pl.semaphore_signal(
            barrier, inc=1, device_id={"tensor": self.inward}, device_id_type=MESH
        )

        @pl.when(self.relay)
        def _():
            pl.semaphore_signal(
                barrier, inc=1, device_id={"tensor": self.outward}, device_id_type=MESH
            )

        pl.semaphore_wait(barrier, jnp.where(self.relay, 2, 1))
        load.wait()
        done.wait()
        for m in range(1, self.micros):
            self.launch(m)
        self.gm_grad[...] = jnp.zeros_like(self.gm_grad)

    def reduce(self, m, c):
        @pl.when(self.relay)
        def _():
            self.move_in(m, c).wait_recv()
            a = self.at(m, c)
            self.s[a, :] = (self.s[a, :].astype(f32) + self.land[a, :].astype(f32)).astype(bf16)
            self.send_in(m, c)

    def store(self, m, c, to):
        a = self.at(m, c)
        return pltpu.make_async_copy(self.res.at[a], to.at[a], self.store_sem.at[m, c])

    def spread(self, which, m, c):
        a = self.at(m, c)

        @pl.when(self.mid)
        def _():
            self.move_swap(m, c).wait_recv()
            self.res[a, :] = (self.s[a, :].astype(f32) + self.swap[a, :].astype(f32)).astype(bf16)

        @pl.when(~self.mid)
        def _():
            self.move_out(m, c).wait_recv()

        @pl.when(self.relay)
        def _():
            self.move_out(m, c).start()

        @pl.when(which == 0)
        def _():
            self.store(m, c, self.proj).start()

        @pl.when(which == 2)
        def _():
            self.store(m, c, self.back).start()

    def load_x(self, m, source):
        return pltpu.make_async_copy(source.at[self.micro(m)], self.xin, self.x_sem)

    def load_c(self, m):
        return pltpu.make_async_copy(self.cot.at[self.micro(m)], self.cin, self.c_sem)

    def store_h(self, m, to):
        return pltpu.make_async_copy(self.h, to.at[self.micro(m)], self.h_sem)

    def store_layer(self, m):
        return pltpu.make_async_copy(self.xin, self.layer.at[self.micro(m)], self.y_sem)

    def cols(self, t, which=0):
        return pl.ds(pl.multiple_of(which * self.hidden_units + t * TILE, TILE), TILE)

    def load_w(self, t, slot):
        return [
            pltpu.make_async_copy(
                self.w.at[:, self.cols(t, which)], to.at[slot], self.w_sem.at[which, slot]
            )
            for which, to in enumerate((self.wgt, self.wut, self.wdt))
        ]

    def load_pre(self, m, t, slot):
        return [
            pltpu.make_async_copy(
                self.pre.at[self.micro(m), self.cols(t, which)],
                to.at[slot],
                self.r_sem.at[which, slot],
            )
            for which, to in enumerate((self.gt, self.ut))
        ]

    def store_tile(self, which, source, to, m, at, slot):
        return pltpu.make_async_copy(
            source.at[slot], to.at[self.micro(m), at], self.t_sem.at[which, slot]
        )

    def store_pre(self, m, t, slot):
        return (
            self.store_tile(0, self.gt, self.pre, m, self.cols(t, 0), slot),
            self.store_tile(1, self.ut, self.pre, m, self.cols(t, 1), slot),
            self.store_tile(2, self.it, self.inner, m, self.cols(t), slot),
        )

    def store_low(self, m, t, slot):
        return (
            self.store_tile(2, self.it, self.gu, m, self.cols(t, 0), slot),
            self.store_tile(3, self.jt, self.gu, m, self.cols(t, 1), slot),
        )

    def row_groups(self, body):
        step = ROW_STEP

        def one(r, carry):
            body(pl.ds(pl.multiple_of(r * step, step), step), r * step)
            return carry

        lax.fori_loop(0, self.rows // step, one, 0)

    def forward_start(self, m):
        @pl.when(m > 0)
        def _():
            self.each_chunk(lambda c: self.store(m, c, self.proj).wait())

        self.load_x(m, self.x).wait()
        base = m * self.rows
        gain = self.ga[...]

        def one(at, r):
            total = self.res[pl.ds(pl.multiple_of(base + r, ROW_STEP), ROW_STEP), :].astype(f32)
            inv = lax.rsqrt(jnp.mean(total * total, axis=1, keepdims=True) + norm_eps)
            self.h[at, :] = (self.xin[at, :].astype(f32) + total * inv * gain).astype(bf16)

        self.row_groups(one)
        self.store_h(m, self.hidden).start()

    def backward_start(self, m):
        for copy in self.load_pre(m, 0, 0):
            copy.start()
        self.load_x(m, self.hidden).wait()
        self.load_c(m).wait()
        base = m * self.rows
        gain = self.gm[...]

        def one(at, r):
            total = self.res[pl.ds(pl.multiple_of(base + r, ROW_STEP), ROW_STEP), :].astype(f32)
            inv = lax.rsqrt(jnp.mean(total * total, axis=1, keepdims=True) + norm_eps)
            unit = total * inv
            c = self.cin[at, :].astype(f32)
            self.xin[at, :] = (self.xin[at, :].astype(f32) + unit * gain).astype(bf16)
            hit = c * unit
            self.gm_grad[...] += fold(hit)
            dy = c * gain
            inner = jnp.mean(hit * gain, axis=1, keepdims=True)
            self.h[at, :] = (inv * (dy - unit * inner)).astype(bf16)

        self.row_groups(one)
        self.store_layer(m).start()
        self.store_h(m, self.low).start()

    def tile_weights(self, t, slot, last):
        for copy in self.load_w(t, slot):
            copy.wait()

        @pl.when(jnp.logical_not(last))
        def _():
            for copy in self.load_w(lax.rem(t + 1, self.tiles), 1 - slot):
                copy.start()

    def add(self, t, at, value):
        @pl.when(t == 0)
        def _():
            self.acc[:, at] = value

        @pl.when(t > 0)
        def _():
            self.acc[:, at] += value

    def forward_tile(self, m, t):
        slot = lax.rem(t, 2)
        self.tile_weights(t, slot, False)

        @pl.when(t >= 2)
        def _():
            for copy in self.store_pre(m, t - 2, slot):
                copy.wait()

        gate = matmul(self.h[...], self.wgt[slot])
        up = matmul(self.h[...], self.wut[slot])
        self.gt[slot] = gate.astype(bf16)
        self.ut[slot] = up.astype(bf16)
        self.it[slot] = (gate * jax.nn.sigmoid(gate) * up).astype(bf16)
        for copy in self.store_pre(m, t, slot):
            copy.start()
        wide = self.acc.shape[1]
        step = math.gcd(wide, 512)
        for k in range(0, wide, step):
            self.add(t, slice(k, k + step), right_t(self.it[slot], self.wdt[slot, k : k + step, :]))

        @pl.when(t == self.tiles - 1)
        def _():
            for back in range(min(2, self.tiles)):
                at = self.tiles - 1 - back
                for copy in self.store_pre(m, at, at % 2):
                    copy.wait()
            self.store_h(m, self.hidden).wait()
            self.finish(m, m > 0)

    def backward_tile(self, m, t, last):
        slot = lax.rem(t, 2)
        self.tile_weights(t, slot, last & (t == self.tiles - 1))
        for copy in self.load_pre(m, t, slot):
            copy.wait()

        @pl.when(t < self.tiles - 1)
        def _():
            for copy in self.load_pre(m, t + 1, 1 - slot):
                copy.start()

        @pl.when(t >= 2)
        def _():
            for copy in self.store_low(m, t - 2, slot):
                copy.wait()

        grad = matmul(self.h[...], self.wdt[slot])
        gate = self.gt[slot].astype(f32)
        sig = jax.nn.sigmoid(gate)
        act = grad * sig
        self.jt[slot] = (act * gate).astype(bf16)
        self.it[slot] = (
            act * self.ut[slot].astype(f32) * (1.0 + gate * (1.0 - sig))
        ).astype(bf16)
        for copy in self.store_low(m, t, slot):
            copy.start()
        wide = self.acc.shape[1]
        step = math.gcd(wide, 512)
        for k in range(0, wide, step):
            self.add(
                t,
                slice(k, k + step),
                right_t(self.it[slot], self.wgt[slot, k : k + step, :])
                + right_t(self.jt[slot], self.wut[slot, k : k + step, :]),
            )

        @pl.when(t == self.tiles - 1)
        def _():
            for back in range(min(2, self.tiles)):
                at = self.tiles - 1 - back
                for copy in self.store_low(m, at, at % 2):
                    copy.wait()
            self.store_h(m, self.low).wait()
            self.store_layer(m).wait()
            self.finish(m, True)

    def load_bigs(self, source):
        return (
            pltpu.make_async_copy(source.at[self.micro(0)], self.xin, self.x_sem),
            pltpu.make_async_copy(source.at[self.micro(1)], self.cin, self.c_sem),
        )

    def load_units(self, source, w, slot):
        return [
            pltpu.make_async_copy(
                source.at[self.micro(m), self.cols(w)], to.at[slot], self.r_sem.at[m, slot]
            )
            for m, to in enumerate((self.gt, self.ut))
        ]

    def start_units(self, w, slot):
        split = 2 * self.tiles

        @pl.when(w < split)
        def _():
            for copy in self.load_units(self.gu, w, slot):
                copy.start()

        @pl.when((w >= split) & (w < 3 * self.tiles))
        def _():
            for copy in self.load_units(self.inner, w - split, slot):
                copy.start()

    def store_grads(self, w, slot):
        return pltpu.make_async_copy(
            self.stage.at[slot], self.grads.at[:, self.cols(w), :], self.g_sem.at[slot]
        )

    def grad_tile(self, w):
        slot = lax.rem(w, 2)
        split = 2 * self.tiles

        @pl.when((w == 0) | (w == split))
        def _():
            for copy in self.load_bigs(self.hidden):
                copy.wait()

        for copy in self.load_units(self.gu, 0, slot):
            copy.wait()
        self.start_units(w + 1, 1 - slot)

        @pl.when(w >= 2)
        def _():
            self.store_grads(w - 2, slot).wait()

        value = left_t(self.gt[slot], self.xin[...]) + left_t(self.ut[slot], self.cin[...])
        owners, _, wide = self.stage.shape[1:]
        for owner in range(owners):
            self.stage[slot, owner] = value[:, owner * wide : (owner + 1) * wide].astype(bf16)
        self.store_grads(w, slot).start()

        @pl.when(w == split - 1)
        def _():
            for copy in self.load_bigs(self.low):
                copy.start()

        @pl.when(w == 3 * self.tiles - 1)
        def _():
            self.store_grads(w - 1, 1 - slot).wait()
            self.store_grads(w, slot).wait()

    def finish(self, m, sent):
        @pl.when(sent)
        def _():
            self.settle(m)

        base = m * self.rows

        def one(at, r):
            self.s[pl.ds(pl.multiple_of(base + r, ROW_STEP), ROW_STEP), :] = self.acc[at, :].astype(bf16)

        self.row_groups(one)
        self.launch(m)

    def job(self, index, step):
        micros = self.micros
        m = lax.rem(index, micros)
        forward = index < micros
        last = index == 2 * micros - 1

        @pl.when(forward & (step == 0))
        def _():
            self.forward_start(m)

        @pl.when(jnp.logical_not(forward) & (step == 0))
        def _():
            self.backward_start(m)

        tiled = (step >= 1) & (step <= self.tiles)

        @pl.when(forward & tiled)
        def _():
            self.forward_tile(m, step - 1)

        @pl.when(jnp.logical_not(forward) & tiled)
        def _():
            self.backward_tile(m, step - 1, last)

        done = step == self.tiles

        @pl.when(done & (index < micros - 1))
        def _():
            self.load_x(index + 1, self.x).start()

        @pl.when(done & (index >= micros - 1) & jnp.logical_not(last))
        def _():
            self.load_x(index + 1 - micros, self.hidden).start()
            self.load_c(index + 1 - micros).start()

        @pl.when(done & last)
        def _():
            for copy in self.load_bigs(self.hidden):
                copy.start()
            self.start_units(0, 0)

    def run(self):
        n, micros = self.chunks, self.micros
        total = 3 * micros * n
        self.begin()

        def clock(k, carry):
            @pl.when(k < total)
            def _():
                self.reduce(lax.rem(k // n, micros), lax.rem(k, n))

            back = k - LAG

            @pl.when((back >= n) & (back < total))
            def _():
                sum_index = back // n
                self.spread(sum_index // micros, lax.rem(sum_index, micros), lax.rem(back, n))

            turn = back - n

            @pl.when((turn >= 0) & (turn < 2 * micros * n))
            def _():
                self.job(turn // n, lax.rem(turn, n))

            turn = turn - 2 * micros * n + n - self.tiles - 1

            @pl.when((turn >= 0) & (turn < 3 * self.tiles))
            def _():
                self.grad_tile(turn)

            return carry

        grads_at = 2 * micros * n + LAG + self.tiles + 1
        lax.fori_loop(n, max(total + LAG, grads_at + 3 * self.tiles), clock, 0)
        for m in range(micros):
            self.settle(m)
            self.each_chunk(lambda c: self.store(m, c, self.back).wait())


def mlp_kernel(n, micros, rows, *refs):
    Mlp(n, micros, rows, *refs).run()


def feed_forward(part, x, cot, w, ga, gm, first, micros, owners):
    assert micros == 2
    both, width = x.shape
    hidden = w.shape[1] // 3
    rows = both // micros
    chunks = rows // LINE_ROWS
    dma = pltpu.SemaphoreType.DMA
    hbm = pl.BlockSpec(memory_space=pl.ANY)
    vmem = pl.BlockSpec(memory_space=pltpu.VMEM)
    wide = jax.ShapeDtypeStruct((both, width), bf16)
    unit = jax.ShapeDtypeStruct((both, hidden), bf16)
    two = jax.ShapeDtypeStruct((both, 2 * hidden), bf16)
    return pl.pallas_call(
        functools.partial(mlp_kernel, lax.axis_size("tensor"), micros, rows),
        in_specs=[hbm] * 4 + [vmem] * 2 + [hbm],
        out_specs=[hbm] * 9 + [vmem],
        out_shape=[wide, wide, unit, wide, wide, two, wide, two]
        + [jax.ShapeDtypeStruct((owners, 3 * hidden, width // owners), bf16)]
        + [jax.ShapeDtypeStruct((8, width), f32)],
        scratch_shapes=[
            pltpu.VMEM((both, width), bf16),
            pltpu.VMEM((both, width), bf16),
            pltpu.VMEM((both, width), bf16),
            pltpu.VMEM((both, width), bf16),
            pltpu.VMEM((rows, width), f32),
            pltpu.VMEM((rows, width), bf16),
            pltpu.VMEM((rows, width), bf16),
            pltpu.VMEM((rows, width), bf16),
            pltpu.VMEM((2, width, TILE), bf16),
            pltpu.VMEM((2, width, TILE), bf16),
            pltpu.VMEM((2, width, TILE), bf16),
            pltpu.VMEM((2, rows, TILE), bf16),
            pltpu.VMEM((2, rows, TILE), bf16),
            pltpu.VMEM((2, rows, TILE), bf16),
            pltpu.VMEM((2, rows, TILE), bf16),
            pltpu.VMEM((2, owners, TILE, width // owners), bf16),
            dma(()),
            dma((micros, chunks)),
            dma((micros, chunks)),
            dma((micros, chunks)),
            dma((micros, chunks)),
            dma((micros, chunks)),
            dma((micros, chunks)),
            dma((3, 2)),
            dma(()),
            dma(()),
            dma(()),
            dma(()),
            dma((4, 2)),
            dma((2, 2)),
            dma((2,)),
        ],
        compiler_params=pltpu.CompilerParams(
            collective_id=1, has_side_effects=True, vmem_limit_bytes=60 << 20
        ),
        cost_estimate=cost(both // 4),
        name="feed_forward",
    )(part, x, cot, w, ga, gm, first)


def attn_scores(meta, i, trunk_rows, q, kt, kp, ko):
    scale = HD ** (-0.5)
    block = meta[i, 0]
    n_par = meta[i, 2]
    n_own = meta[i, 3]
    n_trunk = meta[i, 4]
    st = right_t(q, kt) * scale
    sp = right_t(q, kp) * scale
    so = right_t(q, ko) * scale
    row = lax.broadcasted_iota(jnp.int32, (BLOCK, trunk_rows), 0) + block * BLOCK
    col = lax.broadcasted_iota(jnp.int32, (BLOCK, trunk_rows), 1)
    st = jnp.where((col < n_trunk) & (col <= row), st, masked_score)
    row = lax.broadcasted_iota(jnp.int32, (BLOCK, BLOCK), 0)
    col = lax.broadcasted_iota(jnp.int32, (BLOCK, BLOCK), 1)
    sp = jnp.where(col < n_par, sp, masked_score)
    so = jnp.where((col < n_own) & (col <= row), so, masked_score)
    return st, sp, so


def attn_fwd_kernel(trunk_rows, meta, q, trunk, par, own, out, lse):
    i = pl.program_id(1)
    st, sp, so = attn_scores(meta, i, trunk_rows, q[...], trunk[0], par[0], own[0])
    top = jnp.maximum(
        jnp.max(st, axis=1, keepdims=True),
        jnp.maximum(jnp.max(sp, axis=1, keepdims=True), jnp.max(so, axis=1, keepdims=True)),
    )
    et, ep, eo = jnp.exp(st - top), jnp.exp(sp - top), jnp.exp(so - top)
    total = (
        jnp.sum(et, axis=1, keepdims=True)
        + jnp.sum(ep, axis=1, keepdims=True)
        + jnp.sum(eo, axis=1, keepdims=True)
    )
    acc = matmul(et.astype(bf16), trunk[1])
    acc += matmul(ep.astype(bf16), par[1])
    acc += matmul(eo.astype(bf16), own[1])
    out[...] = (acc / total).astype(bf16)
    lse[...] = jnp.broadcast_to(top + jnp.log(total), (BLOCK, HD))


def attn_bwd_kernel(
    trunk_rows, n_q, meta, q, do, lse, trunk, par, own, dq, d_own, d_src, acc,
):
    i = pl.program_id(1)

    @pl.when(i == 0)
    def _():
        acc[...] = jnp.zeros_like(acc)

    scale = HD ** (-0.5)
    qv, dov = q[...], do[...]
    scores = attn_scores(meta, i, trunk_rows, qv, trunk[0], par[0], own[0])
    top = lse[:, 0:1]
    probs = [jnp.exp(s - top) for s in scores]
    grads = [right_t(dov, v[1]) for v in (trunk, par, own)]
    inner = sum(jnp.sum(p * g, axis=1, keepdims=True) for p, g in zip(probs, grads))
    low = [(p * (g - inner)).astype(bf16) for p, g in zip(probs, grads)]
    probs = [p.astype(bf16) for p in probs]
    dq[...] = scale * (
        matmul(low[0], trunk[0]) + matmul(low[1], par[0]) + matmul(low[2], own[0])
    )
    d_own[0] = scale * left_t(low[2], qv)
    d_own[1] = left_t(probs[2], dov)
    acc[0, :trunk_rows] += left_t(low[0], qv)
    acc[1, :trunk_rows] += left_t(probs[0], dov)
    at = pl.ds(pl.multiple_of(trunk_rows + meta[i, 1] * BLOCK, BLOCK), BLOCK)
    acc[0, at] += left_t(low[1], qv)
    acc[1, at] += left_t(probs[1], dov)

    @pl.when(i == n_q - 1)
    def _():
        d_src[0] = (scale * acc[0]).astype(bf16)
        d_src[1] = acc[1].astype(bf16)


def kv_specs(trunk_rows):
    skip = trunk_rows // BLOCK
    trunk = pl.BlockSpec((2, trunk_rows, HD), lambda h, i, meta: (0, 0, h))
    par = pl.BlockSpec((2, BLOCK, HD), lambda h, i, meta: (0, skip + meta[i, 1], h))
    own = pl.BlockSpec((2, BLOCK, HD), lambda h, i, meta: (0, i, h))
    return [trunk, par, own]


def attend_forward(meta, q, sources, own_kv, trunk_rows):
    rows, width = q.shape
    own = pl.BlockSpec((BLOCK, HD), lambda h, i, meta: (i, h))
    return pl.pallas_call(
        functools.partial(attn_fwd_kernel, trunk_rows),
        grid_spec=pltpu.PrefetchScalarGridSpec(
            num_scalar_prefetch=1,
            grid=(width // HD, rows // BLOCK),
            in_specs=[own] + kv_specs(trunk_rows),
            out_specs=[own, own],
        ),
        out_shape=[
            jax.ShapeDtypeStruct((rows, width), bf16),
            jax.ShapeDtypeStruct((rows, width), f32),
        ],
        compiler_params=pltpu.CompilerParams(vmem_limit_bytes=32 << 20),
        cost_estimate=cost(12),
        name="attend_forward",
    )(meta, q, sources, sources, own_kv)


def attend_backward(meta, q, do, lse, sources, own_kv, trunk_rows):
    rows, width = q.shape
    own = pl.BlockSpec((BLOCK, HD), lambda h, i, meta: (i, h))
    own_two = pl.BlockSpec((2, BLOCK, HD), lambda h, i, meta: (0, i, h))
    all_rows = sources.shape[1]
    n_q = rows // BLOCK
    return pl.pallas_call(
        functools.partial(attn_bwd_kernel, trunk_rows, n_q),
        grid_spec=pltpu.PrefetchScalarGridSpec(
            num_scalar_prefetch=1,
            grid=(width // HD, n_q),
            in_specs=[own, own, own] + kv_specs(trunk_rows),
            out_specs=[
                own,
                own_two,
                pl.BlockSpec((2, all_rows, HD), lambda h, i, meta: (0, 0, h)),
            ],
            scratch_shapes=[pltpu.VMEM((2, all_rows, HD), f32)],
        ),
        out_shape=[
            jax.ShapeDtypeStruct((rows, width), f32),
            jax.ShapeDtypeStruct((2, rows, width), f32),
            jax.ShapeDtypeStruct(sources.shape, bf16),
        ],
        compiler_params=pltpu.CompilerParams(vmem_limit_bytes=40 << 20),
        cost_estimate=cost(22),
        name="attend_backward",
    )(meta, q, do, lse, sources, sources, own_kv)


def group_perm(n, k):
    half = n // 2
    return [(i, i // half * half + (i % half + k) % half) for i in range(n)]


def fetch_sources(block, hold):
    n = lax.axis_size("seq")
    half = n // 2
    place = lax.axis_index("seq")
    spot = lax.rem(place, half)
    got = lax.ppermute(block, "seq", [(i, i + half) for i in range(half)])
    mine = jnp.where(place < half, block, got if hold is None else after(got, hold))
    parts = [mine] + [lax.ppermute(mine, "seq", group_perm(n, k)) for k in range(1, half)]
    out = []
    for source in range(half):
        pick = parts[0]
        for k in range(1, half):
            pick = jnp.where(lax.rem(spot - k + half, half) == source, parts[k], pick)
        out.append(pick)
    return jnp.concatenate(out, axis=1)


def sum_over_group(grads):
    n = lax.axis_size("seq")
    half = n // 2
    spot = lax.rem(lax.axis_index("seq"), half)
    rows = grads.shape[1] // half
    pieces = [grads[:, s * rows : (s + 1) * rows] for s in range(half)]

    def piece(index):
        pick = pieces[0]
        for s in range(1, half):
            pick = jnp.where(index == s, pieces[s], pick)
        return pick

    total = piece(spot).astype(f32)
    for k in range(1, half):
        sent = piece(lax.rem(spot + k, half))
        total += lax.ppermute(sent, "seq", group_perm(n, k)).astype(f32)
    return total.astype(bf16)


def return_to_sources(total):
    n = lax.axis_size("seq")
    half = n // 2
    return lax.ppermute(total, "seq", [(i + half, i) for i in range(half)])


def gather_rows(item):
    return lax.all_gather(item, ("dp", "seq"), axis=0, tiled=True)


def scatter_low(item):
    return lax.psum_scatter(item, ("dp", "seq"), scatter_dimension=0, tiled=True)


def scatter_rows(item):
    return scatter_low(item).astype(f32)


def block_meta(parents, lengths, rows, n_blocks):
    seg_count = parents.shape[0]
    branches = (seg_count - 1) // 3
    trunk_blocks = n_blocks - 3 * branches
    blocks = lax.axis_index("seq") * (rows // BLOCK) + jnp.arange(rows // BLOCK, dtype=jnp.int32)
    seg = jnp.maximum(blocks - trunk_blocks + 1, 0)
    hit = seg[:, None] == jnp.arange(seg_count, dtype=jnp.int32)[None, :]
    parent = jnp.sum(jnp.where(hit, parents[None, :], 0), axis=1)
    own_len = jnp.sum(jnp.where(hit, lengths[None, :], 0), axis=1)
    hit = parent[:, None] == jnp.arange(seg_count, dtype=jnp.int32)[None, :]
    par_len = jnp.sum(jnp.where(hit, lengths[None, :], 0), axis=1)
    return jnp.stack(
        [
            blocks,
            jnp.maximum(parent - 1, 0),
            jnp.where(parent > 0, par_len, 0),
            jnp.where(blocks >= trunk_blocks, own_len, 0),
            jnp.broadcast_to(lengths[0], blocks.shape),
        ],
        axis=1,
    ).astype(jnp.int32)


def per_device(
    tokens, cotangent, w_query, w_key, w_value, w_out, w_gate, w_up, w_down,
    query_gain, key_gain, attn_gain, mlp_gain, parent_of, seg_length,
):
    micros, _, rows, width = tokens.shape
    n_blocks = rows // BLOCK * lax.axis_size("seq")
    heads = w_query.shape[1] // HD
    full_width = heads * HD * lax.axis_size("tensor")
    branches = (parent_of.shape[2] - 1) // 3
    trunk_rows = (n_blocks - 3 * branches) * BLOCK

    cols = w_query.shape[1]
    owners = lax.axis_size("dp") * lax.axis_size("seq")
    w_attn = gather_rows(jnp.concatenate([w_query, w_key, w_value, w_out.T], axis=1))
    gains = [query_gain.reshape(-1), key_gain.reshape(-1), attn_gain, mlp_gain]
    gains = lax.all_gather(jnp.concatenate(gains), ("dp", "seq"), axis=0, tiled=False)
    w_own = jnp.concatenate([w_gate, w_up, w_down.T], axis=1)
    gains = after(gains, w_own)
    own = query_gain.size

    def head_gain(block):
        block = block.reshape(owners, heads, HD // owners)
        return jnp.swapaxes(block, 0, 1).reshape(-1).astype(f32)

    q_gain = head_gain(gains[:, :own])
    k_gain = head_gain(gains[:, own : 2 * own])
    a_gain = gains[:, 2 * own : 2 * own + attn_gain.size].reshape(-1).astype(f32)
    m_gain = gains[:, 2 * own + attn_gain.size :].reshape(-1).astype(f32)
    wo_t = w_attn[:, 3 * cols :]
    q_gain, k_gain, a_gain = q_gain[None], k_gain[None], a_gain[None]

    x = tokens.reshape(micros * rows, width)
    cot = cotangent.reshape(micros * rows, width)
    q_lows, kv_lows, units, squares = zip(
        *(qkv(x, w_attn, q_gain, k_gain, m, rows, 6 + m) for m in range(micros))
    )
    sources, metas, attn_lows, lses, parts, first = [], [], [], [], [], None
    for m in range(micros):
        sources.append(fetch_sources(kv_lows[m], q_lows[1] if m == 0 else first))
        metas.append(block_meta(parent_of[m, 0], seg_length[m, 0], rows, n_blocks))
        attn_low, lse = attend_forward(metas[m], q_lows[m], sources[m], kv_lows[m], trunk_rows)
        attn_lows.append(attn_low)
        lses.append(lse)
        parts.append(right_t(attn_low, wo_t).astype(bf16))
        if m == 0:
            first = line_sum(parts[0], 0)
            w_mlp = gather_rows(after(w_own, sources[0]))
    proj, _, _, layer, _, _, back, _, mlp_grads, gm_grad = feed_forward(
        parts[1], x, cot, w_mlp, a_gain, m_gain[None], first,
        micros, owners,
    )
    hidden = w_gate.shape[1]
    g_attn, qk_grad, ga_grads, layer_out = None, None, [], None
    proj_lows, dqs, d_owns, sums = [], [], [], []
    for m in range(micros):
        proj_low, attn_grad, grad, layer_out = proj_backward(
            cot, back, first if m == 0 else proj, after(a_gain, sums[0]) if m else a_gain, w_attn,
            layer, layer_out, cols, m, rows, m
        )
        ga_grads.append(grad)
        dq, d_own, d_src = attend_backward(
            metas[m], q_lows[m], attn_grad, lses[m], sources[m], kv_lows[m], trunk_rows
        )
        sums.append(sum_over_group(d_src))
        proj_lows.append(proj_low)
        dqs.append(dq)
        d_owns.append(d_own)

    lasts = []
    for m in range(micros):
        got = return_to_sources(sums[m])
        if m > 0:
            got = after(got, lasts[-1])
        else:
            got = after(got, dqs[-1])
            mlp_grads = after(mlp_grads.reshape(-1, mlp_grads.shape[2]), got)
            mlp_grads = scatter_low(mlp_grads)
        extra = [*proj_lows, *attn_lows] if m == 0 else [qk_grad, *ga_grads, gm_grad]
        _, last, qk_grad, g_attn = last_sum(
            dqs[m], d_owns[m], sums[m], got, units[m], squares[m], q_gain, k_gain,
            x.reshape(micros, rows, width), extra, g_attn, w_attn, owners, 5 if m else 3,
        )
        lasts.append(line_sum(last, 4) if m else last)
    g_attn = scatter_low(after(g_attn, mlp_grads))
    g_attn = after(g_attn, qk_grad).astype(f32)
    last = jnp.concatenate(lasts, axis=0)

    lines = g_attn[:, 4 * cols :]
    share = HD // owners
    place = lax.axis_index("dp") * lax.axis_size("seq") + lax.axis_index("seq")
    head_lines = lax.dynamic_slice_in_dim(lines[: 2 * heads], place * share, share, 1)
    own_lines = lines[2 * heads : 2 * heads + 2 * attn_gain.size // LANES].reshape(2, -1)
    input_grad = cot.astype(f32) + back.astype(f32) + last.astype(f32)
    return (
        layer_out.reshape(tokens.shape),
        input_grad.reshape(tokens.shape),
        g_attn[:, :cols],
        g_attn[:, cols : 2 * cols],
        g_attn[:, 2 * cols : 3 * cols],
        g_attn[:, 3 * cols : 4 * cols].T,
        mlp_grads[:hidden].astype(f32).T,
        mlp_grads[hidden : 2 * hidden].astype(f32).T,
        mlp_grads[2 * hidden :].astype(f32),
        head_lines[:heads],
        head_lines[heads:],
        own_lines[0],
        own_lines[1],
    )


def solution(mesh):
    rows = P(None, "dp", "seq", None)
    by_row = P(("dp", "seq"), "tensor")
    by_col = P("tensor", ("dp", "seq"))
    gain = P(("dp", "seq"))
    tree = P(None, "dp", None)
    weights = (by_row, by_row, by_row, by_col, by_row, by_row, by_col, by_col, by_col, gain, gain)
    return jax.shard_map(
        per_device,
        mesh=mesh,
        in_specs=(rows, rows) + weights + (tree, tree),
        out_specs=(rows, rows) + weights,
        check_vma=False,
    )
```

```python
import functools
import math

import jax
import jax.numpy as jnp
from jax import lax
from jax.experimental import pallas as pl
from jax.experimental.pallas import tpu as pltpu
from jax.sharding import PartitionSpec as P

HD = 128
BLOCK = 256

norm_eps = 1e-06
masked_score = -1e30
f32 = jnp.float32
bf16 = jnp.bfloat16


def matmul(left, right):
    return jnp.dot(left, right, preferred_element_type=f32)


def left_t(left, right):
    return lax.dot_general(left, right, (((0,), (0,)), ((), ())), preferred_element_type=f32)


def right_t(left, right):
    return lax.dot_general(left, right, (((1,), (1,)), ((), ())), preferred_element_type=f32)


MESH = pl.DeviceIdType.MESH


def cost(us):
    return pl.CostEstimate(flops=int(us * 1.1e9), bytes_accessed=0, transcendentals=0)


def fold(rows):
    total = rows[0:8]
    for j in range(8, rows.shape[0], 8):
        total += rows[j : j + 8]
    return total


def after(value, *earlier):
    hbm = pl.BlockSpec(memory_space=pl.ANY)
    return pl.pallas_call(
        lambda *refs: None,
        in_specs=[hbm] * (1 + len(earlier)),
        out_specs=hbm,
        out_shape=jax.ShapeDtypeStruct(value.shape, value.dtype),
        input_output_aliases={0: 0},
        name="after",
    )(value, *earlier)


class Line:
    def __init__(self, n, chunks, rows, part, out, s, land, res, sems):
        self.chunks, self.rows = chunks, rows
        self.part, self.out, self.s, self.land, self.res = part, out, s, land, res
        (
            self.load_sem,
            self.in_send,
            self.in_recv,
            self.out_send,
            self.out_recv,
            self.store_sem,
        ) = sems
        i = lax.axis_index("tensor")
        half = n // 2
        left = i < half
        self.inward = jnp.where(left, i + 1, i - 1)
        self.outward = jnp.where(left, i - 1, i + 1)
        self.relay = (i > 0) & (i < n - 1)
        self.mid = (i == half - 1) | (i == half)
        self.slot = jnp.where(self.mid, 1, 0)

    def at(self, c):
        return pl.ds(pl.multiple_of(c * self.rows, self.rows), self.rows)

    def load(self):
        return pltpu.make_async_copy(self.part, self.s, self.load_sem)

    def inward_copy(self, c, slot):
        return pltpu.make_async_remote_copy(
            src_ref=self.s.at[self.at(c)],
            dst_ref=self.land.at[slot, self.at(c)],
            send_sem=self.in_send.at[c],
            recv_sem=self.in_recv.at[slot, c],
            device_id={"tensor": self.inward},
            device_id_type=MESH,
        )

    def outward_copy(self, c):
        return pltpu.make_async_remote_copy(
            src_ref=self.res.at[self.at(c)],
            dst_ref=self.res.at[self.at(c)],
            send_sem=self.out_send.at[c],
            recv_sem=self.out_recv.at[c],
            device_id={"tensor": self.outward},
            device_id_type=MESH,
        )

    def store(self, c):
        return pltpu.make_async_copy(
            self.res.at[self.at(c)], self.out.at[self.at(c)], self.store_sem.at[c]
        )

    def begin(self):
        self.load().start()
        barrier = pltpu.get_barrier_semaphore()
        pl.semaphore_signal(
            barrier, inc=1, device_id={"tensor": self.inward}, device_id_type=MESH
        )

        @pl.when(self.relay)
        def _():
            pl.semaphore_signal(
                barrier, inc=1, device_id={"tensor": self.outward}, device_id_type=MESH
            )

        pl.semaphore_wait(barrier, jnp.where(self.relay, 2, 1))
        self.load().wait()
        self.launch(0, self.chunks)

    def launch(self, first, last):
        @pl.when(~self.relay)
        def _():
            def one(c, carry):
                self.inward_copy(c, self.slot).start()
                return carry

            lax.fori_loop(first, last, one, 0)

    def stream(self, job=None):
        def step(c, carry):
            if job is not None:
                job(c)
            self.reduce(c)

            @pl.when(c > 0)
            def _():
                self.spread(c - 1)

            return carry

        lax.fori_loop(0, self.chunks, step, 0)
        self.spread(self.chunks - 1)
        self.end()

    def reduce(self, c):
        @pl.when(self.relay)
        def _():
            self.inward_copy(c, 0).wait_recv()
            a = self.at(c)
            self.s[a, :] = (self.s[a, :].astype(f32) + self.land[0, a, :].astype(f32)).astype(bf16)
            self.inward_copy(c, self.slot).start()

    def spread(self, c):
        a = self.at(c)

        @pl.when(self.mid)
        def _():
            self.inward_copy(c, 1).wait_recv()
            self.res[a, :] = (
                self.s[a, :].astype(f32) + self.land[1, a, :].astype(f32)
            ).astype(bf16)

        @pl.when(~self.mid)
        def _():
            self.outward_copy(c).wait_recv()

        @pl.when(self.relay)
        def _():
            self.outward_copy(c).start()

        self.store(c).start()

    def end(self):
        def one(c, carry):
            self.inward_copy(c, self.slot).wait_send()

            @pl.when(self.relay)
            def _():
                self.outward_copy(c).wait_send()

            self.store(c).wait()
            return carry

        lax.fori_loop(0, self.chunks, one, 0)


def line_scratch(rows, width, chunks):
    dma = pltpu.SemaphoreType.DMA
    return [
        pltpu.VMEM((rows, width), bf16),
        pltpu.VMEM((2, rows, width), bf16),
        pltpu.VMEM((rows, width), bf16),
        dma(()),
        dma((chunks,)),
        dma((2, chunks)),
        dma((chunks,)),
        dma((chunks,)),
        dma((chunks,)),
    ]


def line_kernel(n, chunks, part, out, s, land, res, *sems):
    line = Line(n, chunks, part.shape[0] // chunks, part, out, s, land, res, sems)
    line.begin()
    line.stream()


def line_sum(part, collective_id):
    rows, width = part.shape
    n = lax.axis_size("tensor")
    chunks = rows // 48
    return pl.pallas_call(
        functools.partial(line_kernel, n, chunks),
        in_specs=[pl.BlockSpec(memory_space=pl.ANY)],
        out_specs=pl.BlockSpec(memory_space=pl.ANY),
        out_shape=jax.ShapeDtypeStruct(part.shape, bf16),
        scratch_shapes=line_scratch(rows, width, chunks),
        compiler_params=pltpu.CompilerParams(
            collective_id=collective_id, has_side_effects=True, vmem_limit_bytes=60 << 20
        ),
        cost_estimate=cost(rows // 9),
        name="line_sum",
    )(part)


def gather_kernel(dps, seqs, own, out, own_sem, recv, send):
    chips = seqs // 2
    dp, seq = lax.axis_index("dp"), lax.axis_index("seq")
    chip, core = seq // 2, lax.rem(seq, 2)
    rows = own.shape[0]
    half = rows // 2
    across = [lax.rem(dp + a, dps) for a in range(1, dps)]
    along = [lax.rem(chip + b, chips) for b in range(1, chips)]
    here = lax.axis_index("tensor")

    def device(d, c, k):
        return {"dp": d, "seq": 2 * c + k, "tensor": here}

    def owner(d, c, k):
        return d * seqs + 2 * c + k

    other = device(dp, chip, 1 - core)
    mine = owner(dp, chip, core)
    by_dp = [device(d, chip, core) for d in across]
    by_chip = [device(dp, c, core) for c in along]
    sends = []

    def copy(index, part, target, number, source=None):
        at = pl.ds(pl.multiple_of(index * rows + part * half, half), half)
        return pltpu.make_async_remote_copy(
            src_ref=out.at[at] if source is None else source,
            dst_ref=out.at[at],
            send_sem=send.at[number],
            recv_sem=recv.at[index, part],
            device_id=target,
            device_id_type=MESH,
        )

    def push(index, part, target):
        source = own.at[pl.ds(part * half, half)] if index is mine else None
        item = copy(index, part, target, len(sends), source)
        item.start()
        sends.append(item)

    def arrived(index, part):
        copy(index, part, other, 0).wait_recv()

    at = pl.ds(pl.multiple_of(mine * rows, rows), rows)
    place = pltpu.make_async_copy(own, out.at[at], own_sem)
    place.start()
    barrier = pltpu.get_barrier_semaphore()
    neighbours = by_dp + by_chip + [other]
    for target in neighbours:
        pl.semaphore_signal(barrier, inc=1, device_id=target, device_id_type=MESH)
    pl.semaphore_wait(barrier, len(neighbours))
    for target in by_dp:
        push(mine, 0, target)
    for target in by_chip:
        push(mine, 1, target)
    for part in range(2):
        push(mine, part, other)
    for target in by_chip:
        push(mine, 0, target)
    for target in by_dp:
        push(mine, 1, target)
    for d in across:
        index = owner(d, chip, core)
        arrived(index, 0)
        for target in by_chip + [other]:
            push(index, 0, target)
    for c in along:
        index = owner(dp, c, core)
        arrived(index, 1)
        for target in by_dp + [other]:
            push(index, 1, target)
    late = [(owner(dp, c, core), 0) for c in along] + [(owner(d, chip, core), 1) for d in across]
    late += [(owner(d, c, core), part) for d in across for c in along for part in range(2)]
    for index, part in late:
        arrived(index, part)
        push(index, part, other)
    for d in [dp] + across:
        for c in [chip] + along:
            for part in range(2):
                arrived(owner(d, c, 1 - core), part)
    place.wait()
    for item in sends:
        item.wait_send()


def gather_shards(own, collective_id):
    dps, seqs = lax.axis_size("dp"), lax.axis_size("seq")
    chips = seqs // 2
    rows, cols = own.shape
    dma = pltpu.SemaphoreType.DMA
    hbm = pl.BlockSpec(memory_space=pl.ANY)
    sends = (dps - 1) * (1 + chips) + (chips - 1) * (1 + dps) + 2 * dps * chips
    return pl.pallas_call(
        functools.partial(gather_kernel, dps, seqs),
        in_specs=[hbm],
        out_specs=hbm,
        out_shape=jax.ShapeDtypeStruct((dps * seqs * rows, cols), own.dtype),
        scratch_shapes=[dma(()), dma((dps * seqs, 2)), dma((sends,))],
        compiler_params=pltpu.CompilerParams(
            collective_id=collective_id, has_side_effects=True, vmem_limit_bytes=60 << 20
        ),
        cost_estimate=cost(40),
        name="gather_shards",
    )(own)


LANES = 128


def diagonal():
    shape = (LANES, LANES)
    return lax.broadcasted_iota(jnp.int32, shape, 0) == lax.broadcasted_iota(jnp.int32, shape, 1)


def to_line(column):
    return jnp.sum(jnp.where(diagonal(), column, 0.0), axis=0, keepdims=True)


def to_column(line):
    return jnp.sum(jnp.where(diagonal(), line, 0.0), axis=1, keepdims=True)


class Exchange:
    def __init__(self, n, lines, land, send, recv):
        self.n, self.lines, self.land, self.send, self.recv = n, lines, land, send, recv
        self.me = lax.axis_index("tensor")
        self.peers = [lax.rem(self.me + d, n) for d in range(1, n)]

    def greet(self):
        barrier = pltpu.get_barrier_semaphore()
        for peer in self.peers:
            pl.semaphore_signal(barrier, inc=1, device_id={"tensor": peer}, device_id_type=MESH)

    def met(self):
        pl.semaphore_wait(pltpu.get_barrier_semaphore(), self.n - 1)

    def copy(self, d, peer, slot):
        return pltpu.make_async_remote_copy(
            src_ref=self.lines,
            dst_ref=self.land.at[slot],
            send_sem=self.send.at[d],
            recv_sem=self.recv.at[slot],
            device_id={"tensor": peer},
            device_id_type=MESH,
        )

    def total(self):
        self.land[self.me] = self.lines[...]
        for d, peer in enumerate(self.peers):
            self.copy(d, peer, self.me).start()
        for d, peer in enumerate(self.peers):
            self.copy(d, peer, peer).wait_recv()
        total = self.land[0]
        for place in range(1, self.n):
            total += self.land[place]
        for d, peer in enumerate(self.peers):
            self.copy(d, peer, self.me).wait_send()
        return total


def exchange_scratch(n, lines):
    dma = pltpu.SemaphoreType.DMA
    return [
        pltpu.VMEM((2 * lines, LANES), f32),
        pltpu.VMEM((n, 2 * lines, LANES), f32),
        dma((n - 1,)),
        dma((n,)),
    ]


def line_count(rows):
    return -(-rows // LANES // 8) * 8


def qkv_kernel(n, rows, cols, x, w, qg, kg, q_low, kv_low, units, squares, raw, *net):
    swap = Exchange(n, *net)
    swap.greet()
    lines = swap.lines.shape[0] // 2
    swap.lines[...] = jnp.zeros_like(swap.lines)
    step = math.gcd(rows, 384)
    for r in range(0, rows, step):
        at = slice(r, r + step)
        for k in range(2):
            value = matmul(x[at, :], w[:, k * cols : (k + 1) * cols])
            raw[k, at, :] = value
            square = jnp.sum(value * value, axis=1, keepdims=True)
            for j in range(0, step, LANES):
                spot = k * lines + (r + j) // LANES
                swap.lines[spot : spot + 1, :] = to_line(square[j : j + LANES])
    swap.met()
    for r in range(0, rows, step):
        at = slice(r, r + step)
        kv_low[1, at, :] = matmul(x[at, :], w[:, 2 * cols : 3 * cols]).astype(bf16)
    total = swap.total()
    squares[...] = total
    width = n * cols
    for r in range(0, rows, LANES):
        at = slice(r, r + LANES)
        for k, gain in enumerate((qg, kg)):
            spot = k * lines + r // LANES
            square = to_column(total[spot : spot + 1, :])
            unit = raw[k, at, :] * lax.rsqrt(square / width + norm_eps)
            units[k, at, :] = unit
            low = (unit * gain[...]).astype(bf16)
            if k == 0:
                q_low[at, :] = low
            else:
                kv_low[0, at, :] = low


def qkv(x, w, qg, kg, m, rows, collective_id):
    n = lax.axis_size("tensor")
    width = x.shape[1]
    cols = qg.shape[1]
    lines = line_count(rows)
    vmem = pl.BlockSpec(memory_space=pltpu.VMEM)
    return pl.pallas_call(
        functools.partial(qkv_kernel, n, rows, cols),
        grid=(1,),
        in_specs=[
            pl.BlockSpec((rows, width), lambda i: (m, 0)),
            pl.BlockSpec((width, 3 * cols), lambda i: (0, 0)),
            vmem,
            vmem,
        ],
        out_specs=[vmem] * 4,
        out_shape=[
            jax.ShapeDtypeStruct((rows, cols), bf16),
            jax.ShapeDtypeStruct((2, rows, cols), bf16),
            jax.ShapeDtypeStruct((2, rows, cols), f32),
            jax.ShapeDtypeStruct((2 * lines, LANES), f32),
        ],
        scratch_shapes=[pltpu.VMEM((2, rows, cols), f32)] + exchange_scratch(n, lines),
        compiler_params=pltpu.CompilerParams(
            collective_id=collective_id, has_side_effects=True, vmem_limit_bytes=60 << 20
        ),
        cost_estimate=cost(15),
        name="qkv",
    )(x, w, qg, kg)


def proj_kernel(cot, back, proj, gain, wo_t, layer, *refs):
    low, grad, gain_grad, layer_out = refs[-4:]
    layer_out[...] = layer[...]

    @pl.when(pl.program_id(0) == 0)
    def _():
        gain_grad[...] = jnp.zeros_like(gain_grad)

    step = ROW_STEP

    def one(r, carry):
        at = pl.ds(pl.multiple_of(r * step, step), step)
        value = proj[at, :].astype(f32)
        inv = lax.rsqrt(jnp.mean(value * value, axis=1, keepdims=True) + norm_eps)
        unit = value * inv
        hidden = cot[at, :].astype(f32) + back[at, :].astype(f32)
        hit = hidden * unit
        gain_grad[...] += fold(hit)
        inner = jnp.mean(hit * gain[...], axis=1, keepdims=True)
        low[at, :] = (inv * (hidden * gain[...] - unit * inner)).astype(bf16)
        return carry

    lax.fori_loop(0, low.shape[0] // step, one, 0)
    grad[...] = matmul(low[...], wo_t[...]).astype(bf16)


def proj_backward(cot, back, proj, gain, w, layer, layer_out, cols, m, rows, proj_m):
    width = cot.shape[1]
    step = BLOCK
    blocks = rows // step

    earlier = [] if layer_out is None else [layer_out]

    def whole(first):
        return pl.BlockSpec((step, width), lambda i: (first * blocks + i, 0))

    return pl.pallas_call(
        proj_kernel,
        grid=(blocks,),
        in_specs=[
            whole(m),
            whole(m),
            whole(proj_m),
            pl.BlockSpec((1, width), lambda i: (0, 0)),
            pl.BlockSpec((width, cols), lambda i: (0, 3)),
            whole(m),
        ]
        + [pl.BlockSpec(memory_space=pl.ANY)] * len(earlier),
        out_specs=[
            whole(0),
            pl.BlockSpec((step, cols), lambda i: (i, 0)),
            pl.BlockSpec((8, width), lambda i: (0, 0)),
            whole(m),
        ],
        out_shape=[
            jax.ShapeDtypeStruct((rows, width), bf16),
            jax.ShapeDtypeStruct((rows, cols), bf16),
            jax.ShapeDtypeStruct((8, width), f32),
            jax.ShapeDtypeStruct(cot.shape, bf16),
        ],
        input_output_aliases={6: 3} if earlier else {},
        compiler_params=pltpu.CompilerParams(vmem_limit_bytes=60 << 20),
        cost_estimate=cost(10),
        name="proj_backward",
    )(cot, back, proj, gain, w, layer, *earlier)


def add_kernel(cot, back, last, *refs):
    refs[-1][...] = cot[...].astype(f32) + back[...].astype(f32) + last[...].astype(f32)


def add_up(cot, back, last, m, out):
    rows, width = last.shape
    step = math.gcd(rows, 128)
    blocks = rows // step
    earlier = [] if out is None else [out]
    whole = pl.BlockSpec((step, width), lambda i: (m * blocks + i, 0))
    return pl.pallas_call(
        add_kernel,
        grid=(blocks,),
        in_specs=[whole, whole, pl.BlockSpec((step, width), lambda i: (i, 0))]
        + [pl.BlockSpec(memory_space=pl.ANY)] * len(earlier),
        out_specs=whole,
        out_shape=jax.ShapeDtypeStruct(cot.shape, f32),
        input_output_aliases={3: 0} if earlier else {},
        compiler_params=pltpu.CompilerParams(vmem_limit_bytes=60 << 20),
        cost_estimate=cost(6),
        name="add_up",
    )(cot, back, last, *earlier)


class Grads:
    def __init__(self, to, stage, sem):
        self.to, self.stage, self.sem = to, stage, sem
        self.wide = stage.shape[1]

    def at(self, owner):
        return pl.ds(pl.multiple_of(owner * self.wide, self.wide), self.wide)

    def store(self, owner, slot):
        width = self.stage.shape[2]
        return pltpu.make_async_copy(
            self.stage.at[slot], self.to.at[self.at(owner), pl.ds(0, width)], self.sem.at[slot]
        )


def last_kernel(
    n, rows, cols, sources, stream, dq, own, mine, got, units, squares, qg, kg, x, proj, attn,
    before, others, w, low, out, gain_grad, g_attn, *scratch,
):
    swap = Exchange(n, *scratch[:4])
    swap.greet()
    xin, x_sem, stage, g_sem = scratch[4:8]
    load_x = pltpu.make_async_copy(x.at[0 if stream else 1], xin, x_sem)
    load_x.start()
    grads = Grads(g_attn, stage, g_sem)
    owners = xin.shape[1] // grads.wide
    if stream:
        s, land, res, pin, p_sem = scratch[8:13]
        loads = [pltpu.make_async_copy(proj[m], pin.at[m], p_sem.at[m]) for m in range(2)]
        for load in loads:
            load.start()
    else:
        s = out
        had, b_sem, gains, n_sem = scratch[8:12]

        def load_before(owner, slot):
            return pltpu.make_async_copy(
                before.at[grads.at(owner), pl.ds(0, 3 * cols)], had.at[slot], b_sem.at[slot]
            )

        load_before(0, 0).start()
    lines = swap.lines.shape[0] // 2
    swap.lines[...] = jnp.zeros_like(swap.lines)
    gain_grad[...] = jnp.zeros_like(gain_grad)
    scale = jnp.where(sources, 1.0, 0.0).astype(f32)
    width = n * cols

    def gathered(k, at):
        both = mine[k, at, :].astype(f32) + got[k, at, :].astype(f32)
        return own[k, at, :] + scale * both

    for r in range(0, rows, LANES):
        at = slice(r, r + LANES)
        for k, gain in enumerate((qg, kg)):
            grad = dq[at, :] if k == 0 else gathered(0, at)
            hit = grad * units[k, at, :]
            gain_grad[8 * k : 8 * k + 8, :] += fold(hit)
            spot = k * lines + r // LANES
            swap.lines[spot : spot + 1, :] = to_line(
                jnp.sum(hit * gain[...], axis=1, keepdims=True)
            )
    swap.met()
    total = swap.total()
    for r in range(0, rows, LANES):
        at = slice(r, r + LANES)
        for k, gain in enumerate((qg, kg)):
            spot = k * lines + r // LANES
            inner = to_column(total[spot : spot + 1, :]) / width
            inv = lax.rsqrt(to_column(squares[spot : spot + 1, :]) / width + norm_eps)
            grad = dq[at, :] if k == 0 else gathered(0, at)
            value = inv * (grad * gain[...] - units[k, at, :] * inner)
            low[at, k * cols : (k + 1) * cols] = value.astype(bf16)
        low[at, 2 * cols :] = gathered(1, at).astype(bf16)
    if stream:
        line = Line(n, out.shape[0] // 48, 48, None, out, s, land, res, scratch[13:])
    step = math.gcd(rows, 384)
    piece = math.gcd(s.shape[1], 512)
    for r in range(0, rows, step):
        at = slice(r, r + step)
        for c in range(0, s.shape[1], piece):
            s[at, c : c + piece] = right_t(low[at, :], w[c : c + piece, :]).astype(bf16)
        if stream:
            line.launch(r // 48, (r + step) // 48)

    def narrow(array, owner, small):
        return left_t(array[:, grads.at(owner)], small)

    def drain():
        for owner in range(max(owners - 2, 0), owners):
            grads.store(owner, owner % 2).wait()

    if stream:

        def job(owner):
            slot = lax.rem(owner, 2)

            @pl.when(owner == 0)
            def _():
                load_x.wait()
                for load in loads:
                    load.wait()

            @pl.when((owner >= 2) & (owner < owners))
            def _():
                grads.store(owner - 2, slot).wait()

            @pl.when(owner < owners)
            def _():
                stage[slot, :, : 3 * cols] = narrow(xin, owner, low[...]).astype(bf16)
                stage[slot, :, 3 * cols :] = (
                    narrow(pin.at[0], owner, attn[0][...])
                    + narrow(pin.at[1], owner, attn[1][...])
                ).astype(bf16)
                grads.store(owner, slot).start()

        assert owners <= rows // 48
        line.stream(job)
        drain()
    else:
        load_x.wait()

        def one(owner, carry):
            slot = lax.rem(owner, 2)
            load_before(owner, slot).wait()

            @pl.when(owner < owners - 1)
            def _():
                load_before(owner + 1, 1 - slot).start()

            @pl.when(owner >= 2)
            def _():
                grads.store(owner - 2, slot).wait()

            value = narrow(xin, owner, low[...]) + had[slot].astype(f32)
            stage[slot] = value.astype(bf16)
            grads.store(owner, slot).start()
            return carry

        lax.fori_loop(0, owners, one, 0)
        heads = cols // HD
        parts = grads.wide // LANES
        gains[...] = jnp.zeros_like(gains)
        first = others[0][...]
        for k in range(2):
            both = gain_grad[8 * k : 8 * k + 8, :] + first[8 * k : 8 * k + 8, :]
            total = jnp.sum(both, axis=0, keepdims=True)
            for owner in range(owners):
                for h in range(heads):
                    gains[owner, k * heads + h, :] = total[0, h * HD : (h + 1) * HD]
        for k, items in enumerate((others[1:3], others[3:])):
            total = sum(jnp.sum(item[...], axis=0, keepdims=True) for item in items)
            for owner in range(owners):
                for j in range(parts):
                    at = (owner * parts + j) * LANES
                    gains[owner, 2 * heads + k * parts + j, :] = total[0, at : at + LANES]
        low_gains, stores = scratch[12], []
        low_gains[...] = gains[...].astype(bf16)
        for owner in range(owners):
            at = pl.ds(owner * grads.wide, low_gains.shape[1])
            to = g_attn.at[at, pl.ds(4 * cols, LANES)]
            stores.append(pltpu.make_async_copy(low_gains.at[owner], to, n_sem.at[owner]))
        for store in stores:
            store.start()
        for store in stores:
            store.wait()
        drain()


def last_sum(
    dq, own, mine, got, units, squares, qg, kg, x, extra, before, w, owners, collective_id
):
    stream = before is None
    n = lax.axis_size("tensor")
    rows, cols = dq.shape
    width = w.shape[0]
    lines = line_count(rows)
    vmem = pl.BlockSpec(memory_space=pltpu.VMEM)
    hbm = pl.BlockSpec(memory_space=pl.ANY)
    dma = pltpu.SemaphoreType.DMA
    wide = width // owners
    weights = pl.BlockSpec((width, 3 * cols), lambda i: (0, 0))

    def kernel(*refs):
        sources = lax.axis_index("seq") < lax.axis_size("seq") // 2
        args = [n, rows, cols, sources, stream, *refs[:9]]
        if stream:
            args += [refs[9:11], refs[11:13], None, None, *refs[13:]]
        else:
            args += [None, None, refs[9], refs[10:14], *refs[14:]]
        last_kernel(*args)

    if stream:
        extra_specs = [hbm, hbm, vmem, vmem]
    else:
        extra, extra_specs = [before, *extra], [hbm] + [vmem] * 4
    shapes = [
        jax.ShapeDtypeStruct((rows, 3 * cols), bf16),
        jax.ShapeDtypeStruct((rows, width), bf16),
        jax.ShapeDtypeStruct((16, cols), f32),
        jax.ShapeDtypeStruct((width, 4 * cols + LANES), bf16),
    ]
    scratch = exchange_scratch(n, lines) + [
        pltpu.VMEM((rows, width), bf16),
        dma(()),
        pltpu.VMEM((2, wide, (4 if stream else 3) * cols), bf16),
        dma((2,)),
    ]
    if stream:
        line = line_scratch(rows, width, rows // 48)
        scratch += line[:3] + [pltpu.VMEM((2, rows, width), bf16), dma((2,))] + line[3:]
    else:
        scratch += [
            pltpu.VMEM((2, wide, 3 * cols), bf16),
            dma((2,)),
            pltpu.VMEM((owners, 16, LANES), f32),
            dma((owners,)),
            pltpu.VMEM((owners, 16, LANES), bf16),
        ]
    return pl.pallas_call(
        kernel,
        grid=(1,),
        in_specs=[vmem] * 8 + [hbm] + extra_specs + [weights],
        out_specs=[vmem, hbm if stream else vmem, vmem, hbm],
        out_shape=shapes,
        scratch_shapes=scratch,
        input_output_aliases={} if stream else {9: 3},
        compiler_params=pltpu.CompilerParams(
            collective_id=collective_id, has_side_effects=True, vmem_limit_bytes=60 << 20
        ),
        cost_estimate=cost(100 if stream else 25),
        name="last_sum" if stream else "last_part",
    )(dq, own, mine, got, units, squares, qg, kg, x, *extra, w)


LINE_ROWS = 48
ROW_STEP = 32
LAG = 3
TILE = 256
NAMES = (
    "part", "x", "cot", "w", "ga", "gm", "first", "proj", "hidden", "inner", "layer", "low",
    "gu", "back", "pre", "grads", "gm_grad", "s", "land", "swap", "res", "acc", "h", "xin", "cin",
    "wgt", "wut", "wdt", "gt", "ut", "it", "jt", "stage", "load_sem", "in_send", "in_recv", "swap_recv",
    "out_send", "out_recv", "store_sem", "w_sem", "x_sem", "c_sem", "h_sem", "y_sem", "t_sem",
    "r_sem", "g_sem",
)


class Mlp:
    def __init__(self, n, micros, rows, *refs):
        for name, ref in zip(NAMES, refs):
            setattr(self, name, ref)
        self.micros, self.rows = micros, rows
        self.chunks = rows // LINE_ROWS
        self.hidden_units = self.w.shape[1] // 3
        self.tiles = self.hidden_units // TILE
        i = lax.axis_index("tensor")
        half = n // 2
        left = i < half
        self.inward = jnp.where(left, i + 1, i - 1)
        self.outward = jnp.where(left, i - 1, i + 1)
        self.relay = (i > 0) & (i < n - 1)
        self.mid = (i == half - 1) | (i == half)

    def at(self, m, c):
        start = pl.multiple_of((m * self.chunks + c) * LINE_ROWS, LINE_ROWS)
        return pl.ds(start, LINE_ROWS)

    def micro(self, m):
        return pl.ds(pl.multiple_of(m * self.rows, self.rows), self.rows)

    def move_in(self, m, c):
        return pltpu.make_async_remote_copy(
            src_ref=self.s.at[self.at(m, c)],
            dst_ref=self.land.at[self.at(m, c)],
            send_sem=self.in_send.at[m, c],
            recv_sem=self.in_recv.at[m, c],
            device_id={"tensor": self.inward},
            device_id_type=MESH,
        )

    def move_swap(self, m, c):
        return pltpu.make_async_remote_copy(
            src_ref=self.s.at[self.at(m, c)],
            dst_ref=self.swap.at[self.at(m, c)],
            send_sem=self.in_send.at[m, c],
            recv_sem=self.swap_recv.at[m, c],
            device_id={"tensor": self.inward},
            device_id_type=MESH,
        )

    def move_out(self, m, c):
        return pltpu.make_async_remote_copy(
            src_ref=self.res.at[self.at(m, c)],
            dst_ref=self.res.at[self.at(m, c)],
            send_sem=self.out_send.at[m, c],
            recv_sem=self.out_recv.at[m, c],
            device_id={"tensor": self.outward},
            device_id_type=MESH,
        )

    def send_in(self, m, c):
        @pl.when(self.mid)
        def _():
            self.move_swap(m, c).start()

        @pl.when(~self.mid)
        def _():
            self.move_in(m, c).start()

    def each_chunk(self, body):
        def one(c, carry):
            body(c)
            return carry

        lax.fori_loop(0, self.chunks, one, 0)

    def launch(self, m):
        @pl.when(~self.relay)
        def _():
            self.each_chunk(lambda c: self.send_in(m, c))

    def settle(self, m):
        def one(c):
            self.move_in(m, c).wait_send()

            @pl.when(self.relay)
            def _():
                self.move_out(m, c).wait_send()

        self.each_chunk(one)

    def begin(self):
        others = pl.ds(self.rows, (self.micros - 1) * self.rows)
        load = pltpu.make_async_copy(self.part, self.s.at[others], self.load_sem)
        load.start()
        rest = self.micro(0)
        done = pltpu.make_async_copy(self.first, self.res.at[rest], self.y_sem)
        done.start()
        self.load_x(0, self.x).start()
        for copy in self.load_w(0, 0):
            copy.start()
        barrier = pltpu.get_barrier_semaphore()
        pl.semaphore_signal(
            barrier, inc=1, device_id={"tensor": self.inward}, device_id_type=MESH
        )

        @pl.when(self.relay)
        def _():
            pl.semaphore_signal(
                barrier, inc=1, device_id={"tensor": self.outward}, device_id_type=MESH
            )

        pl.semaphore_wait(barrier, jnp.where(self.relay, 2, 1))
        load.wait()
        done.wait()
        for m in range(1, self.micros):
            self.launch(m)
        self.gm_grad[...] = jnp.zeros_like(self.gm_grad)

    def reduce(self, m, c):
        @pl.when(self.relay)
        def _():
            self.move_in(m, c).wait_recv()
            a = self.at(m, c)
            self.s[a, :] = (self.s[a, :].astype(f32) + self.land[a, :].astype(f32)).astype(bf16)
            self.send_in(m, c)

    def store(self, m, c, to):
        a = self.at(m, c)
        return pltpu.make_async_copy(self.res.at[a], to.at[a], self.store_sem.at[m, c])

    def spread(self, which, m, c):
        a = self.at(m, c)

        @pl.when(self.mid)
        def _():
            self.move_swap(m, c).wait_recv()
            self.res[a, :] = (self.s[a, :].astype(f32) + self.swap[a, :].astype(f32)).astype(bf16)

        @pl.when(~self.mid)
        def _():
            self.move_out(m, c).wait_recv()

        @pl.when(self.relay)
        def _():
            self.move_out(m, c).start()

        @pl.when(which == 0)
        def _():
            self.store(m, c, self.proj).start()

        @pl.when(which == 2)
        def _():
            self.store(m, c, self.back).start()

    def load_x(self, m, source):
        return pltpu.make_async_copy(source.at[self.micro(m)], self.xin, self.x_sem)

    def load_c(self, m):
        return pltpu.make_async_copy(self.cot.at[self.micro(m)], self.cin, self.c_sem)

    def store_h(self, m, to):
        return pltpu.make_async_copy(self.h, to.at[self.micro(m)], self.h_sem)

    def store_layer(self, m):
        return pltpu.make_async_copy(self.xin, self.layer.at[self.micro(m)], self.y_sem)

    def cols(self, t, which=0):
        return pl.ds(pl.multiple_of(which * self.hidden_units + t * TILE, TILE), TILE)

    def load_w(self, t, slot):
        return [
            pltpu.make_async_copy(
                self.w.at[:, self.cols(t, which)], to.at[slot], self.w_sem.at[which, slot]
            )
            for which, to in enumerate((self.wgt, self.wut, self.wdt))
        ]

    def load_pre(self, m, t, slot):
        return [
            pltpu.make_async_copy(
                self.pre.at[self.micro(m), self.cols(t, which)],
                to.at[slot],
                self.r_sem.at[which, slot],
            )
            for which, to in enumerate((self.gt, self.ut))
        ]

    def store_tile(self, which, source, to, m, at, slot):
        return pltpu.make_async_copy(
            source.at[slot], to.at[self.micro(m), at], self.t_sem.at[which, slot]
        )

    def store_pre(self, m, t, slot):
        return (
            self.store_tile(0, self.gt, self.pre, m, self.cols(t, 0), slot),
            self.store_tile(1, self.ut, self.pre, m, self.cols(t, 1), slot),
            self.store_tile(2, self.it, self.inner, m, self.cols(t), slot),
        )

    def store_low(self, m, t, slot):
        return (
            self.store_tile(2, self.it, self.gu, m, self.cols(t, 0), slot),
            self.store_tile(3, self.jt, self.gu, m, self.cols(t, 1), slot),
        )

    def row_groups(self, body):
        step = ROW_STEP

        def one(r, carry):
            body(pl.ds(pl.multiple_of(r * step, step), step), r * step)
            return carry

        lax.fori_loop(0, self.rows // step, one, 0)

    def forward_start(self, m):
        @pl.when(m > 0)
        def _():
            self.each_chunk(lambda c: self.store(m, c, self.proj).wait())

        self.load_x(m, self.x).wait()
        base = m * self.rows
        gain = self.ga[...]

        def one(at, r):
            total = self.res[pl.ds(pl.multiple_of(base + r, ROW_STEP), ROW_STEP), :].astype(f32)
            inv = lax.rsqrt(jnp.mean(total * total, axis=1, keepdims=True) + norm_eps)
            self.h[at, :] = (self.xin[at, :].astype(f32) + total * inv * gain).astype(bf16)

        self.row_groups(one)
        self.store_h(m, self.hidden).start()

    def backward_start(self, m):
        for copy in self.load_pre(m, 0, 0):
            copy.start()
        self.load_x(m, self.hidden).wait()
        self.load_c(m).wait()
        base = m * self.rows
        gain = self.gm[...]

        def one(at, r):
            total = self.res[pl.ds(pl.multiple_of(base + r, ROW_STEP), ROW_STEP), :].astype(f32)
            inv = lax.rsqrt(jnp.mean(total * total, axis=1, keepdims=True) + norm_eps)
            unit = total * inv
            c = self.cin[at, :].astype(f32)
            self.xin[at, :] = (self.xin[at, :].astype(f32) + unit * gain).astype(bf16)
            hit = c * unit
            self.gm_grad[...] += fold(hit)
            dy = c * gain
            inner = jnp.mean(hit * gain, axis=1, keepdims=True)
            self.h[at, :] = (inv * (dy - unit * inner)).astype(bf16)

        self.row_groups(one)
        self.store_layer(m).start()
        self.store_h(m, self.low).start()

    def tile_weights(self, t, slot, last):
        for copy in self.load_w(t, slot):
            copy.wait()

        @pl.when(jnp.logical_not(last))
        def _():
            for copy in self.load_w(lax.rem(t + 1, self.tiles), 1 - slot):
                copy.start()

    def add(self, t, at, value):
        @pl.when(t == 0)
        def _():
            self.acc[:, at] = value

        @pl.when(t > 0)
        def _():
            self.acc[:, at] += value

    def forward_tile(self, m, t):
        slot = lax.rem(t, 2)
        self.tile_weights(t, slot, False)

        @pl.when(t >= 2)
        def _():
            for copy in self.store_pre(m, t - 2, slot):
                copy.wait()

        gate = matmul(self.h[...], self.wgt[slot])
        up = matmul(self.h[...], self.wut[slot])
        self.gt[slot] = gate.astype(bf16)
        self.ut[slot] = up.astype(bf16)
        self.it[slot] = (gate * jax.nn.sigmoid(gate) * up).astype(bf16)
        for copy in self.store_pre(m, t, slot):
            copy.start()
        wide = self.acc.shape[1]
        step = math.gcd(wide, 512)
        for k in range(0, wide, step):
            self.add(t, slice(k, k + step), right_t(self.it[slot], self.wdt[slot, k : k + step, :]))

        @pl.when(t == self.tiles - 1)
        def _():
            for back in range(min(2, self.tiles)):
                at = self.tiles - 1 - back
                for copy in self.store_pre(m, at, at % 2):
                    copy.wait()
            self.store_h(m, self.hidden).wait()
            self.finish(m, m > 0)

    def backward_tile(self, m, t, last):
        slot = lax.rem(t, 2)
        self.tile_weights(t, slot, last & (t == self.tiles - 1))
        for copy in self.load_pre(m, t, slot):
            copy.wait()

        @pl.when(t < self.tiles - 1)
        def _():
            for copy in self.load_pre(m, t + 1, 1 - slot):
                copy.start()

        @pl.when(t >= 2)
        def _():
            for copy in self.store_low(m, t - 2, slot):
                copy.wait()

        grad = matmul(self.h[...], self.wdt[slot])
        gate = self.gt[slot].astype(f32)
        sig = jax.nn.sigmoid(gate)
        act = grad * sig
        self.jt[slot] = (act * gate).astype(bf16)
        self.it[slot] = (
            act * self.ut[slot].astype(f32) * (1.0 + gate * (1.0 - sig))
        ).astype(bf16)
        for copy in self.store_low(m, t, slot):
            copy.start()
        wide = self.acc.shape[1]
        step = math.gcd(wide, 512)
        for k in range(0, wide, step):
            self.add(
                t,
                slice(k, k + step),
                right_t(self.it[slot], self.wgt[slot, k : k + step, :])
                + right_t(self.jt[slot], self.wut[slot, k : k + step, :]),
            )

        @pl.when(t == self.tiles - 1)
        def _():
            for back in range(min(2, self.tiles)):
                at = self.tiles - 1 - back
                for copy in self.store_low(m, at, at % 2):
                    copy.wait()
            self.store_h(m, self.low).wait()
            self.store_layer(m).wait()
            self.finish(m, True)

    def load_bigs(self, source):
        return (
            pltpu.make_async_copy(source.at[self.micro(0)], self.xin, self.x_sem),
            pltpu.make_async_copy(source.at[self.micro(1)], self.cin, self.c_sem),
        )

    def load_units(self, source, w, slot):
        return [
            pltpu.make_async_copy(
                source.at[self.micro(m), self.cols(w)], to.at[slot], self.r_sem.at[m, slot]
            )
            for m, to in enumerate((self.gt, self.ut))
        ]

    def start_units(self, w, slot):
        split = 2 * self.tiles

        @pl.when(w < split)
        def _():
            for copy in self.load_units(self.gu, w, slot):
                copy.start()

        @pl.when((w >= split) & (w < 3 * self.tiles))
        def _():
            for copy in self.load_units(self.inner, w - split, slot):
                copy.start()

    def store_grads(self, w, slot):
        return pltpu.make_async_copy(
            self.stage.at[slot], self.grads.at[:, self.cols(w), :], self.g_sem.at[slot]
        )

    def grad_tile(self, w):
        slot = lax.rem(w, 2)
        split = 2 * self.tiles

        @pl.when((w == 0) | (w == split))
        def _():
            for copy in self.load_bigs(self.hidden):
                copy.wait()

        for copy in self.load_units(self.gu, 0, slot):
            copy.wait()
        self.start_units(w + 1, 1 - slot)

        @pl.when(w >= 2)
        def _():
            self.store_grads(w - 2, slot).wait()

        value = left_t(self.gt[slot], self.xin[...]) + left_t(self.ut[slot], self.cin[...])
        owners, _, wide = self.stage.shape[1:]
        for owner in range(owners):
            self.stage[slot, owner] = value[:, owner * wide : (owner + 1) * wide].astype(bf16)
        self.store_grads(w, slot).start()

        @pl.when(w == split - 1)
        def _():
            for copy in self.load_bigs(self.low):
                copy.start()

        @pl.when(w == 3 * self.tiles - 1)
        def _():
            self.store_grads(w - 1, 1 - slot).wait()
            self.store_grads(w, slot).wait()

    def finish(self, m, sent):
        @pl.when(sent)
        def _():
            self.settle(m)

        base = m * self.rows

        def one(at, r):
            self.s[pl.ds(pl.multiple_of(base + r, ROW_STEP), ROW_STEP), :] = self.acc[at, :].astype(bf16)

        self.row_groups(one)
        self.launch(m)

    def job(self, index, step):
        micros = self.micros
        m = lax.rem(index, micros)
        forward = index < micros
        last = index == 2 * micros - 1

        @pl.when(forward & (step == 0))
        def _():
            self.forward_start(m)

        @pl.when(jnp.logical_not(forward) & (step == 0))
        def _():
            self.backward_start(m)

        tiled = (step >= 1) & (step <= self.tiles)

        @pl.when(forward & tiled)
        def _():
            self.forward_tile(m, step - 1)

        @pl.when(jnp.logical_not(forward) & tiled)
        def _():
            self.backward_tile(m, step - 1, last)

        done = step == self.tiles

        @pl.when(done & (index < micros - 1))
        def _():
            self.load_x(index + 1, self.x).start()

        @pl.when(done & (index >= micros - 1) & jnp.logical_not(last))
        def _():
            self.load_x(index + 1 - micros, self.hidden).start()
            self.load_c(index + 1 - micros).start()

        @pl.when(done & last)
        def _():
            for copy in self.load_bigs(self.hidden):
                copy.start()
            self.start_units(0, 0)

    def run(self):
        n, micros = self.chunks, self.micros
        total = 3 * micros * n
        self.begin()

        def clock(k, carry):
            @pl.when(k < total)
            def _():
                self.reduce(lax.rem(k // n, micros), lax.rem(k, n))

            back = k - LAG

            @pl.when((back >= n) & (back < total))
            def _():
                sum_index = back // n
                self.spread(sum_index // micros, lax.rem(sum_index, micros), lax.rem(back, n))

            turn = back - n

            @pl.when((turn >= 0) & (turn < 2 * micros * n))
            def _():
                self.job(turn // n, lax.rem(turn, n))

            turn = turn - 2 * micros * n + n - self.tiles - 1

            @pl.when((turn >= 0) & (turn < 3 * self.tiles))
            def _():
                self.grad_tile(turn)

            return carry

        grads_at = 2 * micros * n + LAG + self.tiles + 1
        lax.fori_loop(n, max(total + LAG, grads_at + 3 * self.tiles), clock, 0)
        for m in range(micros):
            self.settle(m)
            self.each_chunk(lambda c: self.store(m, c, self.back).wait())


def mlp_kernel(n, micros, rows, *refs):
    Mlp(n, micros, rows, *refs).run()


def feed_forward(part, x, cot, w, ga, gm, first, micros, owners):
    assert micros == 2
    both, width = x.shape
    hidden = w.shape[1] // 3
    rows = both // micros
    chunks = rows // LINE_ROWS
    dma = pltpu.SemaphoreType.DMA
    hbm = pl.BlockSpec(memory_space=pl.ANY)
    vmem = pl.BlockSpec(memory_space=pltpu.VMEM)
    wide = jax.ShapeDtypeStruct((both, width), bf16)
    unit = jax.ShapeDtypeStruct((both, hidden), bf16)
    two = jax.ShapeDtypeStruct((both, 2 * hidden), bf16)
    return pl.pallas_call(
        functools.partial(mlp_kernel, lax.axis_size("tensor"), micros, rows),
        in_specs=[hbm] * 4 + [vmem] * 2 + [hbm],
        out_specs=[hbm] * 9 + [vmem],
        out_shape=[wide, wide, unit, wide, wide, two, wide, two]
        + [jax.ShapeDtypeStruct((owners, 3 * hidden, width // owners), bf16)]
        + [jax.ShapeDtypeStruct((8, width), f32)],
        scratch_shapes=[
            pltpu.VMEM((both, width), bf16),
            pltpu.VMEM((both, width), bf16),
            pltpu.VMEM((both, width), bf16),
            pltpu.VMEM((both, width), bf16),
            pltpu.VMEM((rows, width), f32),
            pltpu.VMEM((rows, width), bf16),
            pltpu.VMEM((rows, width), bf16),
            pltpu.VMEM((rows, width), bf16),
            pltpu.VMEM((2, width, TILE), bf16),
            pltpu.VMEM((2, width, TILE), bf16),
            pltpu.VMEM((2, width, TILE), bf16),
            pltpu.VMEM((2, rows, TILE), bf16),
            pltpu.VMEM((2, rows, TILE), bf16),
            pltpu.VMEM((2, rows, TILE), bf16),
            pltpu.VMEM((2, rows, TILE), bf16),
            pltpu.VMEM((2, owners, TILE, width // owners), bf16),
            dma(()),
            dma((micros, chunks)),
            dma((micros, chunks)),
            dma((micros, chunks)),
            dma((micros, chunks)),
            dma((micros, chunks)),
            dma((micros, chunks)),
            dma((3, 2)),
            dma(()),
            dma(()),
            dma(()),
            dma(()),
            dma((4, 2)),
            dma((2, 2)),
            dma((2,)),
        ],
        compiler_params=pltpu.CompilerParams(
            collective_id=1, has_side_effects=True, vmem_limit_bytes=60 << 20
        ),
        cost_estimate=cost(both // 4),
        name="feed_forward",
    )(part, x, cot, w, ga, gm, first)


def attn_scores(meta, i, trunk_rows, q, kt, kp, ko):
    scale = HD ** (-0.5)
    block = meta[i, 0]
    n_par = meta[i, 2]
    n_own = meta[i, 3]
    n_trunk = meta[i, 4]
    st = right_t(q, kt) * scale
    sp = right_t(q, kp) * scale
    so = right_t(q, ko) * scale
    row = lax.broadcasted_iota(jnp.int32, (BLOCK, trunk_rows), 0) + block * BLOCK
    col = lax.broadcasted_iota(jnp.int32, (BLOCK, trunk_rows), 1)
    st = jnp.where((col < n_trunk) & (col <= row), st, masked_score)
    row = lax.broadcasted_iota(jnp.int32, (BLOCK, BLOCK), 0)
    col = lax.broadcasted_iota(jnp.int32, (BLOCK, BLOCK), 1)
    sp = jnp.where(col < n_par, sp, masked_score)
    so = jnp.where((col < n_own) & (col <= row), so, masked_score)
    return st, sp, so


def attn_fwd_kernel(trunk_rows, meta, q, trunk, par, own, out, lse):
    i = pl.program_id(1)
    st, sp, so = attn_scores(meta, i, trunk_rows, q[...], trunk[0], par[0], own[0])
    top = jnp.maximum(
        jnp.max(st, axis=1, keepdims=True),
        jnp.maximum(jnp.max(sp, axis=1, keepdims=True), jnp.max(so, axis=1, keepdims=True)),
    )
    et, ep, eo = jnp.exp(st - top), jnp.exp(sp - top), jnp.exp(so - top)
    total = (
        jnp.sum(et, axis=1, keepdims=True)
        + jnp.sum(ep, axis=1, keepdims=True)
        + jnp.sum(eo, axis=1, keepdims=True)
    )
    acc = matmul(et.astype(bf16), trunk[1])
    acc += matmul(ep.astype(bf16), par[1])
    acc += matmul(eo.astype(bf16), own[1])
    out[...] = (acc / total).astype(bf16)
    lse[...] = jnp.broadcast_to(top + jnp.log(total), (BLOCK, HD))


def attn_bwd_kernel(
    trunk_rows, n_q, meta, q, do, lse, trunk, par, own, dq, d_own, d_src, acc,
):
    i = pl.program_id(1)

    @pl.when(i == 0)
    def _():
        acc[...] = jnp.zeros_like(acc)

    scale = HD ** (-0.5)
    qv, dov = q[...], do[...]
    scores = attn_scores(meta, i, trunk_rows, qv, trunk[0], par[0], own[0])
    top = lse[:, 0:1]
    probs = [jnp.exp(s - top) for s in scores]
    grads = [right_t(dov, v[1]) for v in (trunk, par, own)]
    inner = sum(jnp.sum(p * g, axis=1, keepdims=True) for p, g in zip(probs, grads))
    low = [(p * (g - inner)).astype(bf16) for p, g in zip(probs, grads)]
    probs = [p.astype(bf16) for p in probs]
    dq[...] = scale * (
        matmul(low[0], trunk[0]) + matmul(low[1], par[0]) + matmul(low[2], own[0])
    )
    d_own[0] = scale * left_t(low[2], qv)
    d_own[1] = left_t(probs[2], dov)
    acc[0, :trunk_rows] += left_t(low[0], qv)
    acc[1, :trunk_rows] += left_t(probs[0], dov)
    at = pl.ds(pl.multiple_of(trunk_rows + meta[i, 1] * BLOCK, BLOCK), BLOCK)
    acc[0, at] += left_t(low[1], qv)
    acc[1, at] += left_t(probs[1], dov)

    @pl.when(i == n_q - 1)
    def _():
        d_src[0] = (scale * acc[0]).astype(bf16)
        d_src[1] = acc[1].astype(bf16)


def kv_specs(trunk_rows):
    skip = trunk_rows // BLOCK
    trunk = pl.BlockSpec((2, trunk_rows, HD), lambda h, i, meta: (0, 0, h))
    par = pl.BlockSpec((2, BLOCK, HD), lambda h, i, meta: (0, skip + meta[i, 1], h))
    own = pl.BlockSpec((2, BLOCK, HD), lambda h, i, meta: (0, i, h))
    return [trunk, par, own]


def attend_forward(meta, q, sources, own_kv, trunk_rows):
    rows, width = q.shape
    own = pl.BlockSpec((BLOCK, HD), lambda h, i, meta: (i, h))
    return pl.pallas_call(
        functools.partial(attn_fwd_kernel, trunk_rows),
        grid_spec=pltpu.PrefetchScalarGridSpec(
            num_scalar_prefetch=1,
            grid=(width // HD, rows // BLOCK),
            in_specs=[own] + kv_specs(trunk_rows),
            out_specs=[own, own],
        ),
        out_shape=[
            jax.ShapeDtypeStruct((rows, width), bf16),
            jax.ShapeDtypeStruct((rows, width), f32),
        ],
        compiler_params=pltpu.CompilerParams(vmem_limit_bytes=32 << 20),
        cost_estimate=cost(12),
        name="attend_forward",
    )(meta, q, sources, sources, own_kv)


def attend_backward(meta, q, do, lse, sources, own_kv, trunk_rows):
    rows, width = q.shape
    own = pl.BlockSpec((BLOCK, HD), lambda h, i, meta: (i, h))
    own_two = pl.BlockSpec((2, BLOCK, HD), lambda h, i, meta: (0, i, h))
    all_rows = sources.shape[1]
    n_q = rows // BLOCK
    return pl.pallas_call(
        functools.partial(attn_bwd_kernel, trunk_rows, n_q),
        grid_spec=pltpu.PrefetchScalarGridSpec(
            num_scalar_prefetch=1,
            grid=(width // HD, n_q),
            in_specs=[own, own, own] + kv_specs(trunk_rows),
            out_specs=[
                own,
                own_two,
                pl.BlockSpec((2, all_rows, HD), lambda h, i, meta: (0, 0, h)),
            ],
            scratch_shapes=[pltpu.VMEM((2, all_rows, HD), f32)],
        ),
        out_shape=[
            jax.ShapeDtypeStruct((rows, width), f32),
            jax.ShapeDtypeStruct((2, rows, width), f32),
            jax.ShapeDtypeStruct(sources.shape, bf16),
        ],
        compiler_params=pltpu.CompilerParams(vmem_limit_bytes=40 << 20),
        cost_estimate=cost(22),
        name="attend_backward",
    )(meta, q, do, lse, sources, sources, own_kv)


def group_perm(n, k):
    half = n // 2
    return [(i, i // half * half + (i % half + k) % half) for i in range(n)]


def fetch_sources(block, hold):
    n = lax.axis_size("seq")
    half = n // 2
    place = lax.axis_index("seq")
    spot = lax.rem(place, half)
    got = lax.ppermute(block, "seq", [(i, i + half) for i in range(half)])
    got = after(got, *hold)
    mine = jnp.where(place < half, block, got)
    parts = [mine] + [lax.ppermute(mine, "seq", group_perm(n, k)) for k in range(1, half)]
    out = []
    for source in range(half):
        pick = parts[0]
        for k in range(1, half):
            pick = jnp.where(lax.rem(spot - k + half, half) == source, parts[k], pick)
        out.append(pick)
    return jnp.concatenate(out, axis=1), got


def sum_over_group(grads):
    n = lax.axis_size("seq")
    half = n // 2
    spot = lax.rem(lax.axis_index("seq"), half)
    rows = grads.shape[1] // half
    pieces = [grads[:, s * rows : (s + 1) * rows] for s in range(half)]

    def piece(index):
        pick = pieces[0]
        for s in range(1, half):
            pick = jnp.where(index == s, pieces[s], pick)
        return pick

    total = piece(spot).astype(f32)
    for k in range(1, half):
        sent = piece(lax.rem(spot + k, half))
        total += lax.ppermute(sent, "seq", group_perm(n, k)).astype(f32)
    return total.astype(bf16)


def return_to_sources(total):
    n = lax.axis_size("seq")
    half = n // 2
    return lax.ppermute(total, "seq", [(i + half, i) for i in range(half)])


def gather_rows(item):
    return lax.all_gather(item, ("dp", "seq"), axis=0, tiled=True)


def scatter_low(item):
    return lax.psum_scatter(item, ("dp", "seq"), scatter_dimension=0, tiled=True)


def scatter_rows(item):
    return scatter_low(item).astype(f32)


def block_meta(parents, lengths, rows, n_blocks):
    seg_count = parents.shape[0]
    branches = (seg_count - 1) // 3
    trunk_blocks = n_blocks - 3 * branches
    blocks = lax.axis_index("seq") * (rows // BLOCK) + jnp.arange(rows // BLOCK, dtype=jnp.int32)
    seg = jnp.maximum(blocks - trunk_blocks + 1, 0)
    hit = seg[:, None] == jnp.arange(seg_count, dtype=jnp.int32)[None, :]
    parent = jnp.sum(jnp.where(hit, parents[None, :], 0), axis=1)
    own_len = jnp.sum(jnp.where(hit, lengths[None, :], 0), axis=1)
    hit = parent[:, None] == jnp.arange(seg_count, dtype=jnp.int32)[None, :]
    par_len = jnp.sum(jnp.where(hit, lengths[None, :], 0), axis=1)
    return jnp.stack(
        [
            blocks,
            jnp.maximum(parent - 1, 0),
            jnp.where(parent > 0, par_len, 0),
            jnp.where(blocks >= trunk_blocks, own_len, 0),
            jnp.broadcast_to(lengths[0], blocks.shape),
        ],
        axis=1,
    ).astype(jnp.int32)


def per_device(
    tokens, cotangent, w_query, w_key, w_value, w_out, w_gate, w_up, w_down,
    query_gain, key_gain, attn_gain, mlp_gain, parent_of, seg_length,
):
    micros, _, rows, width = tokens.shape
    n_blocks = rows // BLOCK * lax.axis_size("seq")
    heads = w_query.shape[1] // HD
    full_width = heads * HD * lax.axis_size("tensor")
    branches = (parent_of.shape[2] - 1) // 3
    trunk_rows = (n_blocks - 3 * branches) * BLOCK

    cols = w_query.shape[1]
    owners = lax.axis_size("dp") * lax.axis_size("seq")
    gains = [query_gain.reshape(-1), key_gain.reshape(-1), attn_gain, mlp_gain]
    gains = jnp.concatenate(gains)
    count = gains.shape[0]
    lines = -(-count // LANES)
    gains = jnp.pad(gains, (0, lines * LANES - count)).reshape(lines, LANES)
    gains = jnp.pad(gains, ((0, width // owners - lines), (0, 0)))
    w_attn = gather_shards(
        jnp.concatenate([w_query, w_key, w_value, w_out.T, gains], axis=1), 9
    )
    w_own = jnp.concatenate([w_gate, w_up, w_down.T], axis=1)
    gains = w_attn[:, 4 * cols :].reshape(owners, -1, LANES)[:, :lines]
    gains = gains.reshape(owners, lines * LANES)
    own = query_gain.size

    def head_gain(block):
        block = block.reshape(owners, heads, HD // owners)
        return jnp.swapaxes(block, 0, 1).reshape(-1).astype(f32)

    q_gain = head_gain(gains[:, :own])
    k_gain = head_gain(gains[:, own : 2 * own])
    a_gain = gains[:, 2 * own : 2 * own + attn_gain.size].reshape(-1).astype(f32)
    m_gain = gains[:, 2 * own + attn_gain.size : count].reshape(-1).astype(f32)
    wo_t = w_attn[:, 3 * cols : 4 * cols]
    q_gain, k_gain, a_gain = q_gain[None], k_gain[None], a_gain[None]

    x = tokens.reshape(micros * rows, width)
    cot = cotangent.reshape(micros * rows, width)
    q_lows, kv_lows, units, squares = zip(
        *(qkv(x, w_attn, q_gain, k_gain, m, rows, 6 + m) for m in range(micros))
    )
    sources, metas, attn_lows, lses, parts, first = [], [], [], [], [], None
    for m in range(micros):
        block = kv_lows[m] if m == 0 else after(kv_lows[m], attn_lows[0])
        source, got = fetch_sources(block, (q_lows[1], w_own) if m == 0 else (first,))
        sources.append(source)
        metas.append(block_meta(parent_of[m, 0], seg_length[m, 0], rows, n_blocks))
        attn_low, lse = attend_forward(metas[m], q_lows[m], sources[m], kv_lows[m], trunk_rows)
        attn_lows.append(attn_low)
        lses.append(lse)
        parts.append(right_t(attn_low, wo_t).astype(bf16))
        if m == 0:
            first = line_sum(parts[0], 0)
            w_mlp = gather_rows(after(w_own, got))
    proj, _, _, layer, _, _, back, _, mlp_grads, gm_grad = feed_forward(
        parts[1], x, cot, w_mlp, a_gain, m_gain[None], first,
        micros, owners,
    )
    hidden = w_gate.shape[1]
    g_attn, qk_grad, ga_grads, layer_out = None, None, [], None
    proj_lows, dqs, d_owns, sums = [], [], [], []
    for m in range(micros):
        proj_low, attn_grad, grad, layer_out = proj_backward(
            cot, back, first if m == 0 else proj, after(a_gain, sums[0]) if m else a_gain, w_attn,
            layer, layer_out, cols, m, rows, m
        )
        ga_grads.append(grad)
        dq, d_own, d_src = attend_backward(
            metas[m], q_lows[m], attn_grad, lses[m], sources[m], kv_lows[m], trunk_rows
        )
        sums.append(sum_over_group(d_src))
        proj_lows.append(proj_low)
        dqs.append(dq)
        d_owns.append(d_own)

    lasts = []
    for m in range(micros):
        got = return_to_sources(sums[m])
        if m > 0:
            input_grad = add_up(cot, back, lasts[0], 0, None)
            got = after(got, input_grad)
        else:
            got = after(got, dqs[-1])
            mlp_grads = after(mlp_grads.reshape(-1, mlp_grads.shape[2]), got)
            mlp_grads = scatter_low(mlp_grads)
        extra = [*proj_lows, *attn_lows] if m == 0 else [qk_grad, *ga_grads, gm_grad]
        _, last, qk_grad, g_attn = last_sum(
            dqs[m], d_owns[m], sums[m], got, units[m], squares[m], q_gain, k_gain,
            x.reshape(micros, rows, width), extra, g_attn, w_attn, owners, 5 if m else 3,
        )
        lasts.append(line_sum(last, 4) if m else last)
    g_attn = scatter_low(after(g_attn, mlp_grads))
    g_attn = after(g_attn, qk_grad).astype(f32)

    lines = g_attn[:, 4 * cols :]
    share = HD // owners
    place = lax.axis_index("dp") * lax.axis_size("seq") + lax.axis_index("seq")
    head_lines = lax.dynamic_slice_in_dim(lines[: 2 * heads], place * share, share, 1)
    own_lines = lines[2 * heads : 2 * heads + 2 * attn_gain.size // LANES].reshape(2, -1)
    input_grad = add_up(cot, back, lasts[1], 1, input_grad)
    return (
        layer_out.reshape(tokens.shape),
        input_grad.reshape(tokens.shape),
        g_attn[:, :cols],
        g_attn[:, cols : 2 * cols],
        g_attn[:, 2 * cols : 3 * cols],
        g_attn[:, 3 * cols : 4 * cols].T,
        mlp_grads[:hidden].astype(f32).T,
        mlp_grads[hidden : 2 * hidden].astype(f32).T,
        mlp_grads[2 * hidden :].astype(f32),
        head_lines[:heads],
        head_lines[heads:],
        own_lines[0],
        own_lines[1],
    )


def solution(mesh):
    rows = P(None, "dp", "seq", None)
    by_row = P(("dp", "seq"), "tensor")
    by_col = P("tensor", ("dp", "seq"))
    gain = P(("dp", "seq"))
    tree = P(None, "dp", None)
    weights = (by_row, by_row, by_row, by_col, by_row, by_row, by_col, by_col, by_col, gain, gain)
    return jax.shard_map(
        per_device,
        mesh=mesh,
        in_specs=(rows, rows) + weights + (tree, tree),
        out_specs=(rows, rows) + weights,
        check_vma=False,
    )
```

```python
import functools
import math

import jax
import jax.numpy as jnp
from jax import lax
from jax.experimental import pallas as pl
from jax.experimental.pallas import tpu as pltpu
from jax.sharding import PartitionSpec as P

HD = 128
BLOCK = 256

norm_eps = 1e-06
masked_score = -1e30
f32 = jnp.float32
bf16 = jnp.bfloat16


def matmul(left, right):
    return jnp.dot(left, right, preferred_element_type=f32)


def left_t(left, right):
    return lax.dot_general(left, right, (((0,), (0,)), ((), ())), preferred_element_type=f32)


def right_t(left, right):
    return lax.dot_general(left, right, (((1,), (1,)), ((), ())), preferred_element_type=f32)


MESH = pl.DeviceIdType.MESH


def cost(us):
    return pl.CostEstimate(flops=int(us * 1.1e9), bytes_accessed=0, transcendentals=0)


def fold(rows):
    total = rows[0:8]
    for j in range(8, rows.shape[0], 8):
        total += rows[j : j + 8]
    return total


def after(value, *earlier):
    hbm = pl.BlockSpec(memory_space=pl.ANY)
    return pl.pallas_call(
        lambda *refs: None,
        in_specs=[hbm] * (1 + len(earlier)),
        out_specs=hbm,
        out_shape=jax.ShapeDtypeStruct(value.shape, value.dtype),
        input_output_aliases={0: 0},
        name="after",
    )(value, *earlier)


class Line:
    def __init__(self, n, chunks, rows, part, out, s, land, res, sems):
        self.chunks, self.rows = chunks, rows
        self.part, self.out, self.s, self.land, self.res = part, out, s, land, res
        (
            self.load_sem,
            self.in_send,
            self.in_recv,
            self.out_send,
            self.out_recv,
            self.store_sem,
        ) = sems
        i = lax.axis_index("tensor")
        half = n // 2
        left = i < half
        self.inward = jnp.where(left, i + 1, i - 1)
        self.outward = jnp.where(left, i - 1, i + 1)
        self.relay = (i > 0) & (i < n - 1)
        self.mid = (i == half - 1) | (i == half)
        self.slot = jnp.where(self.mid, 1, 0)

    def at(self, c):
        return pl.ds(pl.multiple_of(c * self.rows, self.rows), self.rows)

    def load(self):
        return pltpu.make_async_copy(self.part, self.s, self.load_sem)

    def inward_copy(self, c, slot):
        return pltpu.make_async_remote_copy(
            src_ref=self.s.at[self.at(c)],
            dst_ref=self.land.at[slot, self.at(c)],
            send_sem=self.in_send.at[c],
            recv_sem=self.in_recv.at[slot, c],
            device_id={"tensor": self.inward},
            device_id_type=MESH,
        )

    def outward_copy(self, c):
        return pltpu.make_async_remote_copy(
            src_ref=self.res.at[self.at(c)],
            dst_ref=self.res.at[self.at(c)],
            send_sem=self.out_send.at[c],
            recv_sem=self.out_recv.at[c],
            device_id={"tensor": self.outward},
            device_id_type=MESH,
        )

    def store(self, c):
        return pltpu.make_async_copy(
            self.res.at[self.at(c)], self.out.at[self.at(c)], self.store_sem.at[c]
        )

    def begin(self):
        self.load().start()
        barrier = pltpu.get_barrier_semaphore()
        pl.semaphore_signal(
            barrier, inc=1, device_id={"tensor": self.inward}, device_id_type=MESH
        )

        @pl.when(self.relay)
        def _():
            pl.semaphore_signal(
                barrier, inc=1, device_id={"tensor": self.outward}, device_id_type=MESH
            )

        pl.semaphore_wait(barrier, jnp.where(self.relay, 2, 1))
        self.load().wait()
        self.launch(0, self.chunks)

    def launch(self, first, last):
        @pl.when(~self.relay)
        def _():
            def one(c, carry):
                self.inward_copy(c, self.slot).start()
                return carry

            lax.fori_loop(first, last, one, 0)

    def stream(self, job=None):
        def step(c, carry):
            if job is not None:
                job(c)
            self.reduce(c)

            @pl.when(c > 0)
            def _():
                self.spread(c - 1)

            return carry

        lax.fori_loop(0, self.chunks, step, 0)
        self.spread(self.chunks - 1)
        self.end()

    def reduce(self, c):
        @pl.when(self.relay)
        def _():
            self.inward_copy(c, 0).wait_recv()
            a = self.at(c)
            self.s[a, :] = (self.s[a, :].astype(f32) + self.land[0, a, :].astype(f32)).astype(bf16)
            self.inward_copy(c, self.slot).start()

    def spread(self, c):
        a = self.at(c)

        @pl.when(self.mid)
        def _():
            self.inward_copy(c, 1).wait_recv()
            self.res[a, :] = (
                self.s[a, :].astype(f32) + self.land[1, a, :].astype(f32)
            ).astype(bf16)

        @pl.when(~self.mid)
        def _():
            self.outward_copy(c).wait_recv()

        @pl.when(self.relay)
        def _():
            self.outward_copy(c).start()

        self.store(c).start()

    def end(self):
        def one(c, carry):
            self.inward_copy(c, self.slot).wait_send()

            @pl.when(self.relay)
            def _():
                self.outward_copy(c).wait_send()

            self.store(c).wait()
            return carry

        lax.fori_loop(0, self.chunks, one, 0)


def line_scratch(rows, width, chunks):
    dma = pltpu.SemaphoreType.DMA
    return [
        pltpu.VMEM((rows, width), bf16),
        pltpu.VMEM((2, rows, width), bf16),
        pltpu.VMEM((rows, width), bf16),
        dma(()),
        dma((chunks,)),
        dma((2, chunks)),
        dma((chunks,)),
        dma((chunks,)),
        dma((chunks,)),
    ]


def line_kernel(n, chunks, part, out, s, land, res, *sems):
    line = Line(n, chunks, part.shape[0] // chunks, part, out, s, land, res, sems)
    line.begin()
    line.stream()


def line_sum(part, collective_id):
    rows, width = part.shape
    n = lax.axis_size("tensor")
    chunks = rows // 48
    return pl.pallas_call(
        functools.partial(line_kernel, n, chunks),
        in_specs=[pl.BlockSpec(memory_space=pl.ANY)],
        out_specs=pl.BlockSpec(memory_space=pl.ANY),
        out_shape=jax.ShapeDtypeStruct(part.shape, bf16),
        scratch_shapes=line_scratch(rows, width, chunks),
        compiler_params=pltpu.CompilerParams(
            collective_id=collective_id, has_side_effects=True, vmem_limit_bytes=60 << 20
        ),
        cost_estimate=cost(rows // 9),
        name="line_sum",
    )(part)


def gather_kernel(dps, seqs, own, out, own_sem, recv, send):
    chips = seqs // 2
    dp, seq = lax.axis_index("dp"), lax.axis_index("seq")
    chip, core = seq // 2, lax.rem(seq, 2)
    rows = own.shape[0]
    half = rows // 2
    across = [lax.rem(dp + a, dps) for a in range(1, dps)]
    along = [lax.rem(chip + b, chips) for b in range(1, chips)]
    here = lax.axis_index("tensor")

    def device(d, c, k):
        return {"dp": d, "seq": 2 * c + k, "tensor": here}

    def owner(d, c, k):
        return d * seqs + 2 * c + k

    other = device(dp, chip, 1 - core)
    mine = owner(dp, chip, core)
    by_dp = [device(d, chip, core) for d in across]
    by_chip = [device(dp, c, core) for c in along]
    sends = []

    def copy(index, part, target, number, source=None):
        at = pl.ds(pl.multiple_of(index * rows + part * half, half), half)
        return pltpu.make_async_remote_copy(
            src_ref=out.at[at] if source is None else source,
            dst_ref=out.at[at],
            send_sem=send.at[number],
            recv_sem=recv.at[index, part],
            device_id=target,
            device_id_type=MESH,
        )

    def push(index, part, target):
        source = own.at[pl.ds(part * half, half)] if index is mine else None
        item = copy(index, part, target, len(sends), source)
        item.start()
        sends.append(item)

    def arrived(index, part):
        copy(index, part, other, 0).wait_recv()

    at = pl.ds(pl.multiple_of(mine * rows, rows), rows)
    place = pltpu.make_async_copy(own, out.at[at], own_sem)
    place.start()
    barrier = pltpu.get_barrier_semaphore()
    neighbours = by_dp + by_chip + [other]
    for target in neighbours:
        pl.semaphore_signal(barrier, inc=1, device_id=target, device_id_type=MESH)
    pl.semaphore_wait(barrier, len(neighbours))
    for target in by_dp:
        push(mine, 0, target)
    for target in by_chip:
        push(mine, 1, target)
    for part in range(2):
        push(mine, part, other)
    for target in by_chip:
        push(mine, 0, target)
    for target in by_dp:
        push(mine, 1, target)
    for d in across:
        index = owner(d, chip, core)
        arrived(index, 0)
        for target in by_chip + [other]:
            push(index, 0, target)
    for c in along:
        index = owner(dp, c, core)
        arrived(index, 1)
        for target in by_dp + [other]:
            push(index, 1, target)
    late = [(owner(dp, c, core), 0) for c in along] + [(owner(d, chip, core), 1) for d in across]
    late += [(owner(d, c, core), part) for d in across for c in along for part in range(2)]
    for index, part in late:
        arrived(index, part)
        push(index, part, other)
    for d in [dp] + across:
        for c in [chip] + along:
            for part in range(2):
                arrived(owner(d, c, 1 - core), part)
    place.wait()
    for item in sends:
        item.wait_send()


def gather_shards(own, collective_id):
    dps, seqs = lax.axis_size("dp"), lax.axis_size("seq")
    chips = seqs // 2
    rows, cols = own.shape
    dma = pltpu.SemaphoreType.DMA
    hbm = pl.BlockSpec(memory_space=pl.ANY)
    sends = (dps - 1) * (1 + chips) + (chips - 1) * (1 + dps) + 2 * dps * chips
    return pl.pallas_call(
        functools.partial(gather_kernel, dps, seqs),
        in_specs=[hbm],
        out_specs=hbm,
        out_shape=jax.ShapeDtypeStruct((dps * seqs * rows, cols), own.dtype),
        scratch_shapes=[dma(()), dma((dps * seqs, 2)), dma((sends,))],
        compiler_params=pltpu.CompilerParams(
            collective_id=collective_id, has_side_effects=True, vmem_limit_bytes=60 << 20
        ),
        cost_estimate=cost(40),
        name="gather_shards",
    )(own)


LANES = 128


def diagonal():
    shape = (LANES, LANES)
    return lax.broadcasted_iota(jnp.int32, shape, 0) == lax.broadcasted_iota(jnp.int32, shape, 1)


def to_line(column):
    return jnp.sum(jnp.where(diagonal(), column, 0.0), axis=0, keepdims=True)


def to_column(line):
    return jnp.sum(jnp.where(diagonal(), line, 0.0), axis=1, keepdims=True)


class Exchange:
    def __init__(self, n, lines, land, send, recv):
        self.n, self.lines, self.land, self.send, self.recv = n, lines, land, send, recv
        self.me = lax.axis_index("tensor")
        self.peers = [lax.rem(self.me + d, n) for d in range(1, n)]

    def greet(self):
        barrier = pltpu.get_barrier_semaphore()
        for peer in self.peers:
            pl.semaphore_signal(barrier, inc=1, device_id={"tensor": peer}, device_id_type=MESH)

    def met(self):
        pl.semaphore_wait(pltpu.get_barrier_semaphore(), self.n - 1)

    def copy(self, d, peer, slot):
        return pltpu.make_async_remote_copy(
            src_ref=self.lines,
            dst_ref=self.land.at[slot],
            send_sem=self.send.at[d],
            recv_sem=self.recv.at[slot],
            device_id={"tensor": peer},
            device_id_type=MESH,
        )

    def total(self):
        self.land[self.me] = self.lines[...]
        for d, peer in enumerate(self.peers):
            self.copy(d, peer, self.me).start()
        for d, peer in enumerate(self.peers):
            self.copy(d, peer, peer).wait_recv()
        total = self.land[0]
        for place in range(1, self.n):
            total += self.land[place]
        for d, peer in enumerate(self.peers):
            self.copy(d, peer, self.me).wait_send()
        return total


def exchange_scratch(n, lines):
    dma = pltpu.SemaphoreType.DMA
    return [
        pltpu.VMEM((2 * lines, LANES), f32),
        pltpu.VMEM((n, 2 * lines, LANES), f32),
        dma((n - 1,)),
        dma((n,)),
    ]


def line_count(rows):
    return -(-rows // LANES // 8) * 8


def qkv_kernel(n, rows, cols, x, w, qg, kg, q_low, kv_low, units, squares, raw, *net):
    swap = Exchange(n, *net)
    swap.greet()
    lines = swap.lines.shape[0] // 2
    swap.lines[...] = jnp.zeros_like(swap.lines)
    step = math.gcd(rows, 384)
    for r in range(0, rows, step):
        at = slice(r, r + step)
        for k in range(2):
            value = matmul(x[at, :], w[:, k * cols : (k + 1) * cols])
            raw[k, at, :] = value
            square = jnp.sum(value * value, axis=1, keepdims=True)
            for j in range(0, step, LANES):
                spot = k * lines + (r + j) // LANES
                swap.lines[spot : spot + 1, :] = to_line(square[j : j + LANES])
    swap.met()
    for r in range(0, rows, step):
        at = slice(r, r + step)
        kv_low[1, at, :] = matmul(x[at, :], w[:, 2 * cols : 3 * cols]).astype(bf16)
    total = swap.total()
    squares[...] = total
    width = n * cols
    for r in range(0, rows, LANES):
        at = slice(r, r + LANES)
        for k, gain in enumerate((qg, kg)):
            spot = k * lines + r // LANES
            square = to_column(total[spot : spot + 1, :])
            unit = raw[k, at, :] * lax.rsqrt(square / width + norm_eps)
            units[k, at, :] = unit
            low = (unit * gain[...]).astype(bf16)
            if k == 0:
                q_low[at, :] = low
            else:
                kv_low[0, at, :] = low


def qkv(x, w, qg, kg, m, rows, collective_id):
    n = lax.axis_size("tensor")
    width = x.shape[1]
    cols = qg.shape[1]
    lines = line_count(rows)
    vmem = pl.BlockSpec(memory_space=pltpu.VMEM)
    return pl.pallas_call(
        functools.partial(qkv_kernel, n, rows, cols),
        grid=(1,),
        in_specs=[
            pl.BlockSpec((rows, width), lambda i: (m, 0)),
            pl.BlockSpec((width, 3 * cols), lambda i: (0, 0)),
            vmem,
            vmem,
        ],
        out_specs=[vmem] * 4,
        out_shape=[
            jax.ShapeDtypeStruct((rows, cols), bf16),
            jax.ShapeDtypeStruct((2, rows, cols), bf16),
            jax.ShapeDtypeStruct((2, rows, cols), f32),
            jax.ShapeDtypeStruct((2 * lines, LANES), f32),
        ],
        scratch_shapes=[pltpu.VMEM((2, rows, cols), f32)] + exchange_scratch(n, lines),
        compiler_params=pltpu.CompilerParams(
            collective_id=collective_id, has_side_effects=True, vmem_limit_bytes=60 << 20
        ),
        cost_estimate=cost(15),
        name="qkv",
    )(x, w, qg, kg)


def proj_kernel(cot, back, proj, gain, wo_t, layer, *refs):
    low, grad, gain_grad, layer_out = refs[-4:]
    layer_out[...] = layer[...]

    @pl.when(pl.program_id(0) == 0)
    def _():
        gain_grad[...] = jnp.zeros_like(gain_grad)

    step = ROW_STEP

    def one(r, carry):
        at = pl.ds(pl.multiple_of(r * step, step), step)
        value = proj[at, :].astype(f32)
        inv = lax.rsqrt(jnp.mean(value * value, axis=1, keepdims=True) + norm_eps)
        unit = value * inv
        hidden = cot[at, :].astype(f32) + back[at, :].astype(f32)
        hit = hidden * unit
        gain_grad[...] += fold(hit)
        inner = jnp.mean(hit * gain[...], axis=1, keepdims=True)
        low[at, :] = (inv * (hidden * gain[...] - unit * inner)).astype(bf16)
        return carry

    lax.fori_loop(0, low.shape[0] // step, one, 0)
    grad[...] = matmul(low[...], wo_t[...]).astype(bf16)


def proj_backward(cot, back, proj, gain, w, layer, layer_out, cols, m, rows, proj_m):
    width = cot.shape[1]
    step = BLOCK
    blocks = rows // step

    earlier = [] if layer_out is None else [layer_out]

    def whole(first):
        return pl.BlockSpec((step, width), lambda i: (first * blocks + i, 0))

    return pl.pallas_call(
        proj_kernel,
        grid=(blocks,),
        in_specs=[
            whole(m),
            whole(m),
            whole(proj_m),
            pl.BlockSpec((1, width), lambda i: (0, 0)),
            pl.BlockSpec((width, cols), lambda i: (0, 3)),
            whole(m),
        ]
        + [pl.BlockSpec(memory_space=pl.ANY)] * len(earlier),
        out_specs=[
            whole(0),
            pl.BlockSpec((step, cols), lambda i: (i, 0)),
            pl.BlockSpec((8, width), lambda i: (0, 0)),
            whole(m),
        ],
        out_shape=[
            jax.ShapeDtypeStruct((rows, width), bf16),
            jax.ShapeDtypeStruct((rows, cols), bf16),
            jax.ShapeDtypeStruct((8, width), f32),
            jax.ShapeDtypeStruct(cot.shape, bf16),
        ],
        input_output_aliases={6: 3} if earlier else {},
        compiler_params=pltpu.CompilerParams(vmem_limit_bytes=60 << 20),
        cost_estimate=cost(10),
        name="proj_backward",
    )(cot, back, proj, gain, w, layer, *earlier)


def add_kernel(cot, back, last, *refs):
    refs[-1][...] = cot[...].astype(f32) + back[...].astype(f32) + last[...].astype(f32)


def add_up(cot, back, last, m, out):
    rows, width = last.shape
    step = math.gcd(rows, 128)
    blocks = rows // step
    earlier = [] if out is None else [out]
    whole = pl.BlockSpec((step, width), lambda i: (m * blocks + i, 0))
    return pl.pallas_call(
        add_kernel,
        grid=(blocks,),
        in_specs=[whole, whole, pl.BlockSpec((step, width), lambda i: (i, 0))]
        + [pl.BlockSpec(memory_space=pl.ANY)] * len(earlier),
        out_specs=whole,
        out_shape=jax.ShapeDtypeStruct(cot.shape, f32),
        input_output_aliases={3: 0} if earlier else {},
        compiler_params=pltpu.CompilerParams(vmem_limit_bytes=60 << 20),
        cost_estimate=cost(6),
        name="add_up",
    )(cot, back, last, *earlier)


class Grads:
    def __init__(self, to, stage, sem):
        self.to, self.stage, self.sem = to, stage, sem
        self.wide = stage.shape[1]

    def at(self, owner):
        return pl.ds(pl.multiple_of(owner * self.wide, self.wide), self.wide)

    def store(self, owner, slot):
        width = self.stage.shape[2]
        return pltpu.make_async_copy(
            self.stage.at[slot], self.to.at[self.at(owner), pl.ds(0, width)], self.sem.at[slot]
        )


def last_kernel(
    n, rows, cols, sources, stream, dq, own, mine, got, units, squares, qg, kg, x, proj, attn,
    before, others, w, low, out, gain_grad, g_attn, *scratch,
):
    swap = Exchange(n, *scratch[:4])
    swap.greet()
    xin, x_sem, stage, g_sem = scratch[4:8]
    load_x = pltpu.make_async_copy(x.at[0 if stream else 1], xin, x_sem)
    load_x.start()
    grads = Grads(g_attn, stage, g_sem)
    owners = xin.shape[1] // grads.wide
    if stream:
        s, land, res, pin, p_sem = scratch[8:13]
        loads = [pltpu.make_async_copy(proj[m], pin.at[m], p_sem.at[m]) for m in range(2)]
        for load in loads:
            load.start()
    else:
        s = out
        had, b_sem, gains, n_sem = scratch[8:12]

        def load_before(owner, slot):
            return pltpu.make_async_copy(
                before.at[grads.at(owner), pl.ds(0, 3 * cols)], had.at[slot], b_sem.at[slot]
            )

        load_before(0, 0).start()
    lines = swap.lines.shape[0] // 2
    swap.lines[...] = jnp.zeros_like(swap.lines)
    gain_grad[...] = jnp.zeros_like(gain_grad)
    scale = jnp.where(sources, 1.0, 0.0).astype(f32)
    width = n * cols

    def gathered(k, at):
        both = mine[k, at, :].astype(f32) + got[k, at, :].astype(f32)
        return own[k, at, :] + scale * both

    for r in range(0, rows, LANES):
        at = slice(r, r + LANES)
        for k, gain in enumerate((qg, kg)):
            grad = dq[at, :] if k == 0 else gathered(0, at)
            hit = grad * units[k, at, :]
            gain_grad[8 * k : 8 * k + 8, :] += fold(hit)
            spot = k * lines + r // LANES
            swap.lines[spot : spot + 1, :] = to_line(
                jnp.sum(hit * gain[...], axis=1, keepdims=True)
            )
    swap.met()
    total = swap.total()
    for r in range(0, rows, LANES):
        at = slice(r, r + LANES)
        for k, gain in enumerate((qg, kg)):
            spot = k * lines + r // LANES
            inner = to_column(total[spot : spot + 1, :]) / width
            inv = lax.rsqrt(to_column(squares[spot : spot + 1, :]) / width + norm_eps)
            grad = dq[at, :] if k == 0 else gathered(0, at)
            value = inv * (grad * gain[...] - units[k, at, :] * inner)
            low[at, k * cols : (k + 1) * cols] = value.astype(bf16)
        low[at, 2 * cols :] = gathered(1, at).astype(bf16)
    if stream:
        line = Line(n, out.shape[0] // 48, 48, None, out, s, land, res, scratch[13:])
    step = math.gcd(rows, 384)
    piece = math.gcd(s.shape[1], 512)
    for r in range(0, rows, step):
        at = slice(r, r + step)
        for c in range(0, s.shape[1], piece):
            s[at, c : c + piece] = right_t(low[at, :], w[c : c + piece, :]).astype(bf16)
        if stream:
            line.launch(r // 48, (r + step) // 48)

    def narrow(array, owner, small):
        return left_t(array[:, grads.at(owner)], small)

    def drain():
        for owner in range(max(owners - 2, 0), owners):
            grads.store(owner, owner % 2).wait()

    if stream:

        def job(owner):
            slot = lax.rem(owner, 2)

            @pl.when(owner == 0)
            def _():
                load_x.wait()
                for load in loads:
                    load.wait()

            @pl.when((owner >= 2) & (owner < owners))
            def _():
                grads.store(owner - 2, slot).wait()

            @pl.when(owner < owners)
            def _():
                stage[slot, :, : 3 * cols] = narrow(xin, owner, low[...]).astype(bf16)
                stage[slot, :, 3 * cols :] = (
                    narrow(pin.at[0], owner, attn[0][...])
                    + narrow(pin.at[1], owner, attn[1][...])
                ).astype(bf16)
                grads.store(owner, slot).start()

        assert owners <= rows // 48
        line.stream(job)
        drain()
    else:
        load_x.wait()

        def one(owner, carry):
            slot = lax.rem(owner, 2)
            load_before(owner, slot).wait()

            @pl.when(owner < owners - 1)
            def _():
                load_before(owner + 1, 1 - slot).start()

            @pl.when(owner >= 2)
            def _():
                grads.store(owner - 2, slot).wait()

            value = narrow(xin, owner, low[...]) + had[slot].astype(f32)
            stage[slot] = value.astype(bf16)
            grads.store(owner, slot).start()
            return carry

        lax.fori_loop(0, owners, one, 0)
        heads = cols // HD
        parts = grads.wide // LANES
        gains[...] = jnp.zeros_like(gains)
        first = others[0][...]
        for k in range(2):
            both = gain_grad[8 * k : 8 * k + 8, :] + first[8 * k : 8 * k + 8, :]
            total = jnp.sum(both, axis=0, keepdims=True)
            for owner in range(owners):
                for h in range(heads):
                    gains[owner, k * heads + h, :] = total[0, h * HD : (h + 1) * HD]
        for k, items in enumerate((others[1:3], others[3:])):
            total = sum(jnp.sum(item[...], axis=0, keepdims=True) for item in items)
            for owner in range(owners):
                for j in range(parts):
                    at = (owner * parts + j) * LANES
                    gains[owner, 2 * heads + k * parts + j, :] = total[0, at : at + LANES]
        low_gains, stores = scratch[12], []
        low_gains[...] = gains[...].astype(bf16)
        for owner in range(owners):
            at = pl.ds(owner * grads.wide, low_gains.shape[1])
            to = g_attn.at[at, pl.ds(4 * cols, LANES)]
            stores.append(pltpu.make_async_copy(low_gains.at[owner], to, n_sem.at[owner]))
        for store in stores:
            store.start()
        for store in stores:
            store.wait()
        drain()


def last_sum(
    dq, own, mine, got, units, squares, qg, kg, x, extra, before, w, owners, collective_id
):
    stream = before is None
    n = lax.axis_size("tensor")
    rows, cols = dq.shape
    width = w.shape[0]
    lines = line_count(rows)
    vmem = pl.BlockSpec(memory_space=pltpu.VMEM)
    hbm = pl.BlockSpec(memory_space=pl.ANY)
    dma = pltpu.SemaphoreType.DMA
    wide = width // owners
    weights = pl.BlockSpec((width, 3 * cols), lambda i: (0, 0))

    def kernel(*refs):
        sources = lax.axis_index("seq") < lax.axis_size("seq") // 2
        args = [n, rows, cols, sources, stream, *refs[:9]]
        if stream:
            args += [refs[9:11], refs[11:13], None, None, *refs[13:]]
        else:
            args += [None, None, refs[9], refs[10:14], *refs[14:]]
        last_kernel(*args)

    if stream:
        extra_specs = [hbm, hbm, vmem, vmem]
    else:
        extra, extra_specs = [before, *extra], [hbm] + [vmem] * 4
    shapes = [
        jax.ShapeDtypeStruct((rows, 3 * cols), bf16),
        jax.ShapeDtypeStruct((rows, width), bf16),
        jax.ShapeDtypeStruct((16, cols), f32),
        jax.ShapeDtypeStruct((width, 4 * cols + LANES), bf16),
    ]
    scratch = exchange_scratch(n, lines) + [
        pltpu.VMEM((rows, width), bf16),
        dma(()),
        pltpu.VMEM((2, wide, (4 if stream else 3) * cols), bf16),
        dma((2,)),
    ]
    if stream:
        line = line_scratch(rows, width, rows // 48)
        scratch += line[:3] + [pltpu.VMEM((2, rows, width), bf16), dma((2,))] + line[3:]
    else:
        scratch += [
            pltpu.VMEM((2, wide, 3 * cols), bf16),
            dma((2,)),
            pltpu.VMEM((owners, 16, LANES), f32),
            dma((owners,)),
            pltpu.VMEM((owners, 16, LANES), bf16),
        ]
    return pl.pallas_call(
        kernel,
        grid=(1,),
        in_specs=[vmem] * 8 + [hbm] + extra_specs + [weights],
        out_specs=[vmem, hbm if stream else vmem, vmem, hbm],
        out_shape=shapes,
        scratch_shapes=scratch,
        input_output_aliases={} if stream else {9: 3},
        compiler_params=pltpu.CompilerParams(
            collective_id=collective_id, has_side_effects=True, vmem_limit_bytes=60 << 20
        ),
        cost_estimate=cost(100 if stream else 25),
        name="last_sum" if stream else "last_part",
    )(dq, own, mine, got, units, squares, qg, kg, x, *extra, w)


LINE_ROWS = 48
ROW_STEP = 32
LAG = 3
PARTS = 3
TILE = 256
NAMES = (
    "part", "x", "cot", "w", "ga", "gm", "first", "proj", "hidden", "inner", "layer", "low",
    "gu", "back", "pre", "grads", "grads_down", "gm_grad", "s", "land", "swap", "res", "acc", "h", "xin", "cin",
    "wgt", "wut", "wdt", "gt", "ut", "it", "jt", "stage", "load_sem", "in_send", "in_recv", "swap_recv",
    "out_send", "out_recv", "store_sem", "w_sem", "x_sem", "c_sem", "h_sem", "y_sem", "t_sem",
    "r_sem", "g_sem",
)


class Mlp:
    def __init__(self, n, micros, rows, *refs):
        for name, ref in zip(NAMES, refs):
            setattr(self, name, ref)
        self.micros, self.rows = micros, rows
        self.chunks = rows // LINE_ROWS
        self.hidden_units = self.w.shape[1] // 3
        self.tiles = self.hidden_units // TILE
        i = lax.axis_index("tensor")
        half = n // 2
        left = i < half
        self.inward = jnp.where(left, i + 1, i - 1)
        self.outward = jnp.where(left, i - 1, i + 1)
        self.relay = (i > 0) & (i < n - 1)
        self.mid = (i == half - 1) | (i == half)

    def at(self, m, c):
        start = pl.multiple_of((m * self.chunks + c) * LINE_ROWS, LINE_ROWS)
        return pl.ds(start, LINE_ROWS)

    def micro(self, m):
        return pl.ds(pl.multiple_of(m * self.rows, self.rows), self.rows)

    def move_in(self, m, c):
        return pltpu.make_async_remote_copy(
            src_ref=self.s.at[self.at(m, c)],
            dst_ref=self.land.at[self.at(m, c)],
            send_sem=self.in_send.at[m, c],
            recv_sem=self.in_recv.at[m, c],
            device_id={"tensor": self.inward},
            device_id_type=MESH,
        )

    def move_swap(self, m, c):
        return pltpu.make_async_remote_copy(
            src_ref=self.s.at[self.at(m, c)],
            dst_ref=self.swap.at[self.at(m, c)],
            send_sem=self.in_send.at[m, c],
            recv_sem=self.swap_recv.at[m, c],
            device_id={"tensor": self.inward},
            device_id_type=MESH,
        )

    def move_out(self, m, c):
        return pltpu.make_async_remote_copy(
            src_ref=self.res.at[self.at(m, c)],
            dst_ref=self.res.at[self.at(m, c)],
            send_sem=self.out_send.at[m, c],
            recv_sem=self.out_recv.at[m, c],
            device_id={"tensor": self.outward},
            device_id_type=MESH,
        )

    def send_in(self, m, c):
        @pl.when(self.mid)
        def _():
            self.move_swap(m, c).start()

        @pl.when(~self.mid)
        def _():
            self.move_in(m, c).start()

    def each_chunk(self, body):
        def one(c, carry):
            body(c)
            return carry

        lax.fori_loop(0, self.chunks, one, 0)

    def launch(self, m):
        @pl.when(~self.relay)
        def _():
            self.each_chunk(lambda c: self.send_in(m, c))

    def settle(self, m):
        def one(c):
            self.move_in(m, c).wait_send()

            @pl.when(self.relay)
            def _():
                self.move_out(m, c).wait_send()

        self.each_chunk(one)

    def begin(self):
        others = pl.ds(self.rows, (self.micros - 1) * self.rows)
        load = pltpu.make_async_copy(self.part, self.s.at[others], self.load_sem)
        load.start()
        rest = self.micro(0)
        done = pltpu.make_async_copy(self.first, self.res.at[rest], self.y_sem)
        done.start()
        self.load_x(0, self.x).start()
        for copy in self.load_w(0, 0):
            copy.start()
        barrier = pltpu.get_barrier_semaphore()
        pl.semaphore_signal(
            barrier, inc=1, device_id={"tensor": self.inward}, device_id_type=MESH
        )

        @pl.when(self.relay)
        def _():
            pl.semaphore_signal(
                barrier, inc=1, device_id={"tensor": self.outward}, device_id_type=MESH
            )

        pl.semaphore_wait(barrier, jnp.where(self.relay, 2, 1))
        load.wait()
        done.wait()
        for m in range(1, self.micros):
            self.launch(m)
        self.gm_grad[...] = jnp.zeros_like(self.gm_grad)

    def reduce(self, m, c):
        @pl.when(self.relay)
        def _():
            self.move_in(m, c).wait_recv()
            a = self.at(m, c)
            self.s[a, :] = (self.s[a, :].astype(f32) + self.land[a, :].astype(f32)).astype(bf16)
            self.send_in(m, c)

    def store(self, m, c, to):
        a = self.at(m, c)
        return pltpu.make_async_copy(self.res.at[a], to.at[a], self.store_sem.at[m, c])

    def spread(self, which, m, c):
        a = self.at(m, c)

        @pl.when(self.mid)
        def _():
            self.move_swap(m, c).wait_recv()
            self.res[a, :] = (self.s[a, :].astype(f32) + self.swap[a, :].astype(f32)).astype(bf16)

        @pl.when(~self.mid)
        def _():
            self.move_out(m, c).wait_recv()

        @pl.when(self.relay)
        def _():
            self.move_out(m, c).start()

        @pl.when(which == 0)
        def _():
            self.store(m, c, self.proj).start()

        @pl.when(which == 2)
        def _():
            self.store(m, c, self.back).start()

    def load_x(self, m, source):
        return pltpu.make_async_copy(source.at[self.micro(m)], self.xin, self.x_sem)

    def load_c(self, m):
        return pltpu.make_async_copy(self.cot.at[self.micro(m)], self.cin, self.c_sem)

    def store_h(self, m, to):
        return pltpu.make_async_copy(self.h, to.at[self.micro(m)], self.h_sem)

    def store_layer(self, m):
        return pltpu.make_async_copy(self.xin, self.layer.at[self.micro(m)], self.y_sem)

    def cols(self, t, which=0):
        return pl.ds(pl.multiple_of(which * self.hidden_units + t * TILE, TILE), TILE)

    def load_w(self, t, slot):
        return [
            pltpu.make_async_copy(
                self.w.at[:, self.cols(t, which)], to.at[slot], self.w_sem.at[which, slot]
            )
            for which, to in enumerate((self.wgt, self.wut, self.wdt))
        ]

    def load_pre(self, m, t, slot):
        return [
            pltpu.make_async_copy(
                self.pre.at[self.micro(m), self.cols(t, which)],
                to.at[slot],
                self.r_sem.at[which, slot],
            )
            for which, to in enumerate((self.gt, self.ut))
        ]

    def store_tile(self, which, source, to, m, at, slot):
        return pltpu.make_async_copy(
            source.at[slot], to.at[self.micro(m), at], self.t_sem.at[which, slot]
        )

    def store_pre(self, m, t, slot):
        return (
            self.store_tile(0, self.gt, self.pre, m, self.cols(t, 0), slot),
            self.store_tile(1, self.ut, self.pre, m, self.cols(t, 1), slot),
            self.store_tile(2, self.it, self.inner, m, self.cols(t), slot),
        )

    def store_low(self, m, t, slot):
        return (
            self.store_tile(2, self.it, self.gu, m, self.cols(t, 0), slot),
            self.store_tile(3, self.jt, self.gu, m, self.cols(t, 1), slot),
        )

    def row_groups(self, body):
        step = ROW_STEP

        def one(r, carry):
            body(pl.ds(pl.multiple_of(r * step, step), step), r * step)
            return carry

        lax.fori_loop(0, self.rows // step, one, 0)

    def forward_start(self, m):
        @pl.when(m > 0)
        def _():
            self.each_chunk(lambda c: self.store(m, c, self.proj).wait())

        self.load_x(m, self.x).wait()
        base = m * self.rows
        gain = self.ga[...]

        def one(at, r):
            total = self.res[pl.ds(pl.multiple_of(base + r, ROW_STEP), ROW_STEP), :].astype(f32)
            inv = lax.rsqrt(jnp.mean(total * total, axis=1, keepdims=True) + norm_eps)
            self.h[at, :] = (self.xin[at, :].astype(f32) + total * inv * gain).astype(bf16)

        self.row_groups(one)
        self.store_h(m, self.hidden).start()

    def backward_start(self, m):
        for copy in self.load_pre(m, 0, 0):
            copy.start()
        self.load_x(m, self.hidden).wait()
        self.load_c(m).wait()
        base = m * self.rows
        gain = self.gm[...]

        def one(at, r):
            total = self.res[pl.ds(pl.multiple_of(base + r, ROW_STEP), ROW_STEP), :].astype(f32)
            inv = lax.rsqrt(jnp.mean(total * total, axis=1, keepdims=True) + norm_eps)
            unit = total * inv
            c = self.cin[at, :].astype(f32)
            self.xin[at, :] = (self.xin[at, :].astype(f32) + unit * gain).astype(bf16)
            hit = c * unit
            self.gm_grad[...] += fold(hit)
            dy = c * gain
            inner = jnp.mean(hit * gain, axis=1, keepdims=True)
            self.h[at, :] = (inv * (dy - unit * inner)).astype(bf16)

        self.row_groups(one)
        self.store_layer(m).start()
        self.store_h(m, self.low).start()

    def tile_weights(self, t, slot, last):
        for copy in self.load_w(t, slot):
            copy.wait()

        @pl.when(jnp.logical_not(last))
        def _():
            for copy in self.load_w(lax.rem(t + 1, self.tiles), 1 - slot):
                copy.start()

    def add(self, t, at, value):
        @pl.when(t == 0)
        def _():
            self.acc[:, at] = value

        @pl.when(t > 0)
        def _():
            self.acc[:, at] += value

    def forward_gate(self, m, t):
        slot = lax.rem(t, 2)
        self.tile_weights(t, slot, False)

        @pl.when(t >= 2)
        def _():
            for copy in self.store_pre(m, t - 2, slot):
                copy.wait()

        self.gt[slot] = matmul(self.h[...], self.wgt[slot]).astype(bf16)

    def forward_up(self, m, t):
        slot = lax.rem(t, 2)
        up = matmul(self.h[...], self.wut[slot])
        gate = self.gt[slot].astype(f32)
        self.ut[slot] = up.astype(bf16)
        self.it[slot] = (gate * jax.nn.sigmoid(gate) * up).astype(bf16)
        for copy in self.store_pre(m, t, slot):
            copy.start()

    def forward_down(self, m, t):
        slot = lax.rem(t, 2)
        wide = self.acc.shape[1]
        step = math.gcd(wide, 512)
        for k in range(0, wide, step):
            self.add(t, slice(k, k + step), right_t(self.it[slot], self.wdt[slot, k : k + step, :]))

        @pl.when(t == self.tiles - 1)
        def _():
            for back in range(min(2, self.tiles)):
                at = self.tiles - 1 - back
                for copy in self.store_pre(m, at, at % 2):
                    copy.wait()
            self.store_h(m, self.hidden).wait()
            self.finish(m, m > 0)

    def backward_low(self, m, t, last):
        slot = lax.rem(t, 2)
        self.tile_weights(t, slot, last & (t == self.tiles - 1))
        for copy in self.load_pre(m, t, slot):
            copy.wait()

        @pl.when(t < self.tiles - 1)
        def _():
            for copy in self.load_pre(m, t + 1, 1 - slot):
                copy.start()

        @pl.when(t >= 2)
        def _():
            for copy in self.store_low(m, t - 2, slot):
                copy.wait()

        grad = matmul(self.h[...], self.wdt[slot])
        gate = self.gt[slot].astype(f32)
        sig = jax.nn.sigmoid(gate)
        act = grad * sig
        self.jt[slot] = (act * gate).astype(bf16)
        self.it[slot] = (
            act * self.ut[slot].astype(f32) * (1.0 + gate * (1.0 - sig))
        ).astype(bf16)
        for copy in self.store_low(m, t, slot):
            copy.start()

    def backward_add(self, t, second):
        slot = lax.rem(t, 2)
        half = self.acc.shape[1] // 2
        step = math.gcd(half, 512)
        for k in range(second * half, (second + 1) * half, step):
            self.add(
                t,
                slice(k, k + step),
                right_t(self.it[slot], self.wgt[slot, k : k + step, :])
                + right_t(self.jt[slot], self.wut[slot, k : k + step, :]),
            )

    def backward_end(self, m, t):
        @pl.when(t == self.tiles - 1)
        def _():
            for back in range(min(2, self.tiles)):
                at = self.tiles - 1 - back
                for copy in self.store_low(m, at, at % 2):
                    copy.wait()
            self.store_h(m, self.low).wait()
            self.store_layer(m).wait()
            self.finish(m, True)

    def piece(self, m, forward, last, unit):
        t, which = unit // 3, lax.rem(unit, 3)

        def when(ahead, number, body):
            @pl.when((forward if ahead else jnp.logical_not(forward)) & (which == number))
            def _():
                body()

        when(True, 0, lambda: self.forward_gate(m, t))
        when(True, 1, lambda: self.forward_up(m, t))
        when(True, 2, lambda: self.forward_down(m, t))
        when(False, 0, lambda: self.backward_low(m, t, last))
        when(False, 1, lambda: self.backward_add(t, 0))

        def rest():
            self.backward_add(t, 1)
            self.backward_end(m, t)

        when(False, 2, rest)

    def parts_by(self, step):
        return jnp.minimum(PARTS * (step - 1), 3 * self.tiles)

    def load_bigs(self, source):
        return (
            pltpu.make_async_copy(source.at[self.micro(0)], self.xin, self.x_sem),
            pltpu.make_async_copy(source.at[self.micro(1)], self.cin, self.c_sem),
        )

    def load_units(self, source, w, slot):
        return [
            pltpu.make_async_copy(
                source.at[self.micro(m), self.cols(w)], to.at[slot], self.r_sem.at[m, slot]
            )
            for m, to in enumerate((self.gt, self.ut))
        ]

    def start_units(self, w, slot):
        split = 2 * self.tiles

        @pl.when(w < split)
        def _():
            for copy in self.load_units(self.gu, w, slot):
                copy.start()

        @pl.when((w >= split) & (w < 3 * self.tiles))
        def _():
            for copy in self.load_units(self.inner, w - split, slot):
                copy.start()

    def store_grads(self, w, slot):
        return pltpu.make_async_copy(
            self.stage.at[slot], self.grads.at[:, self.cols(w), :], self.g_sem.at[slot]
        )

    def store_down(self, t, slot):
        return pltpu.make_async_copy(
            self.stage.at[slot], self.grads_down.at[:, self.cols(t), :], self.g_sem.at[slot]
        )

    def grad_tile(self, w):
        slot = lax.rem(w, 2)
        split = 2 * self.tiles

        @pl.when((w == 0) | (w == split))
        def _():
            for copy in self.load_bigs(self.hidden):
                copy.wait()

        for copy in self.load_units(self.gu, 0, slot):
            copy.wait()
        self.start_units(w + 1, 1 - slot)

        @pl.when(w >= 2)
        def _():
            self.store_grads(0, slot).wait()

        value = left_t(self.gt[slot], self.xin[...]) + left_t(self.ut[slot], self.cin[...])
        owners, _, wide = self.stage.shape[1:]
        for owner in range(owners):
            self.stage[slot, owner] = value[:, owner * wide : (owner + 1) * wide].astype(bf16)

        @pl.when(w < split)
        def _():
            self.store_grads(w, slot).start()

        @pl.when(w >= split)
        def _():
            self.store_down(w - split, slot).start()

        @pl.when(w == split - 1)
        def _():
            for copy in self.load_bigs(self.low):
                copy.start()

        @pl.when(w == 3 * self.tiles - 1)
        def _():
            self.store_down(0, 1 - slot).wait()
            self.store_down(0, slot).wait()

    def finish(self, m, sent):
        @pl.when(sent)
        def _():
            self.settle(m)

        base = m * self.rows

        def one(at, r):
            self.s[pl.ds(pl.multiple_of(base + r, ROW_STEP), ROW_STEP), :] = self.acc[at, :].astype(bf16)

        self.row_groups(one)
        self.launch(m)

    def job(self, index, step):
        micros = self.micros
        m = lax.rem(index, micros)
        forward = index < micros
        last = index == 2 * micros - 1

        @pl.when(forward & (step == 0))
        def _():
            self.forward_start(m)

        @pl.when(jnp.logical_not(forward) & (step == 0))
        def _():
            self.backward_start(m)

        first, after_last = self.parts_by(step), self.parts_by(step + 1)

        def one(unit, carry):
            self.piece(m, forward, last, unit)
            return carry

        @pl.when(step >= 1)
        def _():
            lax.fori_loop(first, after_last, one, 0)

        done = (first < 3 * self.tiles) & (after_last == 3 * self.tiles)

        @pl.when(done & (index < micros - 1))
        def _():
            self.load_x(index + 1, self.x).start()

        @pl.when(done & (index >= micros - 1) & jnp.logical_not(last))
        def _():
            self.load_x(index + 1 - micros, self.hidden).start()
            self.load_c(index + 1 - micros).start()

        @pl.when(done & last)
        def _():
            for copy in self.load_bigs(self.hidden):
                copy.start()
            self.start_units(0, 0)

    def run(self):
        n, micros = self.chunks, self.micros
        total = 3 * micros * n
        clocks = 1 + -(-3 * self.tiles // PARTS)
        self.begin()

        def clock(k, carry):
            @pl.when(k < total)
            def _():
                self.reduce(lax.rem(k // n, micros), lax.rem(k, n))

            back = k - LAG

            @pl.when((back >= n) & (back < total))
            def _():
                sum_index = back // n
                self.spread(sum_index // micros, lax.rem(sum_index, micros), lax.rem(back, n))

            turn = back - n

            @pl.when((turn >= 0) & (turn < 2 * micros * n))
            def _():
                self.job(turn // n, lax.rem(turn, n))

            turn = turn - 2 * micros * n + n - clocks

            @pl.when((turn >= 0) & (turn < 3 * self.tiles))
            def _():
                self.grad_tile(turn)

            return carry

        grads_at = 2 * micros * n + LAG + clocks
        lax.fori_loop(n, max(total + LAG, grads_at + 3 * self.tiles), clock, 0)
        for m in range(micros):
            self.settle(m)
            self.each_chunk(lambda c: self.store(m, c, self.back).wait())


def mlp_kernel(n, micros, rows, *refs):
    Mlp(n, micros, rows, *refs).run()


def feed_forward(part, x, cot, w, ga, gm, first, micros, owners):
    assert micros == 2
    both, width = x.shape
    hidden = w.shape[1] // 3
    rows = both // micros
    chunks = rows // LINE_ROWS
    dma = pltpu.SemaphoreType.DMA
    hbm = pl.BlockSpec(memory_space=pl.ANY)
    vmem = pl.BlockSpec(memory_space=pltpu.VMEM)
    wide = jax.ShapeDtypeStruct((both, width), bf16)
    unit = jax.ShapeDtypeStruct((both, hidden), bf16)
    two = jax.ShapeDtypeStruct((both, 2 * hidden), bf16)
    return pl.pallas_call(
        functools.partial(mlp_kernel, lax.axis_size("tensor"), micros, rows),
        in_specs=[hbm] * 4 + [vmem] * 2 + [hbm],
        out_specs=[hbm] * 10 + [vmem],
        out_shape=[wide, wide, unit, wide, wide, two, wide, two]
        + [jax.ShapeDtypeStruct((owners, k * hidden, width // owners), bf16) for k in (2, 1)]
        + [jax.ShapeDtypeStruct((8, width), f32)],
        scratch_shapes=[
            pltpu.VMEM((both, width), bf16),
            pltpu.VMEM((both, width), bf16),
            pltpu.VMEM((both, width), bf16),
            pltpu.VMEM((both, width), bf16),
            pltpu.VMEM((rows, width), f32),
            pltpu.VMEM((rows, width), bf16),
            pltpu.VMEM((rows, width), bf16),
            pltpu.VMEM((rows, width), bf16),
            pltpu.VMEM((2, width, TILE), bf16),
            pltpu.VMEM((2, width, TILE), bf16),
            pltpu.VMEM((2, width, TILE), bf16),
            pltpu.VMEM((2, rows, TILE), bf16),
            pltpu.VMEM((2, rows, TILE), bf16),
            pltpu.VMEM((2, rows, TILE), bf16),
            pltpu.VMEM((2, rows, TILE), bf16),
            pltpu.VMEM((2, owners, TILE, width // owners), bf16),
            dma(()),
            dma((micros, chunks)),
            dma((micros, chunks)),
            dma((micros, chunks)),
            dma((micros, chunks)),
            dma((micros, chunks)),
            dma((micros, chunks)),
            dma((3, 2)),
            dma(()),
            dma(()),
            dma(()),
            dma(()),
            dma((4, 2)),
            dma((2, 2)),
            dma((2,)),
        ],
        compiler_params=pltpu.CompilerParams(
            collective_id=1, has_side_effects=True, vmem_limit_bytes=60 << 20
        ),
        cost_estimate=cost(both // 4),
        name="feed_forward",
    )(part, x, cot, w, ga, gm, first)


def attn_scores(meta, i, trunk_rows, q, kt, kp, ko):
    scale = HD ** (-0.5)
    block = meta[i, 0]
    n_par = meta[i, 2]
    n_own = meta[i, 3]
    n_trunk = meta[i, 4]
    st = right_t(q, kt) * scale
    sp = right_t(q, kp) * scale
    so = right_t(q, ko) * scale
    row = lax.broadcasted_iota(jnp.int32, (BLOCK, trunk_rows), 0) + block * BLOCK
    col = lax.broadcasted_iota(jnp.int32, (BLOCK, trunk_rows), 1)
    st = jnp.where((col < n_trunk) & (col <= row), st, masked_score)
    row = lax.broadcasted_iota(jnp.int32, (BLOCK, BLOCK), 0)
    col = lax.broadcasted_iota(jnp.int32, (BLOCK, BLOCK), 1)
    sp = jnp.where(col < n_par, sp, masked_score)
    so = jnp.where((col < n_own) & (col <= row), so, masked_score)
    return st, sp, so


def attn_fwd_kernel(trunk_rows, meta, q, trunk, par, own, out, lse):
    i = pl.program_id(1)
    st, sp, so = attn_scores(meta, i, trunk_rows, q[...], trunk[0], par[0], own[0])
    top = jnp.maximum(
        jnp.max(st, axis=1, keepdims=True),
        jnp.maximum(jnp.max(sp, axis=1, keepdims=True), jnp.max(so, axis=1, keepdims=True)),
    )
    et, ep, eo = jnp.exp(st - top), jnp.exp(sp - top), jnp.exp(so - top)
    total = (
        jnp.sum(et, axis=1, keepdims=True)
        + jnp.sum(ep, axis=1, keepdims=True)
        + jnp.sum(eo, axis=1, keepdims=True)
    )
    acc = matmul(et.astype(bf16), trunk[1])
    acc += matmul(ep.astype(bf16), par[1])
    acc += matmul(eo.astype(bf16), own[1])
    out[...] = (acc / total).astype(bf16)
    lse[...] = jnp.broadcast_to(top + jnp.log(total), (BLOCK, HD))


def attn_bwd_kernel(
    trunk_rows, n_q, meta, q, do, lse, trunk, par, own, dq, d_own, d_src, acc,
):
    i = pl.program_id(1)

    @pl.when(i == 0)
    def _():
        acc[...] = jnp.zeros_like(acc)

    scale = HD ** (-0.5)
    qv, dov = q[...], do[...]
    scores = attn_scores(meta, i, trunk_rows, qv, trunk[0], par[0], own[0])
    top = lse[:, 0:1]
    probs = [jnp.exp(s - top) for s in scores]
    grads = [right_t(dov, v[1]) for v in (trunk, par, own)]
    inner = sum(jnp.sum(p * g, axis=1, keepdims=True) for p, g in zip(probs, grads))
    low = [(p * (g - inner)).astype(bf16) for p, g in zip(probs, grads)]
    probs = [p.astype(bf16) for p in probs]
    dq[...] = scale * (
        matmul(low[0], trunk[0]) + matmul(low[1], par[0]) + matmul(low[2], own[0])
    )
    d_own[0] = scale * left_t(low[2], qv)
    d_own[1] = left_t(probs[2], dov)
    acc[0, :trunk_rows] += left_t(low[0], qv)
    acc[1, :trunk_rows] += left_t(probs[0], dov)
    at = pl.ds(pl.multiple_of(trunk_rows + meta[i, 1] * BLOCK, BLOCK), BLOCK)
    acc[0, at] += left_t(low[1], qv)
    acc[1, at] += left_t(probs[1], dov)

    @pl.when(i == n_q - 1)
    def _():
        d_src[0] = (scale * acc[0]).astype(bf16)
        d_src[1] = acc[1].astype(bf16)


def kv_specs(trunk_rows):
    skip = trunk_rows // BLOCK
    trunk = pl.BlockSpec((2, trunk_rows, HD), lambda h, i, meta: (0, 0, h))
    par = pl.BlockSpec((2, BLOCK, HD), lambda h, i, meta: (0, skip + meta[i, 1], h))
    own = pl.BlockSpec((2, BLOCK, HD), lambda h, i, meta: (0, i, h))
    return [trunk, par, own]


def attend_forward(meta, q, sources, own_kv, trunk_rows):
    rows, width = q.shape
    own = pl.BlockSpec((BLOCK, HD), lambda h, i, meta: (i, h))
    return pl.pallas_call(
        functools.partial(attn_fwd_kernel, trunk_rows),
        grid_spec=pltpu.PrefetchScalarGridSpec(
            num_scalar_prefetch=1,
            grid=(width // HD, rows // BLOCK),
            in_specs=[own] + kv_specs(trunk_rows),
            out_specs=[own, own],
        ),
        out_shape=[
            jax.ShapeDtypeStruct((rows, width), bf16),
            jax.ShapeDtypeStruct((rows, width), f32),
        ],
        compiler_params=pltpu.CompilerParams(vmem_limit_bytes=32 << 20),
        cost_estimate=cost(12),
        name="attend_forward",
    )(meta, q, sources, sources, own_kv)


def attend_backward(meta, q, do, lse, sources, own_kv, trunk_rows):
    rows, width = q.shape
    own = pl.BlockSpec((BLOCK, HD), lambda h, i, meta: (i, h))
    own_two = pl.BlockSpec((2, BLOCK, HD), lambda h, i, meta: (0, i, h))
    all_rows = sources.shape[1]
    n_q = rows // BLOCK
    return pl.pallas_call(
        functools.partial(attn_bwd_kernel, trunk_rows, n_q),
        grid_spec=pltpu.PrefetchScalarGridSpec(
            num_scalar_prefetch=1,
            grid=(width // HD, n_q),
            in_specs=[own, own, own] + kv_specs(trunk_rows),
            out_specs=[
                own,
                own_two,
                pl.BlockSpec((2, all_rows, HD), lambda h, i, meta: (0, 0, h)),
            ],
            scratch_shapes=[pltpu.VMEM((2, all_rows, HD), f32)],
        ),
        out_shape=[
            jax.ShapeDtypeStruct((rows, width), f32),
            jax.ShapeDtypeStruct((2, rows, width), f32),
            jax.ShapeDtypeStruct(sources.shape, bf16),
        ],
        compiler_params=pltpu.CompilerParams(vmem_limit_bytes=40 << 20),
        cost_estimate=cost(22),
        name="attend_backward",
    )(meta, q, do, lse, sources, sources, own_kv)


def group_perm(n, k):
    half = n // 2
    return [(i, i // half * half + (i % half + k) % half) for i in range(n)]


def fetch_sources(block, hold):
    n = lax.axis_size("seq")
    half = n // 2
    place = lax.axis_index("seq")
    spot = lax.rem(place, half)
    got = lax.ppermute(block, "seq", [(i, i + half) for i in range(half)])
    got = after(got, *hold)
    mine = jnp.where(place < half, block, got)
    parts = [mine] + [lax.ppermute(mine, "seq", group_perm(n, k)) for k in range(1, half)]
    out = []
    for source in range(half):
        pick = parts[0]
        for k in range(1, half):
            pick = jnp.where(lax.rem(spot - k + half, half) == source, parts[k], pick)
        out.append(pick)
    return jnp.concatenate(out, axis=1), got


def sum_over_group(grads):
    n = lax.axis_size("seq")
    half = n // 2
    spot = lax.rem(lax.axis_index("seq"), half)
    rows = grads.shape[1] // half
    pieces = [grads[:, s * rows : (s + 1) * rows] for s in range(half)]

    def piece(index):
        pick = pieces[0]
        for s in range(1, half):
            pick = jnp.where(index == s, pieces[s], pick)
        return pick

    total = piece(spot).astype(f32)
    for k in range(1, half):
        sent = piece(lax.rem(spot + k, half))
        total += lax.ppermute(sent, "seq", group_perm(n, k)).astype(f32)
    return total.astype(bf16)


def return_to_sources(total):
    n = lax.axis_size("seq")
    half = n // 2
    return lax.ppermute(total, "seq", [(i + half, i) for i in range(half)])


def gather_rows(item):
    return lax.all_gather(item, ("dp", "seq"), axis=0, tiled=True)


def scatter_low(item):
    return lax.psum_scatter(item, ("dp", "seq"), scatter_dimension=0, tiled=True)


def scatter_rows(item):
    return scatter_low(item).astype(f32)


def block_meta(parents, lengths, rows, n_blocks):
    seg_count = parents.shape[0]
    branches = (seg_count - 1) // 3
    trunk_blocks = n_blocks - 3 * branches
    blocks = lax.axis_index("seq") * (rows // BLOCK) + jnp.arange(rows // BLOCK, dtype=jnp.int32)
    seg = jnp.maximum(blocks - trunk_blocks + 1, 0)
    hit = seg[:, None] == jnp.arange(seg_count, dtype=jnp.int32)[None, :]
    parent = jnp.sum(jnp.where(hit, parents[None, :], 0), axis=1)
    own_len = jnp.sum(jnp.where(hit, lengths[None, :], 0), axis=1)
    hit = parent[:, None] == jnp.arange(seg_count, dtype=jnp.int32)[None, :]
    par_len = jnp.sum(jnp.where(hit, lengths[None, :], 0), axis=1)
    return jnp.stack(
        [
            blocks,
            jnp.maximum(parent - 1, 0),
            jnp.where(parent > 0, par_len, 0),
            jnp.where(blocks >= trunk_blocks, own_len, 0),
            jnp.broadcast_to(lengths[0], blocks.shape),
        ],
        axis=1,
    ).astype(jnp.int32)


def per_device(
    tokens, cotangent, w_query, w_key, w_value, w_out, w_gate, w_up, w_down,
    query_gain, key_gain, attn_gain, mlp_gain, parent_of, seg_length,
):
    micros, _, rows, width = tokens.shape
    n_blocks = rows // BLOCK * lax.axis_size("seq")
    heads = w_query.shape[1] // HD
    full_width = heads * HD * lax.axis_size("tensor")
    branches = (parent_of.shape[2] - 1) // 3
    trunk_rows = (n_blocks - 3 * branches) * BLOCK

    cols = w_query.shape[1]
    owners = lax.axis_size("dp") * lax.axis_size("seq")
    gains = [query_gain.reshape(-1), key_gain.reshape(-1), attn_gain, mlp_gain]
    gains = jnp.concatenate(gains)
    count = gains.shape[0]
    lines = -(-count // LANES)
    gains = jnp.pad(gains, (0, lines * LANES - count)).reshape(lines, LANES)
    gains = jnp.pad(gains, ((0, width // owners - lines), (0, 0)))
    w_attn = gather_shards(
        jnp.concatenate([w_query, w_key, w_value, w_out.T, gains], axis=1), 9
    )
    w_own = jnp.concatenate([w_gate, w_up, w_down.T], axis=1)
    gains = w_attn[:, 4 * cols :].reshape(owners, -1, LANES)[:, :lines]
    gains = gains.reshape(owners, lines * LANES)
    own = query_gain.size

    def head_gain(block):
        block = block.reshape(owners, heads, HD // owners)
        return jnp.swapaxes(block, 0, 1).reshape(-1).astype(f32)

    q_gain = head_gain(gains[:, :own])
    k_gain = head_gain(gains[:, own : 2 * own])
    a_gain = gains[:, 2 * own : 2 * own + attn_gain.size].reshape(-1).astype(f32)
    m_gain = gains[:, 2 * own + attn_gain.size : count].reshape(-1).astype(f32)
    wo_t = w_attn[:, 3 * cols : 4 * cols]
    q_gain, k_gain, a_gain = q_gain[None], k_gain[None], a_gain[None]

    x = tokens.reshape(micros * rows, width)
    cot = cotangent.reshape(micros * rows, width)
    q_lows, kv_lows, units, squares = zip(
        *(qkv(x, w_attn, q_gain, k_gain, m, rows, 6 + m) for m in range(micros))
    )
    sources, metas, attn_lows, lses, parts, first = [], [], [], [], [], None
    for m in range(micros):
        block = kv_lows[m] if m == 0 else after(kv_lows[m], attn_lows[0])
        source, got = fetch_sources(block, (q_lows[1], w_own) if m == 0 else (first,))
        sources.append(source)
        metas.append(block_meta(parent_of[m, 0], seg_length[m, 0], rows, n_blocks))
        attn_low, lse = attend_forward(metas[m], q_lows[m], sources[m], kv_lows[m], trunk_rows)
        attn_lows.append(attn_low)
        lses.append(lse)
        parts.append(right_t(attn_low, wo_t).astype(bf16))
        if m == 0:
            first = line_sum(parts[0], 0)
            w_mlp = gather_rows(after(w_own, got))
    proj, _, _, layer, _, _, back, _, gu_grads, down_grads, gm_grad = feed_forward(
        parts[1], x, cot, w_mlp, a_gain, m_gain[None], first,
        micros, owners,
    )
    hidden = w_gate.shape[1]
    g_attn, qk_grad, ga_grads, layer_out = None, None, [], None
    wide = width // owners
    proj_lows, dqs, d_owns, sums = [], [], [], []
    for m in range(micros):
        proj_low, attn_grad, grad, layer_out = proj_backward(
            cot, back, first if m == 0 else proj, after(a_gain, sums[0]) if m else a_gain, w_attn,
            layer, layer_out, cols, m, rows, m
        )
        ga_grads.append(grad)
        dq, d_own, d_src = attend_backward(
            metas[m], q_lows[m], attn_grad, lses[m], sources[m], kv_lows[m], trunk_rows
        )
        sums.append(sum_over_group(d_src))
        proj_lows.append(proj_low)
        dqs.append(dq)
        d_owns.append(d_own)

    lasts = []
    for m in range(micros):
        got = return_to_sources(sums[m])
        if m > 0:
            input_grad = add_up(cot, back, lasts[0], 0, None)
            got = after(got, input_grad)
        else:
            got = after(got, dqs[-1])
            g_down = scatter_low(down_grads.reshape(-1, wide))
            gu_grads = after(gu_grads.reshape(-1, wide), got, g_down)
            gu_grads = scatter_low(gu_grads)
        extra = [*proj_lows, *attn_lows] if m == 0 else [qk_grad, *ga_grads, gm_grad]
        _, last, qk_grad, g_attn = last_sum(
            dqs[m], d_owns[m], sums[m], got, units[m], squares[m], q_gain, k_gain,
            x.reshape(micros, rows, width), extra, g_attn, w_attn, owners, 5 if m else 3,
        )
        lasts.append(line_sum(last, 4) if m else last)
    g_attn = scatter_low(after(g_attn, gu_grads))
    g_attn = after(g_attn, qk_grad).astype(f32)

    lines = g_attn[:, 4 * cols :]
    share = HD // owners
    place = lax.axis_index("dp") * lax.axis_size("seq") + lax.axis_index("seq")
    head_lines = lax.dynamic_slice_in_dim(lines[: 2 * heads], place * share, share, 1)
    own_lines = lines[2 * heads : 2 * heads + 2 * attn_gain.size // LANES].reshape(2, -1)
    input_grad = add_up(cot, back, lasts[1], 1, input_grad)
    return (
        layer_out.reshape(tokens.shape),
        input_grad.reshape(tokens.shape),
        g_attn[:, :cols],
        g_attn[:, cols : 2 * cols],
        g_attn[:, 2 * cols : 3 * cols],
        g_attn[:, 3 * cols : 4 * cols].T,
        gu_grads[:hidden].astype(f32).T,
        gu_grads[hidden:].astype(f32).T,
        g_down.astype(f32),
        head_lines[:heads],
        head_lines[heads:],
        own_lines[0],
        own_lines[1],
    )


def solution(mesh):
    rows = P(None, "dp", "seq", None)
    by_row = P(("dp", "seq"), "tensor")
    by_col = P("tensor", ("dp", "seq"))
    gain = P(("dp", "seq"))
    tree = P(None, "dp", None)
    weights = (by_row, by_row, by_row, by_col, by_row, by_row, by_col, by_col, by_col, gain, gain)
    return jax.shard_map(
        per_device,
        mesh=mesh,
        in_specs=(rows, rows) + weights + (tree, tree),
        out_specs=(rows, rows) + weights,
        check_vma=False,
    )
```

```python
import functools
import math

import jax
import jax.numpy as jnp
from jax import lax
from jax.experimental import pallas as pl
from jax.experimental.pallas import tpu as pltpu
from jax.sharding import PartitionSpec as P

HD = 128
BLOCK = 256

norm_eps = 1e-06
masked_score = -1e30
f32 = jnp.float32
bf16 = jnp.bfloat16


def matmul(left, right):
    return jnp.dot(left, right, preferred_element_type=f32)


def left_t(left, right):
    return lax.dot_general(left, right, (((0,), (0,)), ((), ())), preferred_element_type=f32)


def right_t(left, right):
    return lax.dot_general(left, right, (((1,), (1,)), ((), ())), preferred_element_type=f32)


MESH = pl.DeviceIdType.MESH


def cost(us):
    return pl.CostEstimate(flops=int(us * 1.1e9), bytes_accessed=0, transcendentals=0)


def fold(rows):
    total = rows[0:8]
    for j in range(8, rows.shape[0], 8):
        total += rows[j : j + 8]
    return total


def after(value, *earlier):
    hbm = pl.BlockSpec(memory_space=pl.ANY)
    return pl.pallas_call(
        lambda *refs: None,
        in_specs=[hbm] * (1 + len(earlier)),
        out_specs=hbm,
        out_shape=jax.ShapeDtypeStruct(value.shape, value.dtype),
        input_output_aliases={0: 0},
        name="after",
    )(value, *earlier)


class Line:
    def __init__(self, n, chunks, rows, part, out, s, land, res, sems):
        self.chunks, self.rows = chunks, rows
        self.part, self.out, self.s, self.land, self.res = part, out, s, land, res
        (
            self.load_sem,
            self.in_send,
            self.in_recv,
            self.out_send,
            self.out_recv,
            self.store_sem,
        ) = sems
        i = lax.axis_index("tensor")
        half = n // 2
        left = i < half
        self.inward = jnp.where(left, i + 1, i - 1)
        self.outward = jnp.where(left, i - 1, i + 1)
        self.relay = (i > 0) & (i < n - 1)
        self.mid = (i == half - 1) | (i == half)
        self.slot = jnp.where(self.mid, 1, 0)

    def at(self, c):
        return pl.ds(pl.multiple_of(c * self.rows, self.rows), self.rows)

    def load(self):
        return pltpu.make_async_copy(self.part, self.s, self.load_sem)

    def inward_copy(self, c, slot):
        return pltpu.make_async_remote_copy(
            src_ref=self.s.at[self.at(c)],
            dst_ref=self.land.at[slot, self.at(c)],
            send_sem=self.in_send.at[c],
            recv_sem=self.in_recv.at[slot, c],
            device_id={"tensor": self.inward},
            device_id_type=MESH,
        )

    def outward_copy(self, c):
        return pltpu.make_async_remote_copy(
            src_ref=self.res.at[self.at(c)],
            dst_ref=self.res.at[self.at(c)],
            send_sem=self.out_send.at[c],
            recv_sem=self.out_recv.at[c],
            device_id={"tensor": self.outward},
            device_id_type=MESH,
        )

    def store(self, c):
        return pltpu.make_async_copy(
            self.res.at[self.at(c)], self.out.at[self.at(c)], self.store_sem.at[c]
        )

    def begin(self):
        self.load().start()
        barrier = pltpu.get_barrier_semaphore()
        pl.semaphore_signal(
            barrier, inc=1, device_id={"tensor": self.inward}, device_id_type=MESH
        )

        @pl.when(self.relay)
        def _():
            pl.semaphore_signal(
                barrier, inc=1, device_id={"tensor": self.outward}, device_id_type=MESH
            )

        pl.semaphore_wait(barrier, jnp.where(self.relay, 2, 1))
        self.load().wait()
        self.launch(0, self.chunks)

    def launch(self, first, last):
        @pl.when(~self.relay)
        def _():
            def one(c, carry):
                self.inward_copy(c, self.slot).start()
                return carry

            lax.fori_loop(first, last, one, 0)

    def stream(self, job=None):
        def step(c, carry):
            if job is not None:
                job(c)
            self.reduce(c)

            @pl.when(c > 0)
            def _():
                self.spread(c - 1)

            return carry

        lax.fori_loop(0, self.chunks, step, 0)
        self.spread(self.chunks - 1)
        self.end()

    def reduce(self, c):
        @pl.when(self.relay)
        def _():
            self.inward_copy(c, 0).wait_recv()
            a = self.at(c)
            self.s[a, :] = (self.s[a, :].astype(f32) + self.land[0, a, :].astype(f32)).astype(bf16)
            self.inward_copy(c, self.slot).start()

    def spread(self, c):
        a = self.at(c)

        @pl.when(self.mid)
        def _():
            self.inward_copy(c, 1).wait_recv()
            self.res[a, :] = (
                self.s[a, :].astype(f32) + self.land[1, a, :].astype(f32)
            ).astype(bf16)

        @pl.when(~self.mid)
        def _():
            self.outward_copy(c).wait_recv()

        @pl.when(self.relay)
        def _():
            self.outward_copy(c).start()

        self.store(c).start()

    def end(self):
        def one(c, carry):
            self.inward_copy(c, self.slot).wait_send()

            @pl.when(self.relay)
            def _():
                self.outward_copy(c).wait_send()

            self.store(c).wait()
            return carry

        lax.fori_loop(0, self.chunks, one, 0)


def line_scratch(rows, width, chunks):
    dma = pltpu.SemaphoreType.DMA
    return [
        pltpu.VMEM((rows, width), bf16),
        pltpu.VMEM((2, rows, width), bf16),
        pltpu.VMEM((rows, width), bf16),
        dma(()),
        dma((chunks,)),
        dma((2, chunks)),
        dma((chunks,)),
        dma((chunks,)),
        dma((chunks,)),
    ]


def line_kernel(n, chunks, part, out, s, land, res, *sems):
    line = Line(n, chunks, part.shape[0] // chunks, part, out, s, land, res, sems)
    line.begin()
    line.stream()


def line_sum(part, collective_id):
    rows, width = part.shape
    n = lax.axis_size("tensor")
    chunks = rows // 48
    return pl.pallas_call(
        functools.partial(line_kernel, n, chunks),
        in_specs=[pl.BlockSpec(memory_space=pl.ANY)],
        out_specs=pl.BlockSpec(memory_space=pl.ANY),
        out_shape=jax.ShapeDtypeStruct(part.shape, bf16),
        scratch_shapes=line_scratch(rows, width, chunks),
        compiler_params=pltpu.CompilerParams(
            collective_id=collective_id, has_side_effects=True, vmem_limit_bytes=60 << 20
        ),
        cost_estimate=cost(rows // 9),
        name="line_sum",
    )(part)


def gather_kernel(dps, seqs, own, out, own_sem, recv, send):
    chips = seqs // 2
    dp, seq = lax.axis_index("dp"), lax.axis_index("seq")
    chip, core = seq // 2, lax.rem(seq, 2)
    rows = own.shape[0]
    half = rows // 2
    across = [lax.rem(dp + a, dps) for a in range(1, dps)]
    along = [lax.rem(chip + b, chips) for b in range(1, chips)]
    here = lax.axis_index("tensor")

    def device(d, c, k):
        return {"dp": d, "seq": 2 * c + k, "tensor": here}

    def owner(d, c, k):
        return d * seqs + 2 * c + k

    other = device(dp, chip, 1 - core)
    mine = owner(dp, chip, core)
    by_dp = [device(d, chip, core) for d in across]
    by_chip = [device(dp, c, core) for c in along]
    sends = []

    def copy(index, part, target, number, source=None):
        at = pl.ds(pl.multiple_of(index * rows + part * half, half), half)
        return pltpu.make_async_remote_copy(
            src_ref=out.at[at] if source is None else source,
            dst_ref=out.at[at],
            send_sem=send.at[number],
            recv_sem=recv.at[index, part],
            device_id=target,
            device_id_type=MESH,
        )

    def push(index, part, target):
        source = own.at[pl.ds(part * half, half)] if index is mine else None
        item = copy(index, part, target, len(sends), source)
        item.start()
        sends.append(item)

    def arrived(index, part):
        copy(index, part, other, 0).wait_recv()

    at = pl.ds(pl.multiple_of(mine * rows, rows), rows)
    place = pltpu.make_async_copy(own, out.at[at], own_sem)
    place.start()
    barrier = pltpu.get_barrier_semaphore()
    neighbours = by_dp + by_chip + [other]
    for target in neighbours:
        pl.semaphore_signal(barrier, inc=1, device_id=target, device_id_type=MESH)
    pl.semaphore_wait(barrier, len(neighbours))
    for target in by_dp:
        push(mine, 0, target)
    for target in by_chip:
        push(mine, 1, target)
    for part in range(2):
        push(mine, part, other)
    for target in by_chip:
        push(mine, 0, target)
    for target in by_dp:
        push(mine, 1, target)
    for d in across:
        index = owner(d, chip, core)
        arrived(index, 0)
        for target in by_chip + [other]:
            push(index, 0, target)
    for c in along:
        index = owner(dp, c, core)
        arrived(index, 1)
        for target in by_dp + [other]:
            push(index, 1, target)
    late = [(owner(dp, c, core), 0) for c in along] + [(owner(d, chip, core), 1) for d in across]
    late += [(owner(d, c, core), part) for d in across for c in along for part in range(2)]
    for index, part in late:
        arrived(index, part)
        push(index, part, other)
    for d in [dp] + across:
        for c in [chip] + along:
            for part in range(2):
                arrived(owner(d, c, 1 - core), part)
    place.wait()
    for item in sends:
        item.wait_send()


def gather_shards(own, collective_id):
    dps, seqs = lax.axis_size("dp"), lax.axis_size("seq")
    chips = seqs // 2
    rows, cols = own.shape
    dma = pltpu.SemaphoreType.DMA
    hbm = pl.BlockSpec(memory_space=pl.ANY)
    sends = (dps - 1) * (1 + chips) + (chips - 1) * (1 + dps) + 2 * dps * chips
    return pl.pallas_call(
        functools.partial(gather_kernel, dps, seqs),
        in_specs=[hbm],
        out_specs=hbm,
        out_shape=jax.ShapeDtypeStruct((dps * seqs * rows, cols), own.dtype),
        scratch_shapes=[dma(()), dma((dps * seqs, 2)), dma((sends,))],
        compiler_params=pltpu.CompilerParams(
            collective_id=collective_id, has_side_effects=True, vmem_limit_bytes=60 << 20
        ),
        cost_estimate=cost(40),
        name="gather_shards",
    )(own)


LANES = 128


def diagonal():
    shape = (LANES, LANES)
    return lax.broadcasted_iota(jnp.int32, shape, 0) == lax.broadcasted_iota(jnp.int32, shape, 1)


def to_line(column):
    return jnp.sum(jnp.where(diagonal(), column, 0.0), axis=0, keepdims=True)


def to_column(line):
    return jnp.sum(jnp.where(diagonal(), line, 0.0), axis=1, keepdims=True)


class Exchange:
    def __init__(self, n, lines, land, send, recv):
        self.n, self.lines, self.land, self.send, self.recv = n, lines, land, send, recv
        self.me = lax.axis_index("tensor")
        self.peers = [lax.rem(self.me + d, n) for d in range(1, n)]

    def greet(self):
        barrier = pltpu.get_barrier_semaphore()
        for peer in self.peers:
            pl.semaphore_signal(barrier, inc=1, device_id={"tensor": peer}, device_id_type=MESH)

    def met(self):
        pl.semaphore_wait(pltpu.get_barrier_semaphore(), self.n - 1)

    def copy(self, d, peer, slot):
        return pltpu.make_async_remote_copy(
            src_ref=self.lines,
            dst_ref=self.land.at[slot],
            send_sem=self.send.at[d],
            recv_sem=self.recv.at[slot],
            device_id={"tensor": peer},
            device_id_type=MESH,
        )

    def total(self):
        self.land[self.me] = self.lines[...]
        for d, peer in enumerate(self.peers):
            self.copy(d, peer, self.me).start()
        for d, peer in enumerate(self.peers):
            self.copy(d, peer, peer).wait_recv()
        total = self.land[0]
        for place in range(1, self.n):
            total += self.land[place]
        for d, peer in enumerate(self.peers):
            self.copy(d, peer, self.me).wait_send()
        return total


def exchange_scratch(n, lines):
    dma = pltpu.SemaphoreType.DMA
    return [
        pltpu.VMEM((2 * lines, LANES), f32),
        pltpu.VMEM((n, 2 * lines, LANES), f32),
        dma((n - 1,)),
        dma((n,)),
    ]


def line_count(rows):
    return -(-rows // LANES // 8) * 8


def qkv_kernel(n, rows, cols, x, w, qg, kg, q_low, kv_low, units, squares, raw, *net):
    swap = Exchange(n, *net)
    swap.greet()
    lines = swap.lines.shape[0] // 2
    swap.lines[...] = jnp.zeros_like(swap.lines)
    step = math.gcd(rows, 384)
    for r in range(0, rows, step):
        at = slice(r, r + step)
        for k in range(2):
            value = matmul(x[at, :], w[:, k * cols : (k + 1) * cols])
            raw[k, at, :] = value
            square = jnp.sum(value * value, axis=1, keepdims=True)
            for j in range(0, step, LANES):
                spot = k * lines + (r + j) // LANES
                swap.lines[spot : spot + 1, :] = to_line(square[j : j + LANES])
    swap.met()
    for r in range(0, rows, step):
        at = slice(r, r + step)
        kv_low[1, at, :] = matmul(x[at, :], w[:, 2 * cols : 3 * cols]).astype(bf16)
    total = swap.total()
    squares[...] = total
    width = n * cols
    for r in range(0, rows, LANES):
        at = slice(r, r + LANES)
        for k, gain in enumerate((qg, kg)):
            spot = k * lines + r // LANES
            square = to_column(total[spot : spot + 1, :])
            unit = raw[k, at, :] * lax.rsqrt(square / width + norm_eps)
            units[k, at, :] = unit
            low = (unit * gain[...]).astype(bf16)
            if k == 0:
                q_low[at, :] = low
            else:
                kv_low[0, at, :] = low


def qkv(x, w, qg, kg, m, rows, collective_id):
    n = lax.axis_size("tensor")
    width = x.shape[1]
    cols = qg.shape[1]
    lines = line_count(rows)
    vmem = pl.BlockSpec(memory_space=pltpu.VMEM)
    return pl.pallas_call(
        functools.partial(qkv_kernel, n, rows, cols),
        grid=(1,),
        in_specs=[
            pl.BlockSpec((rows, width), lambda i: (m, 0)),
            pl.BlockSpec((width, 3 * cols), lambda i: (0, 0)),
            vmem,
            vmem,
        ],
        out_specs=[vmem] * 4,
        out_shape=[
            jax.ShapeDtypeStruct((rows, cols), bf16),
            jax.ShapeDtypeStruct((2, rows, cols), bf16),
            jax.ShapeDtypeStruct((2, rows, cols), f32),
            jax.ShapeDtypeStruct((2 * lines, LANES), f32),
        ],
        scratch_shapes=[pltpu.VMEM((2, rows, cols), f32)] + exchange_scratch(n, lines),
        compiler_params=pltpu.CompilerParams(
            collective_id=collective_id, has_side_effects=True, vmem_limit_bytes=60 << 20
        ),
        cost_estimate=cost(15),
        name="qkv",
    )(x, w, qg, kg)


def proj_kernel(cot, back, proj, gain, wo_t, layer, *refs):
    low, grad, gain_grad, layer_out = refs[-4:]
    layer_out[...] = layer[...]

    @pl.when(pl.program_id(0) == 0)
    def _():
        gain_grad[...] = jnp.zeros_like(gain_grad)

    step = ROW_STEP

    def one(r, carry):
        at = pl.ds(pl.multiple_of(r * step, step), step)
        value = proj[at, :].astype(f32)
        inv = lax.rsqrt(jnp.mean(value * value, axis=1, keepdims=True) + norm_eps)
        unit = value * inv
        hidden = cot[at, :].astype(f32) + back[at, :].astype(f32)
        hit = hidden * unit
        gain_grad[...] += fold(hit)
        inner = jnp.mean(hit * gain[...], axis=1, keepdims=True)
        low[at, :] = (inv * (hidden * gain[...] - unit * inner)).astype(bf16)
        return carry

    lax.fori_loop(0, low.shape[0] // step, one, 0)
    grad[...] = matmul(low[...], wo_t[...]).astype(bf16)


def proj_backward(cot, back, proj, gain, w, layer, layer_out, cols, m, rows, proj_m):
    width = cot.shape[1]
    step = BLOCK
    blocks = rows // step

    earlier = [] if layer_out is None else [layer_out]

    def whole(first):
        return pl.BlockSpec((step, width), lambda i: (first * blocks + i, 0))

    return pl.pallas_call(
        proj_kernel,
        grid=(blocks,),
        in_specs=[
            whole(m),
            whole(m),
            whole(proj_m),
            pl.BlockSpec((1, width), lambda i: (0, 0)),
            pl.BlockSpec((width, cols), lambda i: (0, 3)),
            whole(m),
        ]
        + [pl.BlockSpec(memory_space=pl.ANY)] * len(earlier),
        out_specs=[
            whole(0),
            pl.BlockSpec((step, cols), lambda i: (i, 0)),
            pl.BlockSpec((8, width), lambda i: (0, 0)),
            whole(m),
        ],
        out_shape=[
            jax.ShapeDtypeStruct((rows, width), bf16),
            jax.ShapeDtypeStruct((rows, cols), bf16),
            jax.ShapeDtypeStruct((8, width), f32),
            jax.ShapeDtypeStruct(cot.shape, bf16),
        ],
        input_output_aliases={6: 3} if earlier else {},
        compiler_params=pltpu.CompilerParams(vmem_limit_bytes=40 << 20),
        cost_estimate=cost(10),
        name="proj_backward",
    )(cot, back, proj, gain, w, layer, *earlier)


def add_kernel(cot, back, last, *refs):
    refs[-1][...] = cot[...].astype(f32) + back[...].astype(f32) + last[...].astype(f32)


def add_up(cot, back, last, m, out):
    rows, width = last.shape
    step = math.gcd(rows, 128)
    blocks = rows // step
    earlier = [] if out is None else [out]
    whole = pl.BlockSpec((step, width), lambda i: (m * blocks + i, 0))
    return pl.pallas_call(
        add_kernel,
        grid=(blocks,),
        in_specs=[whole, whole, pl.BlockSpec((step, width), lambda i: (i, 0))]
        + [pl.BlockSpec(memory_space=pl.ANY)] * len(earlier),
        out_specs=whole,
        out_shape=jax.ShapeDtypeStruct(cot.shape, f32),
        input_output_aliases={3: 0} if earlier else {},
        compiler_params=pltpu.CompilerParams(vmem_limit_bytes=60 << 20),
        cost_estimate=cost(6),
        name="add_up",
    )(cot, back, last, *earlier)


class Grads:
    def __init__(self, to, stage, sem):
        self.to, self.stage, self.sem = to, stage, sem
        self.wide = stage.shape[1]

    def at(self, owner):
        return pl.ds(pl.multiple_of(owner * self.wide, self.wide), self.wide)

    def store(self, owner, slot):
        width = self.stage.shape[2]
        return pltpu.make_async_copy(
            self.stage.at[slot], self.to.at[self.at(owner), pl.ds(0, width)], self.sem.at[slot]
        )


def last_kernel(
    n, rows, cols, sources, stream, dq, own, mine, got, units, squares, qg, kg, x, proj, attn,
    before, others, w, low, out, gain_grad, g_attn, *scratch,
):
    swap = Exchange(n, *scratch[:4])
    swap.greet()
    xin, x_sem, stage, g_sem = scratch[4:8]
    load_x = pltpu.make_async_copy(x.at[0 if stream else 1], xin, x_sem)
    load_x.start()
    grads = Grads(g_attn, stage, g_sem)
    owners = xin.shape[1] // grads.wide
    if stream:
        s, land, res, pin, p_sem = scratch[8:13]
        loads = [pltpu.make_async_copy(proj[m], pin.at[m], p_sem.at[m]) for m in range(2)]
        for load in loads:
            load.start()
    else:
        s = out
        had, b_sem, gains, n_sem = scratch[8:12]

        def load_before(owner, slot):
            return pltpu.make_async_copy(
                before.at[grads.at(owner), pl.ds(0, 3 * cols)], had.at[slot], b_sem.at[slot]
            )

        load_before(0, 0).start()
    lines = swap.lines.shape[0] // 2
    swap.lines[...] = jnp.zeros_like(swap.lines)
    gain_grad[...] = jnp.zeros_like(gain_grad)
    scale = jnp.where(sources, 1.0, 0.0).astype(f32)
    width = n * cols

    def gathered(k, at):
        both = mine[k, at, :].astype(f32) + got[k, at, :].astype(f32)
        return own[k, at, :] + scale * both

    for r in range(0, rows, LANES):
        at = slice(r, r + LANES)
        for k, gain in enumerate((qg, kg)):
            grad = dq[at, :] if k == 0 else gathered(0, at)
            hit = grad * units[k, at, :]
            gain_grad[8 * k : 8 * k + 8, :] += fold(hit)
            spot = k * lines + r // LANES
            swap.lines[spot : spot + 1, :] = to_line(
                jnp.sum(hit * gain[...], axis=1, keepdims=True)
            )
    swap.met()
    total = swap.total()
    for r in range(0, rows, LANES):
        at = slice(r, r + LANES)
        for k, gain in enumerate((qg, kg)):
            spot = k * lines + r // LANES
            inner = to_column(total[spot : spot + 1, :]) / width
            inv = lax.rsqrt(to_column(squares[spot : spot + 1, :]) / width + norm_eps)
            grad = dq[at, :] if k == 0 else gathered(0, at)
            value = inv * (grad * gain[...] - units[k, at, :] * inner)
            low[at, k * cols : (k + 1) * cols] = value.astype(bf16)
        low[at, 2 * cols :] = gathered(1, at).astype(bf16)
    if stream:
        line = Line(n, out.shape[0] // 48, 48, None, out, s, land, res, scratch[13:])
    step = math.gcd(rows, 384)
    piece = math.gcd(s.shape[1], 512)
    for r in range(0, rows, step):
        at = slice(r, r + step)
        for c in range(0, s.shape[1], piece):
            s[at, c : c + piece] = right_t(low[at, :], w[c : c + piece, :]).astype(bf16)
        if stream:
            line.launch(r // 48, (r + step) // 48)

    def narrow(array, owner, small):
        return left_t(array[:, grads.at(owner)], small)

    def drain():
        for owner in range(max(owners - 2, 0), owners):
            grads.store(owner, owner % 2).wait()

    if stream:

        def job(owner):
            slot = lax.rem(owner, 2)

            @pl.when(owner == 0)
            def _():
                load_x.wait()
                for load in loads:
                    load.wait()

            @pl.when((owner >= 2) & (owner < owners))
            def _():
                grads.store(owner - 2, slot).wait()

            @pl.when(owner < owners)
            def _():
                stage[slot, :, : 3 * cols] = narrow(xin, owner, low[...]).astype(bf16)
                stage[slot, :, 3 * cols :] = (
                    narrow(pin.at[0], owner, attn[0][...])
                    + narrow(pin.at[1], owner, attn[1][...])
                ).astype(bf16)
                grads.store(owner, slot).start()

        assert owners <= rows // 48
        line.stream(job)
        drain()
    else:
        load_x.wait()

        def one(owner, carry):
            slot = lax.rem(owner, 2)
            load_before(owner, slot).wait()

            @pl.when(owner < owners - 1)
            def _():
                load_before(owner + 1, 1 - slot).start()

            @pl.when(owner >= 2)
            def _():
                grads.store(owner - 2, slot).wait()

            value = narrow(xin, owner, low[...]) + had[slot].astype(f32)
            stage[slot] = value.astype(bf16)
            grads.store(owner, slot).start()
            return carry

        lax.fori_loop(0, owners, one, 0)
        heads = cols // HD
        parts = grads.wide // LANES
        gains[...] = jnp.zeros_like(gains)
        first = others[0][...]
        for k in range(2):
            both = gain_grad[8 * k : 8 * k + 8, :] + first[8 * k : 8 * k + 8, :]
            total = jnp.sum(both, axis=0, keepdims=True)
            for owner in range(owners):
                for h in range(heads):
                    gains[owner, k * heads + h, :] = total[0, h * HD : (h + 1) * HD]
        for k, items in enumerate((others[1:3], others[3:])):
            total = sum(jnp.sum(item[...], axis=0, keepdims=True) for item in items)
            for owner in range(owners):
                for j in range(parts):
                    at = (owner * parts + j) * LANES
                    gains[owner, 2 * heads + k * parts + j, :] = total[0, at : at + LANES]
        low_gains, stores = scratch[12], []
        low_gains[...] = gains[...].astype(bf16)
        for owner in range(owners):
            at = pl.ds(owner * grads.wide, low_gains.shape[1])
            to = g_attn.at[at, pl.ds(4 * cols, LANES)]
            stores.append(pltpu.make_async_copy(low_gains.at[owner], to, n_sem.at[owner]))
        for store in stores:
            store.start()
        for store in stores:
            store.wait()
        drain()


def last_sum(
    dq, own, mine, got, units, squares, qg, kg, x, extra, before, w, owners, collective_id
):
    stream = before is None
    n = lax.axis_size("tensor")
    rows, cols = dq.shape
    width = w.shape[0]
    lines = line_count(rows)
    vmem = pl.BlockSpec(memory_space=pltpu.VMEM)
    hbm = pl.BlockSpec(memory_space=pl.ANY)
    dma = pltpu.SemaphoreType.DMA
    wide = width // owners
    weights = pl.BlockSpec((width, 3 * cols), lambda i: (0, 0))

    def kernel(*refs):
        sources = lax.axis_index("seq") < lax.axis_size("seq") // 2
        args = [n, rows, cols, sources, stream, *refs[:9]]
        if stream:
            args += [refs[9:11], refs[11:13], None, None, *refs[13:]]
        else:
            args += [None, None, refs[9], refs[10:14], *refs[14:]]
        last_kernel(*args)

    if stream:
        extra_specs = [hbm, hbm, vmem, vmem]
    else:
        extra, extra_specs = [before, *extra], [hbm] + [vmem] * 4
    shapes = [
        jax.ShapeDtypeStruct((rows, 3 * cols), bf16),
        jax.ShapeDtypeStruct((rows, width), bf16),
        jax.ShapeDtypeStruct((16, cols), f32),
        jax.ShapeDtypeStruct((width, 4 * cols + LANES), bf16),
    ]
    scratch = exchange_scratch(n, lines) + [
        pltpu.VMEM((rows, width), bf16),
        dma(()),
        pltpu.VMEM((2, wide, (4 if stream else 3) * cols), bf16),
        dma((2,)),
    ]
    if stream:
        line = line_scratch(rows, width, rows // 48)
        scratch += line[:3] + [pltpu.VMEM((2, rows, width), bf16), dma((2,))] + line[3:]
    else:
        scratch += [
            pltpu.VMEM((2, wide, 3 * cols), bf16),
            dma((2,)),
            pltpu.VMEM((owners, 16, LANES), f32),
            dma((owners,)),
            pltpu.VMEM((owners, 16, LANES), bf16),
        ]
    return pl.pallas_call(
        kernel,
        grid=(1,),
        in_specs=[vmem] * 8 + [hbm] + extra_specs + [weights],
        out_specs=[vmem, hbm if stream else vmem, vmem, hbm],
        out_shape=shapes,
        scratch_shapes=scratch,
        input_output_aliases={} if stream else {9: 3},
        compiler_params=pltpu.CompilerParams(
            collective_id=collective_id, has_side_effects=True, vmem_limit_bytes=60 << 20
        ),
        cost_estimate=cost(100 if stream else 25),
        name="last_sum" if stream else "last_part",
    )(dq, own, mine, got, units, squares, qg, kg, x, *extra, w)


LINE_ROWS = 48
ROW_STEP = 32
LAG = 3
PARTS = 3
TILE = 256
NAMES = (
    "part", "x", "cot", "w", "ga", "gm", "first", "proj", "hidden", "inner", "layer", "low",
    "gu", "back", "pre", "grads", "grads_down", "gm_grad", "s", "land", "swap", "res", "acc", "h", "xin", "cin",
    "wgt", "wut", "wdt", "gt", "ut", "it", "jt", "stage", "load_sem", "in_send", "in_recv", "swap_recv",
    "out_send", "out_recv", "store_sem", "w_sem", "x_sem", "c_sem", "h_sem", "y_sem", "t_sem",
    "r_sem", "g_sem",
)


class Mlp:
    def __init__(self, n, micros, rows, *refs):
        for name, ref in zip(NAMES, refs):
            setattr(self, name, ref)
        self.micros, self.rows = micros, rows
        self.chunks = rows // LINE_ROWS
        self.hidden_units = self.w.shape[1] // 3
        self.tiles = self.hidden_units // TILE
        i = lax.axis_index("tensor")
        half = n // 2
        left = i < half
        self.inward = jnp.where(left, i + 1, i - 1)
        self.outward = jnp.where(left, i - 1, i + 1)
        self.relay = (i > 0) & (i < n - 1)
        self.mid = (i == half - 1) | (i == half)

    def at(self, m, c):
        start = pl.multiple_of((m * self.chunks + c) * LINE_ROWS, LINE_ROWS)
        return pl.ds(start, LINE_ROWS)

    def micro(self, m):
        return pl.ds(pl.multiple_of(m * self.rows, self.rows), self.rows)

    def move_in(self, m, c):
        return pltpu.make_async_remote_copy(
            src_ref=self.s.at[self.at(m, c)],
            dst_ref=self.land.at[self.at(m, c)],
            send_sem=self.in_send.at[m, c],
            recv_sem=self.in_recv.at[m, c],
            device_id={"tensor": self.inward},
            device_id_type=MESH,
        )

    def move_swap(self, m, c):
        return pltpu.make_async_remote_copy(
            src_ref=self.s.at[self.at(m, c)],
            dst_ref=self.swap.at[self.at(m, c)],
            send_sem=self.in_send.at[m, c],
            recv_sem=self.swap_recv.at[m, c],
            device_id={"tensor": self.inward},
            device_id_type=MESH,
        )

    def move_out(self, m, c):
        return pltpu.make_async_remote_copy(
            src_ref=self.res.at[self.at(m, c)],
            dst_ref=self.res.at[self.at(m, c)],
            send_sem=self.out_send.at[m, c],
            recv_sem=self.out_recv.at[m, c],
            device_id={"tensor": self.outward},
            device_id_type=MESH,
        )

    def send_in(self, m, c):
        @pl.when(self.mid)
        def _():
            self.move_swap(m, c).start()

        @pl.when(~self.mid)
        def _():
            self.move_in(m, c).start()

    def each_chunk(self, body):
        def one(c, carry):
            body(c)
            return carry

        lax.fori_loop(0, self.chunks, one, 0)

    def launch(self, m):
        @pl.when(~self.relay)
        def _():
            self.each_chunk(lambda c: self.send_in(m, c))

    def settle(self, m):
        def one(c):
            self.move_in(m, c).wait_send()

            @pl.when(self.relay)
            def _():
                self.move_out(m, c).wait_send()

        self.each_chunk(one)

    def begin(self):
        others = pl.ds(self.rows, (self.micros - 1) * self.rows)
        load = pltpu.make_async_copy(self.part, self.s.at[others], self.load_sem)
        load.start()
        rest = self.micro(0)
        done = pltpu.make_async_copy(self.first, self.res.at[rest], self.y_sem)
        done.start()
        self.load_x(0, self.x).start()
        for copy in self.load_w(0, 0):
            copy.start()
        barrier = pltpu.get_barrier_semaphore()
        pl.semaphore_signal(
            barrier, inc=1, device_id={"tensor": self.inward}, device_id_type=MESH
        )

        @pl.when(self.relay)
        def _():
            pl.semaphore_signal(
                barrier, inc=1, device_id={"tensor": self.outward}, device_id_type=MESH
            )

        pl.semaphore_wait(barrier, jnp.where(self.relay, 2, 1))
        load.wait()
        done.wait()
        for m in range(1, self.micros):
            self.launch(m)
        self.gm_grad[...] = jnp.zeros_like(self.gm_grad)

    def reduce(self, m, c):
        @pl.when(self.relay)
        def _():
            self.move_in(m, c).wait_recv()
            a = self.at(m, c)
            self.s[a, :] = (self.s[a, :].astype(f32) + self.land[a, :].astype(f32)).astype(bf16)
            self.send_in(m, c)

    def store(self, m, c, to):
        a = self.at(m, c)
        return pltpu.make_async_copy(self.res.at[a], to.at[a], self.store_sem.at[m, c])

    def spread(self, which, m, c):
        a = self.at(m, c)

        @pl.when(self.mid)
        def _():
            self.move_swap(m, c).wait_recv()
            self.res[a, :] = (self.s[a, :].astype(f32) + self.swap[a, :].astype(f32)).astype(bf16)

        @pl.when(~self.mid)
        def _():
            self.move_out(m, c).wait_recv()

        @pl.when(self.relay)
        def _():
            self.move_out(m, c).start()

        @pl.when(which == 0)
        def _():
            self.store(m, c, self.proj).start()

        @pl.when(which == 2)
        def _():
            self.store(m, c, self.back).start()

    def load_x(self, m, source):
        return pltpu.make_async_copy(source.at[self.micro(m)], self.xin, self.x_sem)

    def load_c(self, m):
        return pltpu.make_async_copy(self.cot.at[self.micro(m)], self.cin, self.c_sem)

    def store_h(self, m, to):
        return pltpu.make_async_copy(self.h, to.at[self.micro(m)], self.h_sem)

    def store_layer(self, m):
        return pltpu.make_async_copy(self.xin, self.layer.at[self.micro(m)], self.y_sem)

    def cols(self, t, which=0):
        return pl.ds(pl.multiple_of(which * self.hidden_units + t * TILE, TILE), TILE)

    def load_w(self, t, slot):
        return [
            pltpu.make_async_copy(
                self.w.at[:, self.cols(t, which)], to.at[slot], self.w_sem.at[which, slot]
            )
            for which, to in enumerate((self.wgt, self.wut, self.wdt))
        ]

    def load_pre(self, m, t, slot):
        return [
            pltpu.make_async_copy(
                self.pre.at[self.micro(m), self.cols(t, which)],
                to.at[slot],
                self.r_sem.at[which, slot],
            )
            for which, to in enumerate((self.gt, self.ut))
        ]

    def store_tile(self, which, source, to, m, at, slot):
        return pltpu.make_async_copy(
            source.at[slot], to.at[self.micro(m), at], self.t_sem.at[which, slot]
        )

    def store_pre(self, m, t, slot):
        return (
            self.store_tile(0, self.gt, self.pre, m, self.cols(t, 0), slot),
            self.store_tile(1, self.ut, self.pre, m, self.cols(t, 1), slot),
            self.store_tile(2, self.it, self.inner, m, self.cols(t), slot),
        )

    def store_low(self, m, t, slot):
        return (
            self.store_tile(2, self.it, self.gu, m, self.cols(t, 0), slot),
            self.store_tile(3, self.jt, self.gu, m, self.cols(t, 1), slot),
        )

    def row_groups(self, body):
        step = ROW_STEP

        def one(r, carry):
            body(pl.ds(pl.multiple_of(r * step, step), step), r * step)
            return carry

        lax.fori_loop(0, self.rows // step, one, 0)

    def forward_start(self, m):
        @pl.when(m > 0)
        def _():
            self.each_chunk(lambda c: self.store(m, c, self.proj).wait())

        self.load_x(m, self.x).wait()
        base = m * self.rows
        gain = self.ga[...]

        def one(at, r):
            total = self.res[pl.ds(pl.multiple_of(base + r, ROW_STEP), ROW_STEP), :].astype(f32)
            inv = lax.rsqrt(jnp.mean(total * total, axis=1, keepdims=True) + norm_eps)
            self.h[at, :] = (self.xin[at, :].astype(f32) + total * inv * gain).astype(bf16)

        self.row_groups(one)
        self.store_h(m, self.hidden).start()

    def backward_start(self, m):
        for copy in self.load_pre(m, 0, 0):
            copy.start()
        self.load_x(m, self.hidden).wait()
        self.load_c(m).wait()
        base = m * self.rows
        gain = self.gm[...]

        def one(at, r):
            total = self.res[pl.ds(pl.multiple_of(base + r, ROW_STEP), ROW_STEP), :].astype(f32)
            inv = lax.rsqrt(jnp.mean(total * total, axis=1, keepdims=True) + norm_eps)
            unit = total * inv
            c = self.cin[at, :].astype(f32)
            self.xin[at, :] = (self.xin[at, :].astype(f32) + unit * gain).astype(bf16)
            hit = c * unit
            self.gm_grad[...] += fold(hit)
            dy = c * gain
            inner = jnp.mean(hit * gain, axis=1, keepdims=True)
            self.h[at, :] = (inv * (dy - unit * inner)).astype(bf16)

        self.row_groups(one)
        self.store_layer(m).start()
        self.store_h(m, self.low).start()

    def tile_weights(self, t, slot, last):
        for copy in self.load_w(t, slot):
            copy.wait()

        @pl.when(jnp.logical_not(last))
        def _():
            for copy in self.load_w(lax.rem(t + 1, self.tiles), 1 - slot):
                copy.start()

    def add(self, t, at, value):
        @pl.when(t == 0)
        def _():
            self.acc[:, at] = value

        @pl.when(t > 0)
        def _():
            self.acc[:, at] += value

    def forward_gate(self, m, t):
        slot = lax.rem(t, 2)
        self.tile_weights(t, slot, False)

        @pl.when(t >= 2)
        def _():
            for copy in self.store_pre(m, t - 2, slot):
                copy.wait()

        self.gt[slot] = matmul(self.h[...], self.wgt[slot]).astype(bf16)

    def forward_up(self, m, t):
        slot = lax.rem(t, 2)
        up = matmul(self.h[...], self.wut[slot])
        gate = self.gt[slot].astype(f32)
        self.ut[slot] = up.astype(bf16)
        self.it[slot] = (gate * jax.nn.sigmoid(gate) * up).astype(bf16)
        for copy in self.store_pre(m, t, slot):
            copy.start()

    def forward_down(self, m, t):
        slot = lax.rem(t, 2)
        wide = self.acc.shape[1]
        step = math.gcd(wide, 512)
        for k in range(0, wide, step):
            self.add(t, slice(k, k + step), right_t(self.it[slot], self.wdt[slot, k : k + step, :]))

        @pl.when(t == self.tiles - 1)
        def _():
            for back in range(min(2, self.tiles)):
                at = self.tiles - 1 - back
                for copy in self.store_pre(m, at, at % 2):
                    copy.wait()
            self.store_h(m, self.hidden).wait()
            self.finish(m, m > 0)

    def backward_low(self, m, t, last):
        slot = lax.rem(t, 2)
        self.tile_weights(t, slot, last & (t == self.tiles - 1))
        for copy in self.load_pre(m, t, slot):
            copy.wait()

        @pl.when(t < self.tiles - 1)
        def _():
            for copy in self.load_pre(m, t + 1, 1 - slot):
                copy.start()

        @pl.when(t >= 2)
        def _():
            for copy in self.store_low(m, t - 2, slot):
                copy.wait()

        grad = matmul(self.h[...], self.wdt[slot])
        gate = self.gt[slot].astype(f32)
        sig = jax.nn.sigmoid(gate)
        act = grad * sig
        self.jt[slot] = (act * gate).astype(bf16)
        self.it[slot] = (
            act * self.ut[slot].astype(f32) * (1.0 + gate * (1.0 - sig))
        ).astype(bf16)
        for copy in self.store_low(m, t, slot):
            copy.start()

    def backward_add(self, t, second):
        slot = lax.rem(t, 2)
        half = self.acc.shape[1] // 2
        step = math.gcd(half, 512)
        for k in range(second * half, (second + 1) * half, step):
            self.add(
                t,
                slice(k, k + step),
                right_t(self.it[slot], self.wgt[slot, k : k + step, :])
                + right_t(self.jt[slot], self.wut[slot, k : k + step, :]),
            )

    def backward_end(self, m, t):
        @pl.when(t == self.tiles - 1)
        def _():
            for back in range(min(2, self.tiles)):
                at = self.tiles - 1 - back
                for copy in self.store_low(m, at, at % 2):
                    copy.wait()
            self.store_h(m, self.low).wait()
            self.store_layer(m).wait()
            self.finish(m, True)

    def piece(self, m, forward, last, unit):
        t, which = unit // 3, lax.rem(unit, 3)

        def when(ahead, number, body):
            @pl.when((forward if ahead else jnp.logical_not(forward)) & (which == number))
            def _():
                body()

        when(True, 0, lambda: self.forward_gate(m, t))
        when(True, 1, lambda: self.forward_up(m, t))
        when(True, 2, lambda: self.forward_down(m, t))
        when(False, 0, lambda: self.backward_low(m, t, last))
        when(False, 1, lambda: self.backward_add(t, 0))

        def rest():
            self.backward_add(t, 1)
            self.backward_end(m, t)

        when(False, 2, rest)

    def parts_by(self, step):
        return jnp.minimum(PARTS * (step - 1), 3 * self.tiles)

    def load_bigs(self, source):
        return (
            pltpu.make_async_copy(source.at[self.micro(0)], self.xin, self.x_sem),
            pltpu.make_async_copy(source.at[self.micro(1)], self.cin, self.c_sem),
        )

    def load_units(self, source, w, slot):
        return [
            pltpu.make_async_copy(
                source.at[self.micro(m), self.cols(w)], to.at[slot], self.r_sem.at[m, slot]
            )
            for m, to in enumerate((self.gt, self.ut))
        ]

    def start_units(self, w, slot):
        split = 2 * self.tiles

        @pl.when(w < split)
        def _():
            for copy in self.load_units(self.gu, w, slot):
                copy.start()

        @pl.when((w >= split) & (w < 3 * self.tiles))
        def _():
            for copy in self.load_units(self.inner, w - split, slot):
                copy.start()

    def store_grads(self, w, slot):
        return pltpu.make_async_copy(
            self.stage.at[slot], self.grads.at[:, self.cols(w), :], self.g_sem.at[slot]
        )

    def store_down(self, t, slot):
        return pltpu.make_async_copy(
            self.stage.at[slot], self.grads_down.at[:, self.cols(t), :], self.g_sem.at[slot]
        )

    def grad_tile(self, w):
        slot = lax.rem(w, 2)
        split = 2 * self.tiles

        @pl.when((w == 0) | (w == split))
        def _():
            for copy in self.load_bigs(self.hidden):
                copy.wait()

        for copy in self.load_units(self.gu, 0, slot):
            copy.wait()
        self.start_units(w + 1, 1 - slot)

        @pl.when(w >= 2)
        def _():
            self.store_grads(0, slot).wait()

        value = left_t(self.gt[slot], self.xin[...]) + left_t(self.ut[slot], self.cin[...])
        owners, _, wide = self.stage.shape[1:]
        for owner in range(owners):
            self.stage[slot, owner] = value[:, owner * wide : (owner + 1) * wide].astype(bf16)

        @pl.when(w < split)
        def _():
            self.store_grads(w, slot).start()

        @pl.when(w >= split)
        def _():
            self.store_down(w - split, slot).start()

        @pl.when(w == split - 1)
        def _():
            for copy in self.load_bigs(self.low):
                copy.start()

        @pl.when(w == 3 * self.tiles - 1)
        def _():
            self.store_down(0, 1 - slot).wait()
            self.store_down(0, slot).wait()

    def finish(self, m, sent):
        @pl.when(sent)
        def _():
            self.settle(m)

        base = m * self.rows

        def one(at, r):
            self.s[pl.ds(pl.multiple_of(base + r, ROW_STEP), ROW_STEP), :] = self.acc[at, :].astype(bf16)

        self.row_groups(one)
        self.launch(m)

    def job(self, index, step):
        micros = self.micros
        m = lax.rem(index, micros)
        forward = index < micros
        last = index == 2 * micros - 1

        @pl.when(forward & (step == 0))
        def _():
            self.forward_start(m)

        @pl.when(jnp.logical_not(forward) & (step == 0))
        def _():
            self.backward_start(m)

        first, after_last = self.parts_by(step), self.parts_by(step + 1)

        def one(unit, carry):
            self.piece(m, forward, last, unit)
            return carry

        @pl.when(step >= 1)
        def _():
            lax.fori_loop(first, after_last, one, 0)

        done = (first < 3 * self.tiles) & (after_last == 3 * self.tiles)

        @pl.when(done & (index < micros - 1))
        def _():
            self.load_x(index + 1, self.x).start()

        @pl.when(done & (index >= micros - 1) & jnp.logical_not(last))
        def _():
            self.load_x(index + 1 - micros, self.hidden).start()
            self.load_c(index + 1 - micros).start()

        @pl.when(done & last)
        def _():
            for copy in self.load_bigs(self.hidden):
                copy.start()
            self.start_units(0, 0)

    def run(self):
        n, micros = self.chunks, self.micros
        total = 3 * micros * n
        clocks = 1 + -(-3 * self.tiles // PARTS)
        self.begin()

        def clock(k, carry):
            @pl.when(k < total)
            def _():
                self.reduce(lax.rem(k // n, micros), lax.rem(k, n))

            back = k - LAG

            @pl.when((back >= n) & (back < total))
            def _():
                sum_index = back // n
                self.spread(sum_index // micros, lax.rem(sum_index, micros), lax.rem(back, n))

            turn = back - n

            @pl.when((turn >= 0) & (turn < 2 * micros * n))
            def _():
                self.job(turn // n, lax.rem(turn, n))

            turn = turn - 2 * micros * n + n - clocks

            @pl.when((turn >= 0) & (turn < 3 * self.tiles))
            def _():
                self.grad_tile(turn)

            return carry

        grads_at = 2 * micros * n + LAG + clocks
        lax.fori_loop(n, max(total + LAG, grads_at + 3 * self.tiles), clock, 0)
        for m in range(micros):
            self.settle(m)
            self.each_chunk(lambda c: self.store(m, c, self.back).wait())


def mlp_kernel(n, micros, rows, *refs):
    Mlp(n, micros, rows, *refs).run()


def feed_forward(part, x, cot, w, ga, gm, first, micros, owners):
    assert micros == 2
    both, width = x.shape
    hidden = w.shape[1] // 3
    rows = both // micros
    chunks = rows // LINE_ROWS
    dma = pltpu.SemaphoreType.DMA
    hbm = pl.BlockSpec(memory_space=pl.ANY)
    vmem = pl.BlockSpec(memory_space=pltpu.VMEM)
    wide = jax.ShapeDtypeStruct((both, width), bf16)
    unit = jax.ShapeDtypeStruct((both, hidden), bf16)
    two = jax.ShapeDtypeStruct((both, 2 * hidden), bf16)
    return pl.pallas_call(
        functools.partial(mlp_kernel, lax.axis_size("tensor"), micros, rows),
        in_specs=[hbm] * 4 + [vmem] * 2 + [hbm],
        out_specs=[hbm] * 10 + [vmem],
        out_shape=[wide, wide, unit, wide, wide, two, wide, two]
        + [jax.ShapeDtypeStruct((owners, k * hidden, width // owners), bf16) for k in (2, 1)]
        + [jax.ShapeDtypeStruct((8, width), f32)],
        scratch_shapes=[
            pltpu.VMEM((both, width), bf16),
            pltpu.VMEM((both, width), bf16),
            pltpu.VMEM((both, width), bf16),
            pltpu.VMEM((both, width), bf16),
            pltpu.VMEM((rows, width), f32),
            pltpu.VMEM((rows, width), bf16),
            pltpu.VMEM((rows, width), bf16),
            pltpu.VMEM((rows, width), bf16),
            pltpu.VMEM((2, width, TILE), bf16),
            pltpu.VMEM((2, width, TILE), bf16),
            pltpu.VMEM((2, width, TILE), bf16),
            pltpu.VMEM((2, rows, TILE), bf16),
            pltpu.VMEM((2, rows, TILE), bf16),
            pltpu.VMEM((2, rows, TILE), bf16),
            pltpu.VMEM((2, rows, TILE), bf16),
            pltpu.VMEM((2, owners, TILE, width // owners), bf16),
            dma(()),
            dma((micros, chunks)),
            dma((micros, chunks)),
            dma((micros, chunks)),
            dma((micros, chunks)),
            dma((micros, chunks)),
            dma((micros, chunks)),
            dma((3, 2)),
            dma(()),
            dma(()),
            dma(()),
            dma(()),
            dma((4, 2)),
            dma((2, 2)),
            dma((2,)),
        ],
        compiler_params=pltpu.CompilerParams(
            collective_id=1, has_side_effects=True, vmem_limit_bytes=60 << 20
        ),
        cost_estimate=cost(both // 4),
        name="feed_forward",
    )(part, x, cot, w, ga, gm, first)


def attn_scores(meta, i, trunk_rows, q, kt, kp, ko):
    scale = HD ** (-0.5)
    block = meta[i, 0]
    n_par = meta[i, 2]
    n_own = meta[i, 3]
    n_trunk = meta[i, 4]
    st = right_t(q, kt) * scale
    sp = right_t(q, kp) * scale
    so = right_t(q, ko) * scale
    row = lax.broadcasted_iota(jnp.int32, (BLOCK, trunk_rows), 0) + block * BLOCK
    col = lax.broadcasted_iota(jnp.int32, (BLOCK, trunk_rows), 1)
    st = jnp.where((col < n_trunk) & (col <= row), st, masked_score)
    row = lax.broadcasted_iota(jnp.int32, (BLOCK, BLOCK), 0)
    col = lax.broadcasted_iota(jnp.int32, (BLOCK, BLOCK), 1)
    sp = jnp.where(col < n_par, sp, masked_score)
    so = jnp.where((col < n_own) & (col <= row), so, masked_score)
    return st, sp, so


def attn_fwd_kernel(trunk_rows, meta, q, trunk, par, own, out, lse):
    i = pl.program_id(1)
    st, sp, so = attn_scores(meta, i, trunk_rows, q[...], trunk[0], par[0], own[0])
    top = jnp.maximum(
        jnp.max(st, axis=1, keepdims=True),
        jnp.maximum(jnp.max(sp, axis=1, keepdims=True), jnp.max(so, axis=1, keepdims=True)),
    )
    et, ep, eo = jnp.exp(st - top), jnp.exp(sp - top), jnp.exp(so - top)
    total = (
        jnp.sum(et, axis=1, keepdims=True)
        + jnp.sum(ep, axis=1, keepdims=True)
        + jnp.sum(eo, axis=1, keepdims=True)
    )
    acc = matmul(et.astype(bf16), trunk[1])
    acc += matmul(ep.astype(bf16), par[1])
    acc += matmul(eo.astype(bf16), own[1])
    out[...] = (acc / total).astype(bf16)
    lse[...] = jnp.broadcast_to(top + jnp.log(total), (BLOCK, HD))


def attn_bwd_kernel(
    trunk_rows, n_q, meta, q, do, lse, trunk, par, own, dq, d_own, d_src, acc,
):
    i = pl.program_id(1)

    @pl.when(i == 0)
    def _():
        acc[...] = jnp.zeros_like(acc)

    scale = HD ** (-0.5)
    qv, dov = q[...], do[...]
    scores = attn_scores(meta, i, trunk_rows, qv, trunk[0], par[0], own[0])
    top = lse[:, 0:1]
    probs = [jnp.exp(s - top) for s in scores]
    grads = [right_t(dov, v[1]) for v in (trunk, par, own)]
    inner = sum(jnp.sum(p * g, axis=1, keepdims=True) for p, g in zip(probs, grads))
    low = [(p * (g - inner)).astype(bf16) for p, g in zip(probs, grads)]
    probs = [p.astype(bf16) for p in probs]
    dq[...] = scale * (
        matmul(low[0], trunk[0]) + matmul(low[1], par[0]) + matmul(low[2], own[0])
    )
    d_own[0] = scale * left_t(low[2], qv)
    d_own[1] = left_t(probs[2], dov)
    acc[0, :trunk_rows] += left_t(low[0], qv)
    acc[1, :trunk_rows] += left_t(probs[0], dov)
    at = pl.ds(pl.multiple_of(trunk_rows + meta[i, 1] * BLOCK, BLOCK), BLOCK)
    acc[0, at] += left_t(low[1], qv)
    acc[1, at] += left_t(probs[1], dov)

    @pl.when(i == n_q - 1)
    def _():
        d_src[0] = (scale * acc[0]).astype(bf16)
        d_src[1] = acc[1].astype(bf16)


def kv_specs(trunk_rows):
    skip = trunk_rows // BLOCK
    trunk = pl.BlockSpec((2, trunk_rows, HD), lambda h, i, meta: (0, 0, h))
    par = pl.BlockSpec((2, BLOCK, HD), lambda h, i, meta: (0, skip + meta[i, 1], h))
    own = pl.BlockSpec((2, BLOCK, HD), lambda h, i, meta: (0, i, h))
    return [trunk, par, own]


def attend_forward(meta, q, sources, own_kv, trunk_rows):
    rows, width = q.shape
    own = pl.BlockSpec((BLOCK, HD), lambda h, i, meta: (i, h))
    return pl.pallas_call(
        functools.partial(attn_fwd_kernel, trunk_rows),
        grid_spec=pltpu.PrefetchScalarGridSpec(
            num_scalar_prefetch=1,
            grid=(width // HD, rows // BLOCK),
            in_specs=[own] + kv_specs(trunk_rows),
            out_specs=[own, own],
        ),
        out_shape=[
            jax.ShapeDtypeStruct((rows, width), bf16),
            jax.ShapeDtypeStruct((rows, width), f32),
        ],
        compiler_params=pltpu.CompilerParams(vmem_limit_bytes=32 << 20),
        cost_estimate=cost(12),
        name="attend_forward",
    )(meta, q, sources, sources, own_kv)


def attend_backward(meta, q, do, lse, sources, own_kv, trunk_rows):
    rows, width = q.shape
    own = pl.BlockSpec((BLOCK, HD), lambda h, i, meta: (i, h))
    own_two = pl.BlockSpec((2, BLOCK, HD), lambda h, i, meta: (0, i, h))
    all_rows = sources.shape[1]
    n_q = rows // BLOCK
    return pl.pallas_call(
        functools.partial(attn_bwd_kernel, trunk_rows, n_q),
        grid_spec=pltpu.PrefetchScalarGridSpec(
            num_scalar_prefetch=1,
            grid=(width // HD, n_q),
            in_specs=[own, own, own] + kv_specs(trunk_rows),
            out_specs=[
                own,
                own_two,
                pl.BlockSpec((2, all_rows, HD), lambda h, i, meta: (0, 0, h)),
            ],
            scratch_shapes=[pltpu.VMEM((2, all_rows, HD), f32)],
        ),
        out_shape=[
            jax.ShapeDtypeStruct((rows, width), f32),
            jax.ShapeDtypeStruct((2, rows, width), f32),
            jax.ShapeDtypeStruct(sources.shape, bf16),
        ],
        compiler_params=pltpu.CompilerParams(vmem_limit_bytes=40 << 20),
        cost_estimate=cost(22),
        name="attend_backward",
    )(meta, q, do, lse, sources, sources, own_kv)


def group_perm(n, k):
    half = n // 2
    return [(i, i // half * half + (i % half + k) % half) for i in range(n)]


def fetch_sources(block, hold):
    n = lax.axis_size("seq")
    half = n // 2
    place = lax.axis_index("seq")
    spot = lax.rem(place, half)
    got = lax.ppermute(block, "seq", [(i, i + half) for i in range(half)])
    got = after(got, *hold)
    mine = jnp.where(place < half, block, got)
    parts = [mine] + [lax.ppermute(mine, "seq", group_perm(n, k)) for k in range(1, half)]
    out = []
    for source in range(half):
        pick = parts[0]
        for k in range(1, half):
            pick = jnp.where(lax.rem(spot - k + half, half) == source, parts[k], pick)
        out.append(pick)
    return jnp.concatenate(out, axis=1), got


def sum_over_group(grads):
    n = lax.axis_size("seq")
    half = n // 2
    spot = lax.rem(lax.axis_index("seq"), half)
    rows = grads.shape[1] // half
    pieces = [grads[:, s * rows : (s + 1) * rows] for s in range(half)]

    def piece(index):
        pick = pieces[0]
        for s in range(1, half):
            pick = jnp.where(index == s, pieces[s], pick)
        return pick

    total = piece(spot).astype(f32)
    for k in range(1, half):
        sent = piece(lax.rem(spot + k, half))
        total += lax.ppermute(sent, "seq", group_perm(n, k)).astype(f32)
    return total.astype(bf16)


def return_to_sources(total):
    n = lax.axis_size("seq")
    half = n // 2
    return lax.ppermute(total, "seq", [(i + half, i) for i in range(half)])


def gather_rows(item):
    return lax.all_gather(item, ("dp", "seq"), axis=0, tiled=True)


def scatter_low(item):
    return lax.psum_scatter(item, ("dp", "seq"), scatter_dimension=0, tiled=True)


def scatter_rows(item):
    return scatter_low(item).astype(f32)


def block_meta(parents, lengths, rows, n_blocks):
    seg_count = parents.shape[0]
    branches = (seg_count - 1) // 3
    trunk_blocks = n_blocks - 3 * branches
    blocks = lax.axis_index("seq") * (rows // BLOCK) + jnp.arange(rows // BLOCK, dtype=jnp.int32)
    seg = jnp.maximum(blocks - trunk_blocks + 1, 0)
    hit = seg[:, None] == jnp.arange(seg_count, dtype=jnp.int32)[None, :]
    parent = jnp.sum(jnp.where(hit, parents[None, :], 0), axis=1)
    own_len = jnp.sum(jnp.where(hit, lengths[None, :], 0), axis=1)
    hit = parent[:, None] == jnp.arange(seg_count, dtype=jnp.int32)[None, :]
    par_len = jnp.sum(jnp.where(hit, lengths[None, :], 0), axis=1)
    return jnp.stack(
        [
            blocks,
            jnp.maximum(parent - 1, 0),
            jnp.where(parent > 0, par_len, 0),
            jnp.where(blocks >= trunk_blocks, own_len, 0),
            jnp.broadcast_to(lengths[0], blocks.shape),
        ],
        axis=1,
    ).astype(jnp.int32)


def per_device(
    tokens, cotangent, w_query, w_key, w_value, w_out, w_gate, w_up, w_down,
    query_gain, key_gain, attn_gain, mlp_gain, parent_of, seg_length,
):
    micros, _, rows, width = tokens.shape
    n_blocks = rows // BLOCK * lax.axis_size("seq")
    heads = w_query.shape[1] // HD
    full_width = heads * HD * lax.axis_size("tensor")
    branches = (parent_of.shape[2] - 1) // 3
    trunk_rows = (n_blocks - 3 * branches) * BLOCK

    cols = w_query.shape[1]
    owners = lax.axis_size("dp") * lax.axis_size("seq")
    gains = [query_gain.reshape(-1), key_gain.reshape(-1), attn_gain, mlp_gain]
    gains = jnp.concatenate(gains)
    count = gains.shape[0]
    lines = -(-count // LANES)
    gains = jnp.pad(gains, (0, lines * LANES - count)).reshape(lines, LANES)
    gains = jnp.pad(gains, ((0, width // owners - lines), (0, 0)))
    w_attn = gather_shards(
        jnp.concatenate([w_query, w_key, w_value, w_out.T, gains], axis=1), 9
    )
    w_own = jnp.concatenate([w_gate, w_up, w_down.T], axis=1)
    gains = w_attn[:, 4 * cols :].reshape(owners, -1, LANES)[:, :lines]
    gains = gains.reshape(owners, lines * LANES)
    own = query_gain.size

    def head_gain(block):
        block = block.reshape(owners, heads, HD // owners)
        return jnp.swapaxes(block, 0, 1).reshape(-1).astype(f32)

    q_gain = head_gain(gains[:, :own])
    k_gain = head_gain(gains[:, own : 2 * own])
    a_gain = gains[:, 2 * own : 2 * own + attn_gain.size].reshape(-1).astype(f32)
    m_gain = gains[:, 2 * own + attn_gain.size : count].reshape(-1).astype(f32)
    wo_t = w_attn[:, 3 * cols : 4 * cols]
    q_gain, k_gain, a_gain = q_gain[None], k_gain[None], a_gain[None]

    x = tokens.reshape(micros * rows, width)
    cot = cotangent.reshape(micros * rows, width)
    q_lows, kv_lows, units, squares = zip(
        *(qkv(x, w_attn, q_gain, k_gain, m, rows, 6 + m) for m in range(micros))
    )
    sources, metas, attn_lows, lses, parts, first = [], [], [], [], [], None
    for m in range(micros):
        block = kv_lows[m] if m == 0 else after(kv_lows[m], attn_lows[0])
        source, got = fetch_sources(block, (q_lows[1], w_own) if m == 0 else (first,))
        sources.append(source)
        metas.append(block_meta(parent_of[m, 0], seg_length[m, 0], rows, n_blocks))
        attn_low, lse = attend_forward(metas[m], q_lows[m], sources[m], kv_lows[m], trunk_rows)
        attn_lows.append(attn_low)
        lses.append(lse)
        parts.append(right_t(attn_low, wo_t).astype(bf16))
        if m == 0:
            first = line_sum(parts[0], 0)
            w_mlp = gather_rows(after(w_own, got))
    proj, _, _, layer, _, _, back, _, gu_grads, down_grads, gm_grad = feed_forward(
        parts[1], x, cot, w_mlp, a_gain, m_gain[None], first,
        micros, owners,
    )
    hidden = w_gate.shape[1]
    g_attn, qk_grad, ga_grads, layer_out = None, None, [], None
    wide = width // owners
    proj_lows, dqs, d_owns, sums = [], [], [], []
    for m in range(micros):
        proj_low, attn_grad, grad, layer_out = proj_backward(
            cot, back, first if m == 0 else proj, after(a_gain, sums[0]) if m else a_gain, w_attn,
            layer, layer_out, cols, m, rows, m
        )
        ga_grads.append(grad)
        dq, d_own, d_src = attend_backward(
            metas[m], q_lows[m], attn_grad, lses[m], sources[m], kv_lows[m], trunk_rows
        )
        sums.append(sum_over_group(d_src))
        proj_lows.append(proj_low)
        dqs.append(dq)
        d_owns.append(d_own)

    lasts = []
    for m in range(micros):
        got = return_to_sources(sums[m])
        if m > 0:
            input_grad = add_up(cot, back, lasts[0], 0, None)
            got = after(got, input_grad)
        else:
            got = after(got, dqs[-1])
            g_down = scatter_low(down_grads.reshape(-1, wide))
            gu_grads = after(gu_grads.reshape(-1, wide), got, g_down)
            gu_grads = scatter_low(gu_grads)
        extra = [*proj_lows, *attn_lows] if m == 0 else [qk_grad, *ga_grads, gm_grad]
        _, last, qk_grad, g_attn = last_sum(
            dqs[m], d_owns[m], sums[m], got, units[m], squares[m], q_gain, k_gain,
            x.reshape(micros, rows, width), extra, g_attn, w_attn, owners, 5 if m else 3,
        )
        lasts.append(line_sum(last, 4) if m else last)
    g_attn = scatter_low(after(g_attn, gu_grads))
    g_attn = after(g_attn, qk_grad).astype(f32)

    lines = g_attn[:, 4 * cols :]
    share = HD // owners
    place = lax.axis_index("dp") * lax.axis_size("seq") + lax.axis_index("seq")
    head_lines = lax.dynamic_slice_in_dim(lines[: 2 * heads], place * share, share, 1)
    own_lines = lines[2 * heads : 2 * heads + 2 * attn_gain.size // LANES].reshape(2, -1)
    input_grad = add_up(cot, back, lasts[1], 1, input_grad)
    return (
        layer_out.reshape(tokens.shape),
        input_grad.reshape(tokens.shape),
        g_attn[:, :cols],
        g_attn[:, cols : 2 * cols],
        g_attn[:, 2 * cols : 3 * cols],
        g_attn[:, 3 * cols : 4 * cols].T,
        gu_grads[:hidden].astype(f32).T,
        gu_grads[hidden:].astype(f32).T,
        g_down.astype(f32),
        head_lines[:heads],
        head_lines[heads:],
        own_lines[0],
        own_lines[1],
    )


def solution(mesh):
    rows = P(None, "dp", "seq", None)
    by_row = P(("dp", "seq"), "tensor")
    by_col = P("tensor", ("dp", "seq"))
    gain = P(("dp", "seq"))
    tree = P(None, "dp", None)
    weights = (by_row, by_row, by_row, by_col, by_row, by_row, by_col, by_col, by_col, gain, gain)
    return jax.shard_map(
        per_device,
        mesh=mesh,
        in_specs=(rows, rows) + weights + (tree, tree),
        out_specs=(rows, rows) + weights,
        check_vma=False,
    )
```
